32 devices in a mesh: groups: 2 (over y), prow: 4 (over z), pcol: 4 (over x, core).
Axes of the slice: x: 2, y: 2, z: 4, core: 2. Of those that a mesh axis runs over, the one named last changes fastest.
Arguments:
- right_side: float32 [8, 512, 512], P('groups', 'prow', 'pcol'), parts along dimension 0, may hold values from -6 to 6
- earlier: float32 [8, 512, 512], P('groups', 'prow', 'pcol'), parts along dimension 0, may hold values from -6 to 6
- inverse_diag: float32 [8, 512, 512], P('groups', 'prow', 'pcol'), parts along dimension 0, may hold values from -0.25 to 0.25
- dense_tiles: float32 [8, 7, 512, 512], P('groups', None, 'prow', 'pcol'), parts along dimension 0, may hold values from -0.09375 to 0.09375
- left_factor: float32 [8, 7, 512, 64], P('groups', None, 'prow'), parts along dimension 0, may hold values from -0.25 to 0.25
- right_factor: float32 [8, 7, 512, 64], P('groups', None, 'prow'), parts along dimension 0, may hold values from -0.25 to 0.25
- tile_ranks: int32 [8, 7], P('groups'), parts along dimension 0, may hold values from 1 to 64, as said below
- dense_flags: int32 [8, 7], P('groups'), parts along dimension 0, may hold values 0 or 1
Outputs:
- solved: float32 [8, 512, 512], P('groups', 'prow', 'pcol'), parts along dimension 0
The draws below stay inside these ranges and needn't reach their ends.
There are 2 independent parts, one for each index of `groups`. The reference program is written for one: setup_inputs(seed, part) draws one part's arguments, and reference() takes and returns one part's arrays. A program takes and returns all parts, laid end to end along the dimension named above; each array names one. Nothing has to cross between parts.
Inputs may be any that keep to these rules, and one draw needn't show every extreme that they name: `tile_ranks`: ranks of the low-rank tiles; the padded rank 64 is reached by some tile.
All inputs are finite; a program needn't handle non-finite values.
Results may differ from the reference program's by a relative error of at most 0.0001.
Values sent between devices are 32-bit elements; how exact they have to be, the bound alone decides.
No kernel may reach another device: no remote copies, remote signals or barrier semaphores. Data moves between devices by JAX's collectives and lax.ppermute only.
A program may use at most 64 MiB of HBM per device.

```python
import jax
import jax.numpy as jnp
from jax import lax

NB = 512
R = 64
STEPS = 4
PREV = 4
COLS = 7
RHS = 512


def draw_tile_ranks(key, part):
    key = jax.random.fold_in(key, 7)
    rank_key, spot_key = jax.random.split(key)
    drawn = jax.random.randint(rank_key, (STEPS * COLS,), 1, R + 1)
    location = jax.random.randint(spot_key, (), 0, STEPS * COLS)
    drawn = jnp.where(jnp.arange(STEPS * COLS) == location, R, drawn)
    return drawn.reshape(STEPS, COLS).astype(jnp.int32)


def set_ends(values, stream_key, least, top_value):
    index_at = [jax.random.randint(jax.random.fold_in(stream_key, axis), (), 0, length) for axis, length in enumerate(values.shape)]
    longest = values.shape.index(max(values.shape))
    beside = index_at[:longest] + [(index_at[longest] + 1) % values.shape[longest]] + index_at[longest + 1:]
    return values.at[tuple(index_at)].set(least).at[tuple(beside)].set(top_value)


def shard_levels(stream_key, dims, cuts, smallest, top_value):
    level = 1.0
    for dim, shards_of in cuts:
        draws = jax.random.uniform(jax.random.fold_in(jax.random.fold_in(stream_key, 6), dim), (shards_of,), jnp.float32, smallest / len(cuts), top_value / len(cuts))
        level = level * jnp.repeat(jnp.exp(draws), dims[dim] // shards_of).reshape((-1,) + (1,) * (len(dims) - 1 - dim))
    return level


def scatter_about(own_key, dims, spread, reach, shards=(), held_as=jnp.bfloat16):
    values = spread * jax.random.normal(own_key, dims, jnp.float32)
    if shards:
        values = values * shard_levels(own_key, dims, shards, -0.22, 0.18)
    return jnp.clip(values, -reach, reach).astype(held_as)


def setup_inputs(seed: int = 0, part: int = 0) -> dict:
    streams_of = jax.random.split(jax.random.key(seed), 9)
    part_keys = jax.random.split(jax.random.fold_in(streams_of[8], part), 9)
    return {
        "right_side": scatter_about(part_keys[0], (STEPS, NB, RHS), 1.0, 6.0, ((1, 4), (2, 4)), jnp.float32),
        "earlier": scatter_about(part_keys[1], (PREV, NB, RHS), 1.0, 6.0, ((1, 4), (2, 4)), jnp.float32),
        "inverse_diag": scatter_about(part_keys[2], (STEPS, NB, NB), NB ** -0.5, 0.25, ((1, 4), (2, 4)), jnp.float32),
        "dense_tiles": scatter_about(part_keys[3], (STEPS, COLS, NB, NB), (NB * COLS) ** -0.5, 0.09375, ((2, 4), (3, 4)), jnp.float32),
        "left_factor": scatter_about(part_keys[4], (STEPS, COLS, NB, R), (R * COLS) ** -0.5, 0.25, ((2, 4),), jnp.float32),
        "right_factor": scatter_about(part_keys[5], (STEPS, COLS, NB, R), NB ** -0.5, 0.25, ((2, 4),), jnp.float32),
        "tile_ranks": draw_tile_ranks(jax.random.fold_in(jax.random.fold_in(streams_of[8], part), 71), part),
        "dense_flags": set_ends((jax.random.randint(part_keys[7], (STEPS, COLS), 0, 2) < 1).astype(jnp.int32), jax.random.fold_in(part_keys[7], 1), 0, 1),
    }


HIGHEST = lax.Precision.HIGHEST


def reference(right_side, earlier, inverse_diag, dense_tiles, left_factor, right_factor, tile_ranks, dense_flags):
    tile_flags = dense_flags.astype(jnp.float32)
    columns = lax.broadcasted_iota(jnp.int32, (STEPS, COLS, R), 2)
    low_mask = (columns < tile_ranks[:, :, None]).astype(jnp.float32) * (1.0 - tile_flags)[:, :, None]
    left_eff = left_factor * low_mask[:, :, None, :]
    dense_eff = dense_tiles * tile_flags[:, :, None, None]
    known = [earlier[index_j] for index_j in range(PREV)]
    solved = []
    for block_index in range(STEPS):
        pending = right_side[block_index]
        for index_j in range(PREV + block_index):
            source = known[index_j]
            projected = jnp.dot(right_factor[block_index, index_j].T, source, precision=HIGHEST)
            pending = pending - jnp.dot(dense_eff[block_index, index_j], source, precision=HIGHEST)
            pending = pending - jnp.dot(left_eff[block_index, index_j], projected, precision=HIGHEST)
        solved_block = jnp.dot(inverse_diag[block_index], pending, precision=HIGHEST)
        known.append(solved_block)
        solved.append(solved_block)
    return jnp.stack(solved)
```

```python
import functools

import jax
import jax.numpy as jnp
from jax import lax
from jax.experimental import pallas as pl
from jax.experimental.pallas import tpu as pltpu
from jax.sharding import PartitionSpec as P

HIGHEST = lax.Precision.HIGHEST
VMEM_LIMIT = 24 * 1024 * 1024


def any_mesh(
    right_side,
    earlier,
    inverse_diag,
    dense_tiles,
    left_factor,
    right_factor,
    tile_ranks,
    dense_flags,
):
    count_steps = right_side.shape[0]
    prev_cols = earlier.shape[0]
    rank_pad = left_factor.shape[3]
    tile_flags = dense_flags.astype(jnp.float32)
    columns = lax.broadcasted_iota(jnp.int32, tile_ranks.shape + (rank_pad,), 2)
    low_mask = (columns < tile_ranks[:, :, None]).astype(jnp.float32) * (1.0 - tile_flags)[
        :, :, None
    ]
    left_eff = left_factor * low_mask[:, :, None, :]
    tile_rows = (
        lax.all_gather(dense_tiles, "pcol", axis=3, tiled=True) * tile_flags[:, :, None, None]
    )
    inverse_rows = lax.all_gather(inverse_diag, "pcol", axis=2, tiled=True)
    early_sum = jnp.einsum(
        "kjrc,jcs->krs",
        tile_rows[:, :prev_cols],
        lax.all_gather(earlier, "prow", axis=1, tiled=True),
        precision=HIGHEST,
    )
    partial_value = jnp.einsum(
        "kjcq,jcs->kjqs", right_factor[:, :prev_cols], earlier, precision=HIGHEST
    )
    early_coeffs = lax.psum(partial_value, "prow")
    early_sum = early_sum + jnp.einsum(
        "kjrq,kjqs->krs", left_eff[:, :prev_cols], early_coeffs, precision=HIGHEST
    )
    pending = right_side - early_sum
    outputs = []
    for block_index in range(count_steps):
        residual_whole = lax.all_gather(pending[block_index], "prow", axis=0, tiled=True)
        solved_own = jnp.dot(inverse_rows[block_index], residual_whole, precision=HIGHEST)
        outputs.append(solved_own)
        if block_index + 1 < count_steps:
            solved_whole = lax.all_gather(solved_own, "prow", axis=0, tiled=True)
            column = prev_cols + block_index
            later = slice(block_index + 1, None)
            dense_part = jnp.einsum(
                "krc,cs->krs", tile_rows[later, column], solved_whole, precision=HIGHEST
            )
            projected = lax.psum(
                jnp.einsum(
                    "kcq,cs->kqs", right_factor[later, column], solved_own, precision=HIGHEST
                ),
                "prow",
            )
            low_part = jnp.einsum(
                "krq,kqs->krs", left_eff[later, column], projected, precision=HIGHEST
            )
            pending = pending.at[later].add(-(dense_part + low_part))
    return jnp.stack(outputs)


def halves(value):
    high = value.astype(jnp.bfloat16)
    low = (value - high.astype(jnp.float32)).astype(jnp.bfloat16)
    return high, low


def dot_split(left, right, dims=(((1,), (0,)), ((), ()))):
    axis_left = 1 - dims[0][0][0]
    axis_right = 1 - dims[0][1][0]
    rows, cols = left.shape[axis_left], right.shape[axis_right]
    left2 = jnp.concatenate(halves(left), axis=axis_left)
    right2 = jnp.concatenate(halves(right), axis=axis_right)
    out = lax.dot_general(left2, right2, dims, preferred_element_type=jnp.float32)
    return (out[:rows, :cols] + (out[:rows, cols:] + out[rows:, :cols])) + out[rows:, cols:]


def merge_kernel(step, count, ranks_ref, flags_ref, dense_ref, left_ref, right_ref, inv_ref, out_ref):
    rank_pad, rows = left_ref.shape[2:]
    row_at = lax.broadcasted_iota(jnp.int32, (rank_pad, rows), 0)
    for col in range(count):
        flag = flags_ref[step, col].astype(jnp.float32)
        mask = jnp.where(row_at < ranks_ref[step, col], 1.0 - flag, 0.0)
        low = dot_split(left_ref[0, col] * mask, right_ref[col], (((0,), (0,)), ((), ())))
        out_ref[col] = dense_ref[0, col] * flag + low
    out_ref[count] = inv_ref[0]


def product_kernel(n, sign, blocks, tiles, *refs):
    strips = refs[:n]
    sources = refs[n : n + n * blocks]
    rest = refs[n + n * blocks :]
    base_ref, (out_ref, source_scr) = (rest[0], rest[1:]) if sign else (None, rest)
    nb = out_ref.shape[-2]
    per_block = tiles // blocks
    turn = lax.axis_index("prow") ^ lax.axis_index("pcol")
    for slot in range(n):
        place = pl.multiple_of((turn ^ slot) * nb, nb)
        for block in range(blocks):
            ref = sources[block * n + slot]
            for tile in range(per_block):
                value = ref[tile] if len(ref.shape) == 3 else ref[...]
                source_scr[block * per_block + tile, pl.ds(place, nb), :] = value
    total = None
    for tile in range(tiles):
        strip = jnp.concatenate([strips[d][tile] for d in range(n)], axis=1)
        part = dot_split(strip, source_scr[tile])
        total = part if total is None else total + part
    if sign:
        base = base_ref[0] if len(base_ref.shape) == 3 else base_ref[...]
        total = base - total
    out_ref[...] = total


def spec_of(shape, index=None):
    if index is None:
        return pl.BlockSpec(shape, lambda i: (0,) * len(shape))
    return pl.BlockSpec(shape, lambda i: index)


def square_mesh(
    n,
    right_side,
    earlier,
    inverse_diag,
    dense_tiles,
    left_factor,
    right_factor,
    tile_ranks,
    dense_flags,
):
    steps, nb, rhs = right_side.shape
    prev = earlier.shape[0]
    cols = dense_tiles.shape[1]
    rank_pad = left_factor.shape[3]
    left_t = jnp.swapaxes(left_factor, 2, 3)
    right_t = jnp.swapaxes(right_factor, 2, 3)
    params = pltpu.CompilerParams(vmem_limit_bytes=VMEM_LIMIT)
    f32 = jnp.float32

    def shift(value, axis, step):
        return lax.ppermute(value, axis, [(i, i ^ step) for i in range(n)])

    def over_rows(value):
        return [value] + [shift(value, "prow", d) for d in range(1, n)]

    flip = [(a * n + b, b * n + a) for a in range(n) for b in range(n)]

    known = over_rows(earlier)
    strips = []
    for step in range(steps):
        count = prev + step
        right_own = lax.ppermute(right_t[step, :count], ("prow", "pcol"), flip)
        own = pl.pallas_call(
            functools.partial(merge_kernel, step, count),
            grid=(1,),
            out_shape=jax.ShapeDtypeStruct((count + 1, nb, nb), f32),
            in_specs=[
                pl.BlockSpec(memory_space=pltpu.SMEM),
                pl.BlockSpec(memory_space=pltpu.SMEM),
                spec_of((1, cols, nb, nb), (step, 0, 0, 0)),
                spec_of((1, cols, rank_pad, nb), (step, 0, 0, 0)),
                spec_of((count, rank_pad, nb)),
                spec_of((1, nb, nb), (step, 0, 0)),
            ],
            out_specs=spec_of((count + 1, nb, nb)),
            compiler_params=params,
            name=f"merge{step}",
        )(tile_ranks, dense_flags, dense_tiles, left_t, right_own, inverse_diag)
        slots = [own]
        reach = n // 2
        while reach >= 1:
            slots = slots + [shift(v, "pcol", reach) for v in slots]
            reach //= 2
        order = [0]
        reach = n // 2
        while reach >= 1:
            order = order + [o ^ reach for o in order]
            reach //= 2
        strips.append([slots[order.index(d)] for d in range(n)])

    def product(step, first, tiles, blocks, base, name):
        args = list(strips[step])
        specs = [spec_of((tiles, nb, nb), (first // tiles, 0, 0))] * n
        for block in blocks:
            for value in block:
                args.append(value)
                specs.append(spec_of(value.shape))
        if base is not None:
            value, index = base
            args.append(value)
            specs.append(
                spec_of((nb, rhs)) if index is None else spec_of((1, nb, rhs), (index, 0, 0))
            )
        return pl.pallas_call(
            functools.partial(
                product_kernel, n, 0 if base is None else 1, len(blocks), tiles
            ),
            grid=(1,),
            out_shape=jax.ShapeDtypeStruct((nb, rhs), f32),
            in_specs=specs,
            out_specs=spec_of((nb, rhs)),
            scratch_shapes=[pltpu.VMEM((tiles, n * nb, rhs), f32)],
            compiler_params=params,
            name=name,
        )(*args)

    pending = [
        product(step, 0, prev, [known], (right_side, step), f"early{step}")
        for step in range(steps)
    ]
    solved = []
    for step in range(steps):
        whole = over_rows(pending[step])
        solved.append(product(step, prev + step, 1, [whole], None, f"solve{step}"))
        if step + 1 < steps:
            block = over_rows(solved[step])
            for later in range(step + 1, steps):
                pending[later] = product(
                    later, prev + step, 1, [block], (pending[later], None), f"update{later}{step}"
                )
    return jnp.stack(solved)


def solution(mesh):
    placed = (
        P("groups", "prow", "pcol"),
        P("groups", "prow", "pcol"),
        P("groups", "prow", "pcol"),
        P("groups", None, "prow", "pcol"),
        P("groups", None, "prow", None),
        P("groups", None, "prow", None),
        P("groups", None),
        P("groups", None),
    )
    n = mesh.shape["prow"]
    square = n == mesh.shape["pcol"] and n & (n - 1) == 0 and n <= 8

    def local(*args):
        nb, cols = args[3].shape[2:]
        if square and nb % 128 == 0 and cols % 128 == 0 and args[0].shape[2] % 128 == 0:
            return square_mesh(n, *args)
        return any_mesh(*args)

    return jax.shard_map(
        local, mesh=mesh, in_specs=placed, out_specs=P("groups", "prow", "pcol"), check_vma=False
    )
```

```python
import functools

import jax
import jax.numpy as jnp
from jax import lax
from jax.experimental import pallas as pl
from jax.experimental.pallas import tpu as pltpu
from jax.sharding import PartitionSpec as P

HIGHEST = lax.Precision.HIGHEST
VMEM_LIMIT = 24 * 1024 * 1024


def any_mesh(
    right_side,
    earlier,
    inverse_diag,
    dense_tiles,
    left_factor,
    right_factor,
    tile_ranks,
    dense_flags,
):
    count_steps = right_side.shape[0]
    prev_cols = earlier.shape[0]
    rank_pad = left_factor.shape[3]
    tile_flags = dense_flags.astype(jnp.float32)
    columns = lax.broadcasted_iota(jnp.int32, tile_ranks.shape + (rank_pad,), 2)
    low_mask = (columns < tile_ranks[:, :, None]).astype(jnp.float32) * (1.0 - tile_flags)[
        :, :, None
    ]
    left_eff = left_factor * low_mask[:, :, None, :]
    tile_rows = (
        lax.all_gather(dense_tiles, "pcol", axis=3, tiled=True) * tile_flags[:, :, None, None]
    )
    inverse_rows = lax.all_gather(inverse_diag, "pcol", axis=2, tiled=True)
    early_sum = jnp.einsum(
        "kjrc,jcs->krs",
        tile_rows[:, :prev_cols],
        lax.all_gather(earlier, "prow", axis=1, tiled=True),
        precision=HIGHEST,
    )
    partial_value = jnp.einsum(
        "kjcq,jcs->kjqs", right_factor[:, :prev_cols], earlier, precision=HIGHEST
    )
    early_coeffs = lax.psum(partial_value, "prow")
    early_sum = early_sum + jnp.einsum(
        "kjrq,kjqs->krs", left_eff[:, :prev_cols], early_coeffs, precision=HIGHEST
    )
    pending = right_side - early_sum
    outputs = []
    for block_index in range(count_steps):
        residual_whole = lax.all_gather(pending[block_index], "prow", axis=0, tiled=True)
        solved_own = jnp.dot(inverse_rows[block_index], residual_whole, precision=HIGHEST)
        outputs.append(solved_own)
        if block_index + 1 < count_steps:
            solved_whole = lax.all_gather(solved_own, "prow", axis=0, tiled=True)
            column = prev_cols + block_index
            later = slice(block_index + 1, None)
            dense_part = jnp.einsum(
                "krc,cs->krs", tile_rows[later, column], solved_whole, precision=HIGHEST
            )
            projected = lax.psum(
                jnp.einsum(
                    "kcq,cs->kqs", right_factor[later, column], solved_own, precision=HIGHEST
                ),
                "prow",
            )
            low_part = jnp.einsum(
                "krq,kqs->krs", left_eff[later, column], projected, precision=HIGHEST
            )
            pending = pending.at[later].add(-(dense_part + low_part))
    return jnp.stack(outputs)


def halves(value):
    high = value.astype(jnp.bfloat16)
    low = (value - high.astype(jnp.float32)).astype(jnp.bfloat16)
    return high, low


def dot_split(left, right, dims=(((1,), (0,)), ((), ()))):
    axis_left = 1 - dims[0][0][0]
    axis_right = 1 - dims[0][1][0]
    rows, cols = left.shape[axis_left], right.shape[axis_right]
    left2 = jnp.concatenate(halves(left), axis=axis_left)
    right2 = jnp.concatenate(halves(right), axis=axis_right)
    out = lax.dot_general(left2, right2, dims, preferred_element_type=jnp.float32)
    return (out[:rows, :cols] + (out[:rows, cols:] + out[rows:, :cols])) + out[rows:, cols:]


def pack_kernel(count, right_ref, *refs):
    refs[-1][...] = right_ref[0, :count]


def merge_kernel(step, count, ranks_ref, flags_ref, dense_ref, left_ref, right_ref, inv_ref, out_ref):
    rank_pad, rows = left_ref.shape[2:]
    row_at = lax.broadcasted_iota(jnp.int32, (rank_pad, rows), 0)
    for col in range(count):
        flag = flags_ref[step, col].astype(jnp.float32)
        mask = jnp.where(row_at < ranks_ref[step, col], 1.0 - flag, 0.0)
        low = dot_split(left_ref[0, col] * mask, right_ref[col], (((0,), (0,)), ((), ())))
        out_ref[col] = dense_ref[0, col] * flag + low
    out_ref[count] = inv_ref[0]


def product_kernel(n, based, blocks, tiles, before, *refs):
    strips = refs[:n]
    sources = refs[n : n + n * blocks]
    rest = refs[n + n * blocks :]
    out_ref, source_scr = rest[-2:]
    nb = out_ref.shape[-2]
    per_block = tiles // blocks
    turn = lax.axis_index("prow") ^ lax.axis_index("pcol")
    for slot in range(n):
        place = pl.multiple_of((turn ^ slot) * nb, nb)
        for block in range(blocks):
            ref = sources[block * n + slot]
            for tile in range(per_block):
                value = ref[tile] if len(ref.shape) == 3 else ref[...]
                source_scr[block * per_block + tile, pl.ds(place, nb), :] = value
    total = None
    for tile in range(tiles):
        strip = jnp.concatenate([strips[d][tile] for d in range(n)], axis=1)
        part = dot_split(strip, source_scr[tile])
        total = part if total is None else total + part
    if based:
        base_ref = rest[0]
        base = base_ref[0] if len(base_ref.shape) == 3 else base_ref[...]
        total = base - total
    if before < 0:
        out_ref[...] = total
    else:
        for index in range(before):
            out_ref[index] = rest[index][...]
        out_ref[before] = total


def spec_of(shape, index=None):
    if index is None:
        return pl.BlockSpec(shape, lambda i: (0,) * len(shape))
    return pl.BlockSpec(shape, lambda i: index)


def square_mesh(
    n,
    right_side,
    earlier,
    inverse_diag,
    dense_tiles,
    left_factor,
    right_factor,
    tile_ranks,
    dense_flags,
):
    steps, nb, rhs = right_side.shape
    prev = earlier.shape[0]
    cols = dense_tiles.shape[1]
    rank_pad = left_factor.shape[3]
    left_t = jnp.swapaxes(left_factor, 2, 3)
    right_t = jnp.swapaxes(right_factor, 2, 3)
    params = pltpu.CompilerParams(vmem_limit_bytes=VMEM_LIMIT)
    f32 = jnp.float32

    def shift(value, axis, step):
        return lax.ppermute(value, axis, [(i, i ^ step) for i in range(n)])

    def over_rows(value):
        return [value] + [shift(value, "prow", d) for d in range(1, n)]

    flip = []
    for owner in range(n):
        for row in range(n):
            source = row ^ owner
            source = (source >> 1) | ((source & 1) * (n // 2)) if n > 1 else 0
            flip.append((owner * n + source, row * n + owner))

    any_spec = pl.BlockSpec(memory_space=pl.ANY)
    known = over_rows(earlier)
    strips = []
    own = []
    for step in range(steps):
        count = prev + step
        after = [] if step < 2 else [own[0]]
        packed = pl.pallas_call(
            functools.partial(pack_kernel, count),
            grid=(1,),
            out_shape=jax.ShapeDtypeStruct((count, rank_pad, nb), f32),
            in_specs=[spec_of((1, cols, rank_pad, nb), (step, 0, 0, 0))] + [any_spec] * len(after),
            out_specs=spec_of((count, rank_pad, nb)),
            compiler_params=params,
            name=f"pack{step}",
        )(right_t, *after)
        right_own = lax.ppermute(packed, ("prow", "pcol"), flip)
        own.append(pl.pallas_call(
            functools.partial(merge_kernel, step, count),
            grid=(1,),
            out_shape=jax.ShapeDtypeStruct((count + 1, nb, nb), f32),
            in_specs=[
                pl.BlockSpec(memory_space=pltpu.SMEM),
                pl.BlockSpec(memory_space=pltpu.SMEM),
                spec_of((1, cols, nb, nb), (step, 0, 0, 0)),
                spec_of((1, cols, rank_pad, nb), (step, 0, 0, 0)),
                spec_of((count, rank_pad, nb)),
                spec_of((1, nb, nb), (step, 0, 0)),
            ],
            out_specs=spec_of((count + 1, nb, nb)),
            compiler_params=params,
            name=f"merge{step}",
        )(tile_ranks, dense_flags, dense_tiles, left_t, right_own, inverse_diag))
        slots = [own[step]]
        reach = n // 2
        while reach >= 1:
            slots = slots + [shift(v, "pcol", reach) for v in slots]
            reach //= 2
        order = [0]
        reach = n // 2
        while reach >= 1:
            order = order + [o ^ reach for o in order]
            reach //= 2
        strips.append([slots[order.index(d)] for d in range(n)])

    def product(step, first, tiles, blocks, name, base=None, after=(), stacked=None):
        args = list(strips[step])
        specs = [spec_of((tiles, nb, nb), (first // tiles, 0, 0))] * n
        for block in blocks:
            for value in block:
                args.append(value)
                specs.append(spec_of(value.shape))
        if base is not None:
            value, index = base
            args.append(value)
            specs.append(
                spec_of((nb, rhs)) if index is None else spec_of((1, nb, rhs), (index, 0, 0))
            )
        shape, before = (nb, rhs), -1
        if stacked is not None:
            before = len(stacked)
            shape = (before + 1, nb, rhs)
            args += stacked
            specs += [spec_of((nb, rhs))] * before
        args += after
        specs += [any_spec] * len(after)
        return pl.pallas_call(
            functools.partial(product_kernel, n, base is not None, len(blocks), tiles, before),
            grid=(1,),
            out_shape=jax.ShapeDtypeStruct(shape, f32),
            in_specs=specs,
            out_specs=spec_of(shape),
            scratch_shapes=[pltpu.VMEM((tiles, n * nb, rhs), f32)],
            compiler_params=params,
            name=name,
        )(*args)

    def early(step):
        return product(step, 0, prev, [known], f"early{step}", (right_side, step))

    pending = [early(step) for step in range(steps)]
    waits = {("solve", 0): 1, ("update", 1): 2, ("solve", 1): 3}
    fronts = list(pending)
    solved = []
    for step in range(steps):
        whole = over_rows(pending[step])
        ahead = waits.get(("solve", step), 0)
        after = [fronts[ahead]] if step < ahead < steps else []
        stacked = solved if step + 1 == steps else None
        block = product(step, prev + step, 1, [whole], f"solve{step}", after=after, stacked=stacked)
        if stacked is not None:
            return block
        solved.append(block)
        spread = over_rows(block)
        for later in range(step + 1, steps):
            ahead = waits.get(("update", later), 0) if later == step + 1 else 0
            after = [fronts[ahead]] if later < ahead < steps else []
            pending[later] = product(
                later, prev + step, 1, [spread], f"update{later}{step}", (pending[later], None), after
            )
    return None


def solution(mesh):
    placed = (
        P("groups", "prow", "pcol"),
        P("groups", "prow", "pcol"),
        P("groups", "prow", "pcol"),
        P("groups", None, "prow", "pcol"),
        P("groups", None, "prow", None),
        P("groups", None, "prow", None),
        P("groups", None),
        P("groups", None),
    )
    n = mesh.shape["prow"]
    square = n == mesh.shape["pcol"] and n & (n - 1) == 0 and n <= 8

    def local(*args):
        nb, cols = args[3].shape[2:]
        if square and nb % 128 == 0 and cols % 128 == 0 and args[0].shape[2] % 128 == 0:
            return square_mesh(n, *args)
        return any_mesh(*args)

    return jax.shard_map(
        local, mesh=mesh, in_specs=placed, out_specs=P("groups", "prow", "pcol"), check_vma=False
    )
```

```python
import functools

import jax
import jax.numpy as jnp
from jax import lax
from jax.experimental import pallas as pl
from jax.experimental.pallas import tpu as pltpu
from jax.sharding import PartitionSpec as P

HIGHEST = lax.Precision.HIGHEST
VMEM_LIMIT = 24 * 1024 * 1024


def any_mesh(
    right_side,
    earlier,
    inverse_diag,
    dense_tiles,
    left_factor,
    right_factor,
    tile_ranks,
    dense_flags,
):
    count_steps = right_side.shape[0]
    prev_cols = earlier.shape[0]
    rank_pad = left_factor.shape[3]
    tile_flags = dense_flags.astype(jnp.float32)
    columns = lax.broadcasted_iota(jnp.int32, tile_ranks.shape + (rank_pad,), 2)
    low_mask = (columns < tile_ranks[:, :, None]).astype(jnp.float32) * (1.0 - tile_flags)[
        :, :, None
    ]
    left_eff = left_factor * low_mask[:, :, None, :]
    tile_rows = (
        lax.all_gather(dense_tiles, "pcol", axis=3, tiled=True) * tile_flags[:, :, None, None]
    )
    inverse_rows = lax.all_gather(inverse_diag, "pcol", axis=2, tiled=True)
    early_sum = jnp.einsum(
        "kjrc,jcs->krs",
        tile_rows[:, :prev_cols],
        lax.all_gather(earlier, "prow", axis=1, tiled=True),
        precision=HIGHEST,
    )
    partial_value = jnp.einsum(
        "kjcq,jcs->kjqs", right_factor[:, :prev_cols], earlier, precision=HIGHEST
    )
    early_coeffs = lax.psum(partial_value, "prow")
    early_sum = early_sum + jnp.einsum(
        "kjrq,kjqs->krs", left_eff[:, :prev_cols], early_coeffs, precision=HIGHEST
    )
    pending = right_side - early_sum
    outputs = []
    for block_index in range(count_steps):
        residual_whole = lax.all_gather(pending[block_index], "prow", axis=0, tiled=True)
        solved_own = jnp.dot(inverse_rows[block_index], residual_whole, precision=HIGHEST)
        outputs.append(solved_own)
        if block_index + 1 < count_steps:
            solved_whole = lax.all_gather(solved_own, "prow", axis=0, tiled=True)
            column = prev_cols + block_index
            later = slice(block_index + 1, None)
            dense_part = jnp.einsum(
                "krc,cs->krs", tile_rows[later, column], solved_whole, precision=HIGHEST
            )
            projected = lax.psum(
                jnp.einsum(
                    "kcq,cs->kqs", right_factor[later, column], solved_own, precision=HIGHEST
                ),
                "prow",
            )
            low_part = jnp.einsum(
                "krq,kqs->krs", left_eff[later, column], projected, precision=HIGHEST
            )
            pending = pending.at[later].add(-(dense_part + low_part))
    return jnp.stack(outputs)


def halves(value):
    high = value.astype(jnp.bfloat16)
    low = (value - high.astype(jnp.float32)).astype(jnp.bfloat16)
    return high, low


def dot_split(left, right, dims=(((1,), (0,)), ((), ()))):
    axis_left = 1 - dims[0][0][0]
    axis_right = 1 - dims[0][1][0]
    rows, cols = left.shape[axis_left], right.shape[axis_right]
    left2 = jnp.concatenate(halves(left), axis=axis_left)
    right2 = jnp.concatenate(halves(right), axis=axis_right)
    out = lax.dot_general(left2, right2, dims, preferred_element_type=jnp.float32)
    return (out[:rows, :cols] + (out[:rows, cols:] + out[rows:, :cols])) + out[rows:, cols:]


def pack_kernel(pieces, right_ref, *refs):
    out_ref = refs[-1]
    place = 0
    for index, count in enumerate(pieces):
        out_ref[place : place + count] = right_ref[index, :count]
        place += count


def merge_kernel(order, ranks_ref, flags_ref, dense_ref, left_ref, right_ref, inv_ref, *refs):
    out_ref = refs[-1]
    rank_pad, rows = left_ref.shape[2:]
    row_at = lax.broadcasted_iota(jnp.int32, (rank_pad, rows), 0)
    for place, (first, step, col, packed) in enumerate(order):
        if col is None:
            out_ref[place] = inv_ref[step - first]
            continue
        flag = flags_ref[step, col].astype(jnp.float32)
        mask = jnp.where(row_at < ranks_ref[step, col], 1.0 - flag, 0.0)
        left = left_ref[step - first, col] * mask
        low = dot_split(left, right_ref[packed], (((0,), (0,)), ((), ())))
        out_ref[place] = dense_ref[step - first, col] * flag + low


def product_kernel(n, slots, wholes, based, tiles, before, *refs):
    count = n if slots else 1
    strips = refs[:count]
    sources = refs[count : count + (1 if wholes else n)]
    rest = refs[count + len(sources) :]
    out_ref, source_scr = rest[-2:]
    nb = out_ref.shape[-2]
    turn = 0
    if slots:
        turn = turn ^ lax.axis_index("pcol")
    if not wholes:
        turn = turn ^ lax.axis_index("prow")
    for slot in range(n):
        place = (turn ^ slot) * nb
        if slots or not wholes:
            place = pl.multiple_of(place, nb)
        for tile in range(tiles):
            value = sources[0][slot, tile] if wholes else sources[slot][...]
            source_scr[tile, pl.ds(place, nb), :] = value
    total = None
    for tile in range(tiles):
        parts = [strips[d][tile] if slots else strips[0][d, tile] for d in range(n)]
        part = dot_split(jnp.concatenate(parts, axis=1), source_scr[tile])
        total = part if total is None else total + part
    if based:
        base_ref = rest[0]
        base = base_ref[0] if len(base_ref.shape) == 3 else base_ref[...]
        total = base - total
    if before < 0:
        out_ref[...] = total
    else:
        for index in range(before):
            out_ref[index] = rest[index][...]
        out_ref[before] = total


def spec_of(shape, index=None):
    if index is None:
        return pl.BlockSpec(shape, lambda i: (0,) * len(shape))
    return pl.BlockSpec(shape, lambda i: index)


def square_mesh(
    n,
    right_side,
    earlier,
    inverse_diag,
    dense_tiles,
    left_factor,
    right_factor,
    tile_ranks,
    dense_flags,
):
    steps, nb, rhs = right_side.shape
    prev = earlier.shape[0]
    cols = dense_tiles.shape[1]
    rank_pad = left_factor.shape[3]
    left_t = jnp.swapaxes(left_factor, 2, 3)
    right_t = jnp.swapaxes(right_factor, 2, 3)
    params = pltpu.CompilerParams(vmem_limit_bytes=VMEM_LIMIT)
    f32 = jnp.float32

    def shift(value, axis, step):
        return lax.ppermute(value, axis, [(i, i ^ step) for i in range(n)])

    def over_rows(value):
        return [value] + [shift(value, "prow", d) for d in range(1, n)]

    flip = []
    for owner in range(n):
        for row in range(n):
            source = row ^ owner
            source = (source >> 1) | ((source & 1) * (n // 2)) if n > 1 else 0
            flip.append((owner * n + source, row * n + owner))

    any_spec = pl.BlockSpec(memory_space=pl.ANY)

    def packed(first, pieces, after=()):
        shape = (sum(pieces), rank_pad, nb)
        own = pl.pallas_call(
            functools.partial(pack_kernel, pieces),
            grid=(1,),
            out_shape=jax.ShapeDtypeStruct(shape, f32),
            in_specs=[spec_of((len(pieces), cols, rank_pad, nb), (first // len(pieces), 0, 0, 0))]
            + [any_spec] * len(after),
            out_specs=spec_of(shape),
            compiler_params=params,
            name=f"pack{first}",
        )(right_t, *after)
        return lax.ppermute(own, ("prow", "pcol"), flip)

    def merged(order, block_rows, right_own, after=()):
        first = order[0][0]
        shape = (len(order), nb, nb)
        index = first // block_rows
        return pl.pallas_call(
            functools.partial(merge_kernel, order),
            grid=(1,),
            out_shape=jax.ShapeDtypeStruct(shape, f32),
            in_specs=[
                pl.BlockSpec(memory_space=pltpu.SMEM),
                pl.BlockSpec(memory_space=pltpu.SMEM),
                spec_of((block_rows, cols, nb, nb), (index, 0, 0, 0)),
                spec_of((block_rows, cols, rank_pad, nb), (index, 0, 0, 0)),
                spec_of(right_own.shape),
                spec_of((block_rows, nb, nb), (index, 0, 0)),
            ]
            + [any_spec] * len(after),
            out_specs=spec_of(shape),
            compiler_params=params,
            name=f"merge{first}",
        )(tile_ranks, dense_flags, dense_tiles, left_t, right_own, inverse_diag, *after)

    def by_distance(own):
        held = {0: own}
        reach = n // 2
        while reach >= 1:
            held |= {d ^ reach: shift(v, "pcol", reach) for d, v in held.items()}
            reach //= 2
        return [held[d] for d in range(n)]

    def product(strip, first, tiles, source, name, base=None, stacked=None):
        slots, wholes = isinstance(strip, list), not isinstance(source, list)
        if slots:
            args = list(strip)
            specs = [spec_of((tiles, nb, nb), (first // tiles, 0, 0))] * n
        else:
            args = [strip]
            specs = [spec_of((n, tiles, nb, nb), (0, first // tiles, 0, 0))]
        values = [source] if wholes else source
        args += values
        specs += [spec_of(value.shape) for value in values]
        if base is not None:
            value, index = base
            args.append(value)
            specs.append(
                spec_of((nb, rhs)) if index is None else spec_of((1, nb, rhs), (index, 0, 0))
            )
        shape, before = (nb, rhs), -1
        if stacked is not None:
            before = len(stacked)
            shape = (before + 1, nb, rhs)
            args += stacked
            specs += [spec_of((nb, rhs))] * before
        return pl.pallas_call(
            functools.partial(product_kernel, n, slots, wholes, base is not None, tiles, before),
            grid=(1,),
            out_shape=jax.ShapeDtypeStruct(shape, f32),
            in_specs=specs,
            out_specs=spec_of(shape),
            scratch_shapes=[pltpu.VMEM((tiles, n * nb, rhs), f32)],
            compiler_params=params,
            name=name,
        )(*args)

    known = lax.all_gather(earlier, "prow", axis=0)

    ahead = 2 if steps % 2 == 0 else 1
    groups = [tuple(range(ahead))] + [(step,) for step in range(ahead, steps)]
    strips, where, orders = [], {}, []
    for number, rows in enumerate(groups):
        starts = {step: sum(prev + other for other in rows if other < step) for step in rows}
        order = [(step, col) for step in rows for col in range(prev)]
        order += [(step, prev + col) for step in rows for col in range(step)]
        order += [(step, None) for step in rows]
        for place, key in enumerate(order):
            where[key] = (number, place)
        orders.append(
            tuple((rows[0], s, c, None if c is None else starts[s] + c) for s, c in order)
        )

    right_ahead = packed(0, tuple(prev + step for step in groups[0]))
    own = merged(orders[0], ahead, right_ahead)
    strips.append(by_distance(own))
    later = [packed(step, (prev + step,), [own]) for step in range(ahead, steps)]

    def merge_next(whole):
        number = len(strips)
        if number < len(groups):
            own = merged(orders[number], 1, later[number - 1], whole[1:])
            strips.append(lax.all_gather(own, "pcol", axis=0))

    def times(key, tiles, source, name, **rest):
        number, place = where[key]
        return product(strips[number], place, tiles, source, name, **rest)

    solved, spread = [], []
    for step in range(steps):
        pending = times((step, 0), prev, known, f"early{step}", base=(right_side, step))
        for index in range(step):
            name = f"update{step}{index}"
            pending = times((step, prev + index), 1, spread[index], name, base=(pending, None))
        whole = over_rows(pending)
        merge_next(whole)
        if step + 1 == steps:
            return times((step, None), 1, whole, f"solve{step}", stacked=solved)
        solved.append(times((step, None), 1, whole, f"solve{step}"))
        spread.append(over_rows(solved[step]))
        merge_next(spread[step])
    return None


def solution(mesh):
    placed = (
        P("groups", "prow", "pcol"),
        P("groups", "prow", "pcol"),
        P("groups", "prow", "pcol"),
        P("groups", None, "prow", "pcol"),
        P("groups", None, "prow", None),
        P("groups", None, "prow", None),
        P("groups", None),
        P("groups", None),
    )
    n = mesh.shape["prow"]
    square = n == mesh.shape["pcol"] and n & (n - 1) == 0 and n <= 8

    def local(*args):
        nb, cols = args[3].shape[2:]
        if square and nb % 128 == 0 and cols % 128 == 0 and args[0].shape[2] % 128 == 0:
            return square_mesh(n, *args)
        return any_mesh(*args)

    return jax.shard_map(
        local, mesh=mesh, in_specs=placed, out_specs=P("groups", "prow", "pcol"), check_vma=False
    )
```

```python
import functools

import jax
import jax.numpy as jnp
from jax import lax
from jax.experimental import pallas as pl
from jax.experimental.pallas import tpu as pltpu
from jax.sharding import PartitionSpec as P

HIGHEST = lax.Precision.HIGHEST
VMEM_LIMIT = 24 * 1024 * 1024


def any_mesh(
    right_side,
    earlier,
    inverse_diag,
    dense_tiles,
    left_factor,
    right_factor,
    tile_ranks,
    dense_flags,
):
    count_steps = right_side.shape[0]
    prev_cols = earlier.shape[0]
    rank_pad = left_factor.shape[3]
    tile_flags = dense_flags.astype(jnp.float32)
    columns = lax.broadcasted_iota(jnp.int32, tile_ranks.shape + (rank_pad,), 2)
    low_mask = (columns < tile_ranks[:, :, None]).astype(jnp.float32) * (1.0 - tile_flags)[
        :, :, None
    ]
    left_eff = left_factor * low_mask[:, :, None, :]
    tile_rows = (
        lax.all_gather(dense_tiles, "pcol", axis=3, tiled=True) * tile_flags[:, :, None, None]
    )
    inverse_rows = lax.all_gather(inverse_diag, "pcol", axis=2, tiled=True)
    early_sum = jnp.einsum(
        "kjrc,jcs->krs",
        tile_rows[:, :prev_cols],
        lax.all_gather(earlier, "prow", axis=1, tiled=True),
        precision=HIGHEST,
    )
    partial_value = jnp.einsum(
        "kjcq,jcs->kjqs", right_factor[:, :prev_cols], earlier, precision=HIGHEST
    )
    early_coeffs = lax.psum(partial_value, "prow")
    early_sum = early_sum + jnp.einsum(
        "kjrq,kjqs->krs", left_eff[:, :prev_cols], early_coeffs, precision=HIGHEST
    )
    pending = right_side - early_sum
    outputs = []
    for block_index in range(count_steps):
        residual_whole = lax.all_gather(pending[block_index], "prow", axis=0, tiled=True)
        solved_own = jnp.dot(inverse_rows[block_index], residual_whole, precision=HIGHEST)
        outputs.append(solved_own)
        if block_index + 1 < count_steps:
            solved_whole = lax.all_gather(solved_own, "prow", axis=0, tiled=True)
            column = prev_cols + block_index
            later = slice(block_index + 1, None)
            dense_part = jnp.einsum(
                "krc,cs->krs", tile_rows[later, column], solved_whole, precision=HIGHEST
            )
            projected = lax.psum(
                jnp.einsum(
                    "kcq,cs->kqs", right_factor[later, column], solved_own, precision=HIGHEST
                ),
                "prow",
            )
            low_part = jnp.einsum(
                "krq,kqs->krs", left_eff[later, column], projected, precision=HIGHEST
            )
            pending = pending.at[later].add(-(dense_part + low_part))
    return jnp.stack(outputs)


def halves(value, axis):
    high = value.astype(jnp.bfloat16)
    low = (value - high.astype(jnp.float32)).astype(jnp.bfloat16)
    return jnp.concatenate([high, low], axis=axis)


def dot_halves(left2, right2, dims=(((1,), (0,)), ((), ()))):
    rows = left2.shape[1 - dims[0][0][0]] // 2
    cols = right2.shape[1 - dims[0][1][0]] // 2
    out = lax.dot_general(left2, right2, dims, preferred_element_type=jnp.float32)
    return (out[:rows, :cols] + (out[:rows, cols:] + out[rows:, :cols])) + out[rows:, cols:]


def place_slots(scratch, refs, turn, nb):
    for slot, ref in enumerate(refs):
        place = pl.multiple_of((turn ^ slot) * nb, nb)
        if len(ref.shape) == 3:
            scratch[:, pl.ds(place, nb), :] = ref[...]
        else:
            scratch[pl.ds(place, nb), :] = ref[...]


def pack_kernel(pieces, right_ref, *refs):
    out_ref = refs[-1]
    place = 0
    for index, count in enumerate(pieces):
        out_ref[place : place + count] = right_ref[index, :count]
        place += count


def merge_kernel(order, ranks_ref, flags_ref, dense_ref, left_ref, right_ref, inv_ref, *refs):
    out_ref = refs[-1]
    rank_pad, rows = left_ref.shape[2:]
    row_at = lax.broadcasted_iota(jnp.int32, (rank_pad, rows), 0)
    for place, (first, step, col, packed) in enumerate(order):
        if col is None:
            out_ref[place] = inv_ref[step - first]
            continue
        flag = flags_ref[step, col].astype(jnp.float32)
        mask = jnp.where(row_at < ranks_ref[step, col], 1.0 - flag, 0.0)
        left = left_ref[step - first, col] * mask
        over_rows = (((0,), (0,)), ((), ()))
        low = dot_halves(halves(left, 1), halves(right_ref[packed], 1), over_rows)
        out_ref[place] = dense_ref[step - first, col] * flag + low


def early_kernel(n, slots, tiles, picks, solved_at, *refs):
    refs = list(refs)
    strips = [refs.pop(0) for _ in range(n if slots else 1)]
    sources = [refs.pop(0) for _ in range(n)]
    solved = [refs.pop(0) for _ in solved_at]
    base_ref = refs.pop(0)
    out_ref, *picked, source_scr = refs
    nb = out_ref.shape[0]
    turn = lax.axis_index("pcol") if slots else 0

    def strip(tile):
        parts = [strips[d][tile] if slots else strips[0][d, tile] for d in range(n)]
        return halves(jnp.concatenate(parts, axis=1), 0)

    place_slots(source_scr, sources, lax.axis_index("prow") ^ turn, nb)
    total = base_ref[0]
    for index in range(source_scr.shape[0]):
        total = total - dot_halves(strip(tiles + index), halves(source_scr[index], 1))
    for tile, ref in zip(solved_at, solved):
        total = total - dot_halves(strip(tile), halves(ref[...], 1))
    out_ref[...] = total
    if picks:
        for index, tile in enumerate(picks):
            for d in range(n):
                value = strips[d][tile] if slots else strips[0][d, tile]
                place = pl.multiple_of((turn ^ d) * nb, nb) if slots else d * nb
                picked[0][index, :, pl.ds(place, nb)] = halves(value, 0)


def inverse_kernel(n, whole_ref, *out_refs):
    nb = whole_ref.shape[-1]
    for step, out_ref in enumerate(out_refs):
        for row in range(n):
            for col in range(n):
                both = halves(whole_ref[row * n + col, step], 0)
                at = pl.ds(col * nb, nb)
                out_ref[pl.ds(row * nb, nb), at] = both[:nb]
                out_ref[pl.ds((n + row) * nb, nb), at] = both[nb:]


def step_kernel(n, *refs):
    inverse_ref, strip_ref, base_ref, pending_ref, solved_ref, scratch = refs[n:]
    nb = base_ref.shape[0]
    place_slots(scratch, refs[:n], lax.axis_index("prow"), nb)
    solved = dot_halves(inverse_ref[...], halves(scratch[...], 1))
    solved_ref[...] = solved
    pending_ref[...] = base_ref[...] - dot_halves(strip_ref[0], halves(solved, 1))


def last_kernel(n, *refs):
    strip_ref, *solved, out_ref, scratch = refs[n:]
    nb = out_ref.shape[1]
    own = lax.axis_index("prow")
    place_slots(scratch, refs[:n], own, nb)
    for step, ref in enumerate(solved):
        out_ref[step] = ref[pl.ds(pl.multiple_of(own * nb, nb), nb), :]
    out_ref[len(solved)] = dot_halves(strip_ref[0], halves(scratch[...], 1))


def spec_of(shape, index=None):
    if index is None:
        return pl.BlockSpec(shape, lambda i: (0,) * len(shape))
    return pl.BlockSpec(shape, lambda i: index)


def square_mesh(
    n,
    right_side,
    earlier,
    inverse_diag,
    dense_tiles,
    left_factor,
    right_factor,
    tile_ranks,
    dense_flags,
):
    steps, nb, rhs = right_side.shape
    prev = earlier.shape[0]
    cols = dense_tiles.shape[1]
    rank_pad = left_factor.shape[3]
    left_t = jnp.swapaxes(left_factor, 2, 3)
    right_t = jnp.swapaxes(right_factor, 2, 3)
    params = pltpu.CompilerParams(vmem_limit_bytes=VMEM_LIMIT)
    f32 = jnp.float32

    def shift(value, axis, step):
        return lax.ppermute(value, axis, [(i, i ^ step) for i in range(n)])

    def over_rows(value):
        return [value] + [shift(value, "prow", d) for d in range(1, n)]

    flip = []
    for owner in range(n):
        for row in range(n):
            source = row ^ owner
            source = (source >> 1) | ((source & 1) * (n // 2)) if n > 1 else 0
            flip.append((owner * n + source, row * n + owner))

    any_spec = pl.BlockSpec(memory_space=pl.ANY)

    def packed(first, pieces, after=()):
        shape = (sum(pieces), rank_pad, nb)
        own = pl.pallas_call(
            functools.partial(pack_kernel, pieces),
            grid=(1,),
            out_shape=jax.ShapeDtypeStruct(shape, f32),
            in_specs=[spec_of((len(pieces), cols, rank_pad, nb), (first // len(pieces), 0, 0, 0))]
            + [any_spec] * len(after),
            out_specs=spec_of(shape),
            compiler_params=params,
            name=f"pack{first}",
        )(right_t, *after)
        return lax.ppermute(own, ("prow", "pcol"), flip)

    def merged(order, block_rows, right_own, after=()):
        first = order[0][0]
        shape = (len(order), nb, nb)
        index = first // block_rows
        return pl.pallas_call(
            functools.partial(merge_kernel, order),
            grid=(1,),
            out_shape=jax.ShapeDtypeStruct(shape, f32),
            in_specs=[
                pl.BlockSpec(memory_space=pltpu.SMEM),
                pl.BlockSpec(memory_space=pltpu.SMEM),
                spec_of((block_rows, cols, nb, nb), (index, 0, 0, 0)),
                spec_of((block_rows, cols, rank_pad, nb), (index, 0, 0, 0)),
                spec_of(right_own.shape),
                spec_of((block_rows, nb, nb), (index, 0, 0)),
            ]
            + [any_spec] * len(after),
            out_specs=spec_of(shape),
            compiler_params=params,
            name=f"merge{first}",
        )(tile_ranks, dense_flags, dense_tiles, left_t, right_own, inverse_diag, *after)

    def by_distance(own):
        held = {0: own}
        reach = n // 2
        while reach >= 1:
            held |= {d ^ reach: shift(v, "pcol", reach) for d, v in held.items()}
            reach //= 2
        return [held[d] for d in range(n)]

    def call(kernel, name, shapes, args, specs=None, scratch=()):
        specs = specs or [spec_of(value.shape) for value in args]
        many = isinstance(shapes, list)
        out_specs = [spec_of(x.shape) for x in shapes] if many else spec_of(shapes.shape)
        return pl.pallas_call(
            kernel,
            grid=(1,),
            out_shape=shapes,
            in_specs=specs,
            out_specs=out_specs,
            scratch_shapes=list(scratch),
            compiler_params=params,
            name=name,
        )(*args)

    known = over_rows(earlier)
    bf16 = jnp.bfloat16
    rows_all = n * nb
    block_shape = jax.ShapeDtypeStruct((nb, rhs), f32)
    whole_shape = jax.ShapeDtypeStruct((rows_all, rhs), f32)
    inverse_blocks = lax.all_gather(inverse_diag[: steps - 1], ("prow", "pcol"), axis=0)

    ahead = 2 if steps % 2 == 0 else 1
    groups = [tuple(range(ahead))] + [(step,) for step in range(ahead, steps)]
    strips, where, orders = [], {}, []
    for number, rows in enumerate(groups):
        starts = {step: sum(prev + other for other in rows if other < step) for step in rows}
        order = [(step, col) for step in rows for col in range(prev)]
        order += [(step, prev + col) for step in rows for col in range(step)]
        order += [(step, None) for step in rows if step + 1 == steps]
        for place, key in enumerate(order):
            where[key] = (number, place)
        orders.append(
            tuple((rows[0], s, c, None if c is None else starts[s] + c) for s, c in order)
        )

    right_ahead = packed(0, tuple(prev + step for step in groups[0]))
    own = merged(orders[0], ahead, right_ahead)
    strips.append(by_distance(own))
    later = [packed(step, (prev + step,), [own]) for step in range(ahead, steps)]
    def merge_later(whole):
        for number in range(1, len(groups)):
            own = merged(orders[number], 1, later[number - 1], whole[1:])
            strips.append(lax.all_gather(own, "pcol", axis=0))

    def early(step, solved):
        number, tiles = where[(step, 0)]
        strip = strips[number]
        slots = isinstance(strip, list)
        keys = [(step, prev + step - 1)] if step else []
        keys += [(step, None)] if step + 1 == steps else []
        picks = [where[key][1] for key in keys]
        solved_at = [where[(step, prev + index)][1] for index in range(len(solved))]
        args = (strip if slots else [strip]) + known + solved + [right_side]
        specs = [spec_of(value.shape) for value in args[:-1]] + [spec_of((1, nb, rhs), (step, 0, 0))]
        shapes = [block_shape]
        if picks:
            shapes.append(jax.ShapeDtypeStruct((len(picks), 2 * nb, rows_all), bf16))
        return call(
            functools.partial(early_kernel, n, slots, tiles, picks, solved_at),
            f"early{step}",
            shapes,
            args,
            specs,
            [pltpu.VMEM((prev, rows_all, rhs), f32)],
        )

    inverse = call(
        functools.partial(inverse_kernel, n),
        "inverses",
        [jax.ShapeDtypeStruct((2 * rows_all, rows_all), bf16)] * (steps - 1),
        [inverse_blocks],
    )
    room = [pltpu.VMEM((rows_all, rhs), f32)]
    strip_spec = spec_of((1, 2 * nb, rows_all), (0, 0, 0))
    pending, solved = early(0, [])[0], []
    for step in range(steps - 1):
        whole = over_rows(pending)
        if step == 0:
            merge_later(whole)
        base, chain = early(step + 1, solved)
        args = whole + [inverse[step], chain, base]
        specs = [spec_of(value.shape) for value in args]
        specs[n + 1] = strip_spec
        pending, block = call(
            functools.partial(step_kernel, n), f"step{step}", [block_shape, whole_shape], args, specs, room
        )
        solved.append(block)
    whole = over_rows(pending)
    args = whole + [chain] + solved
    specs = [spec_of(value.shape) for value in args]
    specs[n] = spec_of((1, 2 * nb, rows_all), (1, 0, 0))
    shape = jax.ShapeDtypeStruct((steps, nb, rhs), f32)
    return call(functools.partial(last_kernel, n), "last", shape, args, specs, room)


def solution(mesh):
    placed = (
        P("groups", "prow", "pcol"),
        P("groups", "prow", "pcol"),
        P("groups", "prow", "pcol"),
        P("groups", None, "prow", "pcol"),
        P("groups", None, "prow", None),
        P("groups", None, "prow", None),
        P("groups", None),
        P("groups", None),
    )
    n = mesh.shape["prow"]
    square = n > 1 and n == mesh.shape["pcol"] and n & (n - 1) == 0 and n <= 8

    def local(*args):
        nb, cols = args[3].shape[2:]
        if square and nb % 128 == 0 and cols % 128 == 0 and args[0].shape[2] % 128 == 0:
            return square_mesh(n, *args)
        return any_mesh(*args)

    return jax.shard_map(
        local, mesh=mesh, in_specs=placed, out_specs=P("groups", "prow", "pcol"), check_vma=False
    )
```

```python
import functools

import jax
import jax.numpy as jnp
from jax import lax
from jax.experimental import pallas as pl
from jax.experimental.pallas import tpu as pltpu
from jax.sharding import PartitionSpec as P

HIGHEST = lax.Precision.HIGHEST
VMEM_LIMIT = 24 * 1024 * 1024


def any_mesh(
    right_side,
    earlier,
    inverse_diag,
    dense_tiles,
    left_factor,
    right_factor,
    tile_ranks,
    dense_flags,
):
    count_steps = right_side.shape[0]
    prev_cols = earlier.shape[0]
    rank_pad = left_factor.shape[3]
    tile_flags = dense_flags.astype(jnp.float32)
    columns = lax.broadcasted_iota(jnp.int32, tile_ranks.shape + (rank_pad,), 2)
    low_mask = (columns < tile_ranks[:, :, None]).astype(jnp.float32) * (1.0 - tile_flags)[
        :, :, None
    ]
    left_eff = left_factor * low_mask[:, :, None, :]
    tile_rows = (
        lax.all_gather(dense_tiles, "pcol", axis=3, tiled=True) * tile_flags[:, :, None, None]
    )
    inverse_rows = lax.all_gather(inverse_diag, "pcol", axis=2, tiled=True)
    early_sum = jnp.einsum(
        "kjrc,jcs->krs",
        tile_rows[:, :prev_cols],
        lax.all_gather(earlier, "prow", axis=1, tiled=True),
        precision=HIGHEST,
    )
    partial_value = jnp.einsum(
        "kjcq,jcs->kjqs", right_factor[:, :prev_cols], earlier, precision=HIGHEST
    )
    early_coeffs = lax.psum(partial_value, "prow")
    early_sum = early_sum + jnp.einsum(
        "kjrq,kjqs->krs", left_eff[:, :prev_cols], early_coeffs, precision=HIGHEST
    )
    pending = right_side - early_sum
    outputs = []
    for block_index in range(count_steps):
        residual_whole = lax.all_gather(pending[block_index], "prow", axis=0, tiled=True)
        solved_own = jnp.dot(inverse_rows[block_index], residual_whole, precision=HIGHEST)
        outputs.append(solved_own)
        if block_index + 1 < count_steps:
            solved_whole = lax.all_gather(solved_own, "prow", axis=0, tiled=True)
            column = prev_cols + block_index
            later = slice(block_index + 1, None)
            dense_part = jnp.einsum(
                "krc,cs->krs", tile_rows[later, column], solved_whole, precision=HIGHEST
            )
            projected = lax.psum(
                jnp.einsum(
                    "kcq,cs->kqs", right_factor[later, column], solved_own, precision=HIGHEST
                ),
                "prow",
            )
            low_part = jnp.einsum(
                "krq,kqs->krs", left_eff[later, column], projected, precision=HIGHEST
            )
            pending = pending.at[later].add(-(dense_part + low_part))
    return jnp.stack(outputs)


def halves(value, axis):
    high = value.astype(jnp.bfloat16)
    low = (value - high.astype(jnp.float32)).astype(jnp.bfloat16)
    return jnp.concatenate([high, low], axis=axis)


def dot_halves(left2, right2, dims=(((1,), (0,)), ((), ()))):
    rows = left2.shape[1 - dims[0][0][0]] // 2
    cols = right2.shape[1 - dims[0][1][0]] // 2
    out = lax.dot_general(left2, right2, dims, preferred_element_type=jnp.float32)
    return (out[:rows, :cols] + (out[:rows, cols:] + out[rows:, :cols])) + out[rows:, cols:]


def pack_kernel(pieces, right_ref, *refs):
    out_ref = refs[-1]
    place = 0
    for index, count in enumerate(pieces):
        out_ref[place : place + count] = right_ref[index, :count]
        place += count


def merge_kernel(order, ranks_ref, flags_ref, dense_ref, left_ref, right_ref, inv_ref, *refs):
    out_ref = refs[-1]
    rank_pad, rows = left_ref.shape[2:]
    row_at = lax.broadcasted_iota(jnp.int32, (rank_pad, rows), 0)
    for place, (first, step, col, packed) in enumerate(order):
        if col is None:
            out_ref[place] = inv_ref[step - first]
            continue
        flag = flags_ref[step, col].astype(jnp.float32)
        mask = jnp.where(row_at < ranks_ref[step, col], 1.0 - flag, 0.0)
        left = left_ref[step - first, col] * mask
        over_rows = (((0,), (0,)), ((), ()))
        low = dot_halves(halves(left, 1), halves(right_ref[packed], 1), over_rows)
        out_ref[place] = dense_ref[step - first, col] * flag + low


def first_kernel(prev, flags_ref, known_ref, dense_ref, right_ref, inv_ref, sent_ref, own_ref):
    nb = own_ref.shape[-1]
    rank_pad = right_ref.shape[2]
    for col in range(prev):
        known = known_ref[col]
        sent_ref[col * nb : (col + 1) * nb] = known
        at = prev * nb + col * rank_pad
        sent_ref[at : at + rank_pad] = dot_halves(halves(right_ref[0, col], 0), halves(known, 1))
        own_ref[col] = dense_ref[0, col] * flags_ref[0, col].astype(jnp.float32)
    own_ref[prev] = inv_ref[0]


def early_kernel(n, prev, step, tiles, picks, solved_at, low, *refs):
    refs = list(refs)
    strips = [refs.pop(0) for _ in range(n)]
    sources = [refs.pop(0) for _ in range(n)]
    solved = [[refs.pop(0) for _ in range(n)] for _ in solved_at]
    ranks_ref, flags_ref, left_ref = [refs.pop(0) for _ in range(3)] if low else (None,) * 3
    base_ref, out_ref, picked_ref, scratch = refs
    nb = out_ref.shape[0]
    own_col = lax.axis_index("pcol")
    turn = own_col ^ lax.axis_index("prow")

    def strip(tile):
        return halves(jnp.concatenate([ref[tile] for ref in strips], axis=1), 0)

    def take(total, tile, blocks):
        for slot, block in enumerate(blocks):
            scratch[pl.ds(pl.multiple_of((turn ^ slot) * nb, nb), nb), :] = block
        return total - dot_halves(strip(tile), halves(scratch[...], 1))

    total = base_ref[0]
    for col in range(prev):
        total = take(total, tiles + col, [ref[col * nb : (col + 1) * nb] for ref in sources])
    for tile, blocks in zip(solved_at, solved):
        total = take(total, tile, [ref[...] for ref in blocks])
    if low:
        rank_pad, rows = left_ref.shape[2:]
        row_at = lax.broadcasted_iota(jnp.int32, (rank_pad, rows), 0)
        lefts, coeffs = [], []
        for col in range(prev):
            flag = flags_ref[step, col].astype(jnp.float32)
            mask = jnp.where(row_at < ranks_ref[step, col], 1.0 - flag, 0.0)
            lefts.append(left_ref[0, col] * mask)
            at = prev * nb + col * rank_pad
            coeffs.append(sum(ref[at : at + rank_pad] for ref in sources))
        left2 = halves(jnp.concatenate(lefts, axis=0), 1)
        coeff2 = halves(jnp.concatenate(coeffs, axis=0), 1)
        total = total - dot_halves(left2, coeff2, (((0,), (0,)), ((), ())))
    out_ref[...] = total
    for index, tile in enumerate(picks):
        for slot, ref in enumerate(strips):
            place = pl.multiple_of((own_col ^ slot) * nb, nb)
            picked_ref[index, :, pl.ds(place, nb)] = halves(ref[tile], 0)


def chain_kernel(n, minus, stacked, *refs):
    strip_ref, *rest, out_ref, scratch = refs[n:]
    nb = out_ref.shape[-2]
    own = lax.axis_index("prow")
    for slot, ref in enumerate(refs[:n]):
        scratch[pl.ds(pl.multiple_of((own ^ slot) * nb, nb), nb), :] = ref[...]
    total = dot_halves(strip_ref[0], halves(scratch[...], 1))
    if minus:
        total = rest[0][...] - total
    if stacked:
        for index, ref in enumerate(rest):
            out_ref[index] = ref[...]
        out_ref[len(rest)] = total
    else:
        out_ref[...] = total


def spec_of(shape, index=None):
    if index is None:
        return pl.BlockSpec(shape, lambda i: (0,) * len(shape))
    return pl.BlockSpec(shape, lambda i: index)


def square_mesh(
    n,
    right_side,
    earlier,
    inverse_diag,
    dense_tiles,
    left_factor,
    right_factor,
    tile_ranks,
    dense_flags,
):
    steps, nb, rhs = right_side.shape
    prev = earlier.shape[0]
    cols = dense_tiles.shape[1]
    rank_pad = left_factor.shape[3]
    left_t = jnp.swapaxes(left_factor, 2, 3)
    right_t = jnp.swapaxes(right_factor, 2, 3)
    params = pltpu.CompilerParams(vmem_limit_bytes=VMEM_LIMIT)
    f32 = jnp.float32

    def shift(value, axis, step):
        return lax.ppermute(value, axis, [(i, i ^ step) for i in range(n)])

    def over_rows(value):
        return [value] + [shift(value, "prow", d) for d in range(1, n)]

    flip = []
    for owner in range(n):
        for row in range(n):
            source = row ^ owner
            source = (source >> 1) | ((source & 1) * (n // 2)) if n > 1 else 0
            flip.append((owner * n + source, row * n + owner))

    any_spec = pl.BlockSpec(memory_space=pl.ANY)
    smem = pl.BlockSpec(memory_space=pltpu.SMEM)
    bf16 = jnp.bfloat16

    def pinned(value):
        return pltpu.with_memory_space_constraint(value, pltpu.HBM)

    def shaped(*shape, dtype=f32):
        return jax.ShapeDtypeStruct(shape, dtype)

    def call(kernel, name, shapes, args, specs, scratch=()):
        many = isinstance(shapes, list)
        out_specs = [spec_of(x.shape) for x in shapes] if many else spec_of(shapes.shape)
        return pl.pallas_call(
            kernel,
            grid=(1,),
            out_shape=shapes,
            in_specs=specs,
            out_specs=out_specs,
            scratch_shapes=list(scratch),
            compiler_params=params,
            name=name,
        )(*args)

    def packed(step, after):
        own = call(
            functools.partial(pack_kernel, (prev + step,)),
            f"pack{step}",
            shaped(prev + step, rank_pad, nb),
            [pinned(right_t), *after],
            [spec_of((1, cols, rank_pad, nb), (step, 0, 0, 0))] + [any_spec] * len(after),
        )
        return lax.ppermute(own, ("prow", "pcol"), flip)

    def merged(step, right_own, after):
        order = tuple((step, step, col, col) for col in range(prev + step)) + ((step, step, None, None),)
        return call(
            functools.partial(merge_kernel, order),
            f"merge{step}",
            shaped(len(order), nb, nb),
            [tile_ranks, dense_flags]
            + [pinned(dense_tiles), pinned(left_t), right_own, pinned(inverse_diag), *after],
            [
                smem,
                smem,
                spec_of((1, cols, nb, nb), (step, 0, 0, 0)),
                spec_of((1, cols, rank_pad, nb), (step, 0, 0, 0)),
                spec_of(right_own.shape),
                spec_of((1, nb, nb), (step, 0, 0)),
            ]
            + [any_spec] * len(after),
        )

    def over_cols(own, near):
        held = {0: own}
        reach = n // 2
        while near and reach >= 1:
            held |= {d ^ reach: shift(v, "pcol", reach) for d, v in held.items()}
            reach //= 2
        return [held[d] if d in held else shift(own, "pcol", d) for d in range(n)]

    sent, own = call(
        functools.partial(first_kernel, prev),
        "first",
        [shaped(prev * (nb + rank_pad), rhs), shaped(prev + 1, nb, nb)],
        [dense_flags, pinned(earlier), pinned(dense_tiles), pinned(right_t), pinned(inverse_diag)],
        [
            smem,
            spec_of(earlier.shape),
            spec_of((1, cols, nb, nb), (0, 0, 0, 0)),
            spec_of((1, cols, rank_pad, nb), (0, 0, 0, 0)),
            spec_of((1, nb, nb), (0, 0, 0)),
        ],
    )
    known = over_rows(sent)
    strips = [over_cols(own, True)]
    right_own = [None] + [packed(step, known[1:] if step > 1 else []) for step in range(1, steps)]

    def early(step, spread):
        low = step == 0
        tiles = 0
        picks = ([prev + step - 1] if step else []) + [prev + step]
        solved_at = [prev + index for index in range(len(spread))]
        args = strips[step] + known + [ref for blocks in spread for ref in blocks]
        specs = [spec_of(value.shape) for value in strips[step]]
        specs += [spec_of((prev * (nb + rank_pad) if low else prev * nb, rhs))] * n
        specs += [spec_of((nb, rhs))] * (n * len(spread))
        if low:
            args += [tile_ranks, dense_flags, pinned(left_t)]
            specs += [smem, smem, spec_of((1, cols, rank_pad, nb), (0, 0, 0, 0))]
        return call(
            functools.partial(early_kernel, n, prev, step, tiles, picks, solved_at, low),
            f"early{step}",
            [shaped(nb, rhs), shaped(len(picks), 2 * nb, n * nb, dtype=bf16)],
            args + [pinned(right_side)],
            specs + [spec_of((1, nb, rhs), (step, 0, 0))],
            [pltpu.VMEM((n * nb, rhs), f32)],
        )

    def chain(name, chain_strips, place, slots, rest, minus, stacked=False):
        return call(
            functools.partial(chain_kernel, n, minus, stacked),
            name,
            shaped(len(rest) + 1, nb, rhs) if stacked else shaped(nb, rhs),
            slots + [chain_strips] + rest,
            [spec_of((nb, rhs))] * n
            + [spec_of((1, 2 * nb, n * nb), (place, 0, 0))]
            + [spec_of((nb, rhs))] * len(rest),
            [pltpu.VMEM((n * nb, rhs), f32)],
        )

    pending, picked = early(0, [])
    solved, spread = [], []
    for step in range(steps):
        whole = over_rows(pending)
        if step == 0:
            strips.append(over_cols(merged(1, right_own[1], []), True))
            strips.append(over_cols(merged(2, right_own[2], whole[1:]), False))
        last = step + 1 == steps
        rest = solved if last else []
        block = chain(f"solve{step}", picked, 1 if step else 0, whole, rest, False, last)
        if last:
            return block
        solved.append(block)
        blocks = over_rows(block)
        if step == 0:
            strips.append(over_cols(merged(3, right_own[3], blocks[1:]), False))
        base, picked = early(step + 1, spread)
        pending = chain(f"update{step + 1}", picked, 0, blocks, [base], True)
        spread.append(blocks)
    return None


def solution(mesh):
    placed = (
        P("groups", "prow", "pcol"),
        P("groups", "prow", "pcol"),
        P("groups", "prow", "pcol"),
        P("groups", None, "prow", "pcol"),
        P("groups", None, "prow", None),
        P("groups", None, "prow", None),
        P("groups", None),
        P("groups", None),
    )
    n = mesh.shape["prow"]
    square = n > 1 and n == mesh.shape["pcol"] and n & (n - 1) == 0 and n <= 8

    def local(*args):
        nb, cols = args[3].shape[2:]
        if square and nb % 128 == 0 and cols % 128 == 0 and args[0].shape[2] % 128 == 0:
            return square_mesh(n, *args)
        return any_mesh(*args)

    return jax.shard_map(
        local, mesh=mesh, in_specs=placed, out_specs=P("groups", "prow", "pcol"), check_vma=False
    )
```

```python
import functools

import jax
import jax.numpy as jnp
from jax import lax
from jax.experimental import pallas as pl
from jax.experimental.pallas import tpu as pltpu
from jax.sharding import PartitionSpec as P

HIGHEST = lax.Precision.HIGHEST
VMEM_LIMIT = 24 * 1024 * 1024


def any_mesh(
    right_side,
    earlier,
    inverse_diag,
    dense_tiles,
    left_factor,
    right_factor,
    tile_ranks,
    dense_flags,
):
    count_steps = right_side.shape[0]
    prev_cols = earlier.shape[0]
    rank_pad = left_factor.shape[3]
    tile_flags = dense_flags.astype(jnp.float32)
    columns = lax.broadcasted_iota(jnp.int32, tile_ranks.shape + (rank_pad,), 2)
    low_mask = (columns < tile_ranks[:, :, None]).astype(jnp.float32) * (1.0 - tile_flags)[
        :, :, None
    ]
    left_eff = left_factor * low_mask[:, :, None, :]
    tile_rows = (
        lax.all_gather(dense_tiles, "pcol", axis=3, tiled=True) * tile_flags[:, :, None, None]
    )
    inverse_rows = lax.all_gather(inverse_diag, "pcol", axis=2, tiled=True)
    early_sum = jnp.einsum(
        "kjrc,jcs->krs",
        tile_rows[:, :prev_cols],
        lax.all_gather(earlier, "prow", axis=1, tiled=True),
        precision=HIGHEST,
    )
    partial_value = jnp.einsum(
        "kjcq,jcs->kjqs", right_factor[:, :prev_cols], earlier, precision=HIGHEST
    )
    early_coeffs = lax.psum(partial_value, "prow")
    early_sum = early_sum + jnp.einsum(
        "kjrq,kjqs->krs", left_eff[:, :prev_cols], early_coeffs, precision=HIGHEST
    )
    pending = right_side - early_sum
    outputs = []
    for block_index in range(count_steps):
        residual_whole = lax.all_gather(pending[block_index], "prow", axis=0, tiled=True)
        solved_own = jnp.dot(inverse_rows[block_index], residual_whole, precision=HIGHEST)
        outputs.append(solved_own)
        if block_index + 1 < count_steps:
            solved_whole = lax.all_gather(solved_own, "prow", axis=0, tiled=True)
            column = prev_cols + block_index
            later = slice(block_index + 1, None)
            dense_part = jnp.einsum(
                "krc,cs->krs", tile_rows[later, column], solved_whole, precision=HIGHEST
            )
            projected = lax.psum(
                jnp.einsum(
                    "kcq,cs->kqs", right_factor[later, column], solved_own, precision=HIGHEST
                ),
                "prow",
            )
            low_part = jnp.einsum(
                "krq,kqs->krs", left_eff[later, column], projected, precision=HIGHEST
            )
            pending = pending.at[later].add(-(dense_part + low_part))
    return jnp.stack(outputs)


def halves(value, axis):
    high = value.astype(jnp.bfloat16)
    low = (value - high.astype(jnp.float32)).astype(jnp.bfloat16)
    return jnp.concatenate([high, low], axis=axis)


def dot_halves(left2, right2, dims=(((1,), (0,)), ((), ()))):
    rows = left2.shape[1 - dims[0][0][0]] // 2
    cols = right2.shape[1 - dims[0][1][0]] // 2
    out = lax.dot_general(left2, right2, dims, preferred_element_type=jnp.float32)
    return (out[:rows, :cols] + (out[:rows, cols:] + out[rows:, :cols])) + out[rows:, cols:]


def pack_kernel(pieces, right_ref, *refs):
    out_ref = refs[-1]
    place = 0
    for index, count in enumerate(pieces):
        out_ref[place : place + count] = right_ref[index, :count]
        place += count


def merge_kernel(order, ranks_ref, flags_ref, dense_ref, left_ref, right_ref, inv_ref, *refs):
    out_ref = refs[-1]
    rank_pad, rows = left_ref.shape[2:]
    row_at = lax.broadcasted_iota(jnp.int32, (rank_pad, rows), 0)
    for place, (first, step, col, packed) in enumerate(order):
        if col is None:
            out_ref[place] = inv_ref[step - first]
            continue
        flag = flags_ref[step, col].astype(jnp.float32)
        mask = jnp.where(row_at < ranks_ref[step, col], 1.0 - flag, 0.0)
        left = left_ref[step - first, col] * mask
        over_rows = (((0,), (0,)), ((), ()))
        low = dot_halves(halves(left, 1), halves(right_ref[packed], 1), over_rows)
        out_ref[place] = dense_ref[step - first, col] * flag + low


def first_kernel(prev, flags_ref, known_ref, dense_ref, right_ref, inv_ref, sent_ref, own_ref):
    nb = own_ref.shape[-1]
    rank_pad = right_ref.shape[2]
    for col in range(prev):
        known = known_ref[col]
        sent_ref[col * nb : (col + 1) * nb] = known
        at = prev * nb + col * rank_pad
        sent_ref[at : at + rank_pad] = dot_halves(halves(right_ref[0, col], 0), halves(known, 1))
        own_ref[col] = dense_ref[0, col] * flags_ref[0, col].astype(jnp.float32)
    own_ref[prev] = inv_ref[0]


def early_kernel(n, prev, step, at, picks, solved_at, low, *refs):
    refs = list(refs)
    arrays = [refs.pop(0) for _ in range(1 + max(index for index, _ in at))]
    sources = [refs.pop(0) for _ in range(n)]
    solved = [[refs.pop(0) for _ in range(n)] for _ in solved_at]
    ranks_ref, flags_ref, left_ref = [refs.pop(0) for _ in range(3)] if low else (None,) * 3
    base_ref, out_ref, picked_ref, scratch = refs
    nb = out_ref.shape[0]
    own_col = lax.axis_index("pcol")
    turn = own_col ^ lax.axis_index("prow")

    def block(slot, tile):
        index, begin = at[slot]
        return arrays[index][begin + tile]

    def strip(tile):
        return halves(jnp.concatenate([block(slot, tile) for slot in range(n)], axis=1), 0)

    def take(total, tile, blocks):
        for slot, value in enumerate(blocks):
            scratch[pl.ds(pl.multiple_of((turn ^ slot) * nb, nb), nb), :] = value
        return total - dot_halves(strip(tile), halves(scratch[...], 1))

    total = base_ref[0]
    for col in range(prev):
        total = take(total, col, [ref[col * nb : (col + 1) * nb] for ref in sources])
    for tile, blocks in zip(solved_at, solved):
        total = take(total, tile, [ref[...] for ref in blocks])
    if low:
        rank_pad, rows = left_ref.shape[2:]
        row_at = lax.broadcasted_iota(jnp.int32, (rank_pad, rows), 0)
        lefts, coeffs = [], []
        for col in range(prev):
            flag = flags_ref[step, col].astype(jnp.float32)
            mask = jnp.where(row_at < ranks_ref[step, col], 1.0 - flag, 0.0)
            lefts.append(left_ref[0, col] * mask)
            place = prev * nb + col * rank_pad
            coeffs.append(sum(ref[place : place + rank_pad] for ref in sources))
        left2 = halves(jnp.concatenate(lefts, axis=0), 1)
        coeff2 = halves(jnp.concatenate(coeffs, axis=0), 1)
        total = total - dot_halves(left2, coeff2, (((0,), (0,)), ((), ())))
    out_ref[...] = total
    for index, tile in enumerate(picks):
        for slot in range(n):
            place = pl.multiple_of((own_col ^ slot) * nb, nb)
            picked_ref[index, :, pl.ds(place, nb)] = halves(block(slot, tile), 0)


def pair_kernel(near_ref, far_ref, out_ref):
    count = near_ref.shape[0]
    out_ref[:count] = near_ref[...]
    out_ref[count:] = far_ref[...]


def chain_kernel(n, minus, stacked, *refs):
    strip_ref, *rest, out_ref, scratch = refs[n:]
    nb = out_ref.shape[-2]
    own = lax.axis_index("prow")
    for slot, ref in enumerate(refs[:n]):
        scratch[pl.ds(pl.multiple_of((own ^ slot) * nb, nb), nb), :] = ref[...]
    total = dot_halves(strip_ref[0], halves(scratch[...], 1))
    if minus:
        total = rest[0][...] - total
    if stacked:
        for index, ref in enumerate(rest):
            out_ref[index] = ref[...]
        out_ref[len(rest)] = total
    else:
        out_ref[...] = total


def spec_of(shape, index=None):
    if index is None:
        return pl.BlockSpec(shape, lambda i: (0,) * len(shape))
    return pl.BlockSpec(shape, lambda i: index)


def square_mesh(
    n,
    right_side,
    earlier,
    inverse_diag,
    dense_tiles,
    left_factor,
    right_factor,
    tile_ranks,
    dense_flags,
):
    steps, nb, rhs = right_side.shape
    prev = earlier.shape[0]
    cols = dense_tiles.shape[1]
    rank_pad = left_factor.shape[3]
    left_t = jnp.swapaxes(left_factor, 2, 3)
    right_t = jnp.swapaxes(right_factor, 2, 3)
    params = pltpu.CompilerParams(vmem_limit_bytes=VMEM_LIMIT)
    f32 = jnp.float32

    def shift(value, axis, step):
        return lax.ppermute(value, axis, [(i, i ^ step) for i in range(n)])

    def over_rows(value):
        return [value] + [shift(value, "prow", d) for d in range(1, n)]

    flip = []
    for owner in range(n):
        for row in range(n):
            source = row ^ owner
            source = (source >> 1) | ((source & 1) * (n // 2)) if n > 1 else 0
            flip.append((owner * n + source, row * n + owner))

    any_spec = pl.BlockSpec(memory_space=pl.ANY)
    smem = pl.BlockSpec(memory_space=pltpu.SMEM)
    bf16 = jnp.bfloat16

    def pinned(value):
        return pltpu.with_memory_space_constraint(value, pltpu.HBM)

    def shaped(*shape, dtype=f32):
        return jax.ShapeDtypeStruct(shape, dtype)

    def call(kernel, name, shapes, args, specs, scratch=(), after=()):
        many = isinstance(shapes, list)
        out_specs = [spec_of(x.shape) for x in shapes] if many else spec_of(shapes.shape)

        def body(*refs):
            kernel(*refs[: len(args)], *refs[len(args) + len(after) :])

        return pl.pallas_call(
            body,
            grid=(1,),
            out_shape=shapes,
            in_specs=specs + [any_spec] * len(after),
            out_specs=out_specs,
            scratch_shapes=list(scratch),
            compiler_params=params,
            name=name,
        )(*args, *after)

    def packed(step, after):
        own = call(
            functools.partial(pack_kernel, (prev + step,)),
            f"pack{step}",
            shaped(prev + step, rank_pad, nb),
            [pinned(right_t)],
            [spec_of((1, cols, rank_pad, nb), (step, 0, 0, 0))],
            after=after,
        )
        return lax.ppermute(own, ("prow", "pcol"), flip)

    def merged(step, right_own, after=()):
        order = tuple((step, step, col, col) for col in range(prev + step)) + ((step, step, None, None),)
        return call(
            functools.partial(merge_kernel, order),
            f"merge{step}",
            shaped(len(order), nb, nb),
            [tile_ranks, dense_flags]
            + [pinned(dense_tiles), pinned(left_t), right_own, pinned(inverse_diag)],
            [
                smem,
                smem,
                spec_of((1, cols, nb, nb), (step, 0, 0, 0)),
                spec_of((1, cols, rank_pad, nb), (step, 0, 0, 0)),
                spec_of(right_own.shape),
                spec_of((1, nb, nb), (step, 0, 0)),
            ],
            after=after,
        )

    def over_cols(own):
        held = {0: own}
        reach = n // 2
        while reach >= 1:
            held |= {d ^ reach: shift(v, "pcol", reach) for d, v in held.items()}
            reach //= 2
        return [held[d] for d in range(n)], [(d, 0) for d in range(n)]

    def over_cols_paired(own, far, after):
        count = own.shape[0]
        both = call(
            pair_kernel,
            f"pair{count}",
            shaped(2 * count, nb, nb),
            [own, far],
            [spec_of(own.shape)] * 2,
            after=after,
        )
        return [both, shift(both, "pcol", 1)], [(d & 1, (d >> 1) * count) for d in range(n)]

    sent, own = call(
        functools.partial(first_kernel, prev),
        "first",
        [shaped(prev * (nb + rank_pad), rhs), shaped(prev + 1, nb, nb)],
        [dense_flags, pinned(earlier), pinned(dense_tiles), pinned(right_t), pinned(inverse_diag)],
        [
            smem,
            spec_of(earlier.shape),
            spec_of((1, cols, nb, nb), (0, 0, 0, 0)),
            spec_of((1, cols, rank_pad, nb), (0, 0, 0, 0)),
            spec_of((1, nb, nb), (0, 0, 0)),
        ],
    )
    known = over_rows(sent)
    strips = {0: over_cols(own)}

    def early(step, spread, after=()):
        low = step == 0
        arrays, at = strips[step]
        picks = ([prev + step - 1] if step else []) + [prev + step]
        solved_at = [prev + index for index in range(len(spread))]
        args = arrays + known + [ref for blocks in spread for ref in blocks]
        specs = [spec_of(value.shape) for value in arrays]
        specs += [spec_of((prev * (nb + rank_pad) if low else prev * nb, rhs))] * n
        specs += [spec_of((nb, rhs))] * (n * len(spread))
        if low:
            args += [tile_ranks, dense_flags, pinned(left_t)]
            specs += [smem, smem, spec_of((1, cols, rank_pad, nb), (0, 0, 0, 0))]
        return call(
            functools.partial(early_kernel, n, prev, step, at, picks, solved_at, low),
            f"early{step}",
            [shaped(nb, rhs), shaped(len(picks), 2 * nb, n * nb, dtype=bf16)],
            args + [pinned(right_side)],
            specs + [spec_of((1, nb, rhs), (step, 0, 0))],
            [pltpu.VMEM((n * nb, rhs), f32)],
            after=after,
        )

    def chain(name, picked, place, slots, rest, minus, stacked=False, after=()):
        return call(
            functools.partial(chain_kernel, n, minus, stacked),
            name,
            shaped(len(rest) + 1, nb, rhs) if stacked else shaped(nb, rhs),
            slots + [picked] + rest,
            [spec_of((nb, rhs))] * n
            + [spec_of((1, 2 * nb, n * nb), (place, 0, 0))]
            + [spec_of((nb, rhs))] * len(rest),
            [pltpu.VMEM((n * nb, rhs), f32)],
            after=after,
        )

    strips[1] = over_cols(merged(1, packed(1, [])))
    pending, picked0 = early(0, [])
    right2 = packed(2, known[1:])
    whole = over_rows(pending)
    solved0 = chain("solve0", picked0, 0, whole, [], False, after=[right2])

    own2 = merged(2, right2, [solved0])
    far2 = shift(own2, "pcol", n // 2)
    right3 = packed(3, [solved0])
    blocks0 = over_rows(solved0)
    base, picked1 = early(1, [])
    pending = chain("update1", picked1, 0, blocks0, [base], True, after=[far2])
    strips[2] = over_cols_paired(own2, far2, [pending])
    whole = over_rows(pending)
    solved1 = chain("solve1", picked1, 1, whole, [], False, after=[right3] + strips[2][0][1:])

    own3 = merged(3, right3, [solved1])
    far3 = shift(own3, "pcol", n // 2)
    blocks1 = over_rows(solved1)
    base, picked2 = early(2, [blocks0])
    pending = chain("update2", picked2, 0, blocks1, [base], True)
    whole = over_rows(pending)
    solved2 = chain("solve2", picked2, 1, whole, [], False, after=[far3])

    strips[3] = over_cols_paired(own3, far3, [solved2])
    blocks2 = over_rows(solved2)
    base, picked3 = early(3, [blocks0, blocks1])
    pending = chain("update3", picked3, 0, blocks2, [base], True)
    whole = over_rows(pending)
    return chain("solve3", picked3, 1, whole, [solved0, solved1, solved2], False, True)


def solution(mesh):
    placed = (
        P("groups", "prow", "pcol"),
        P("groups", "prow", "pcol"),
        P("groups", "prow", "pcol"),
        P("groups", None, "prow", "pcol"),
        P("groups", None, "prow", None),
        P("groups", None, "prow", None),
        P("groups", None),
        P("groups", None),
    )
    n = mesh.shape["prow"]
    square = n == 4 and n == mesh.shape["pcol"]

    def local(*args):
        nb, cols = args[3].shape[2:]
        steps = args[0].shape[0]
        if square and steps == 4 and nb % 128 == 0 and cols % 128 == 0 and args[0].shape[2] % 128 == 0:
            return square_mesh(n, *args)
        return any_mesh(*args)

    return jax.shard_map(
        local, mesh=mesh, in_specs=placed, out_specs=P("groups", "prow", "pcol"), check_vma=False
    )
```

```python
import functools

import jax
import jax.numpy as jnp
from jax import lax
from jax.experimental import pallas as pl
from jax.experimental.pallas import tpu as pltpu
from jax.sharding import PartitionSpec as P

HIGHEST = lax.Precision.HIGHEST
VMEM_LIMIT = 24 * 1024 * 1024


def any_mesh(
    right_side,
    earlier,
    inverse_diag,
    dense_tiles,
    left_factor,
    right_factor,
    tile_ranks,
    dense_flags,
):
    count_steps = right_side.shape[0]
    prev_cols = earlier.shape[0]
    rank_pad = left_factor.shape[3]
    tile_flags = dense_flags.astype(jnp.float32)
    columns = lax.broadcasted_iota(jnp.int32, tile_ranks.shape + (rank_pad,), 2)
    low_mask = (columns < tile_ranks[:, :, None]).astype(jnp.float32) * (1.0 - tile_flags)[
        :, :, None
    ]
    left_eff = left_factor * low_mask[:, :, None, :]
    tile_rows = (
        lax.all_gather(dense_tiles, "pcol", axis=3, tiled=True) * tile_flags[:, :, None, None]
    )
    inverse_rows = lax.all_gather(inverse_diag, "pcol", axis=2, tiled=True)
    early_sum = jnp.einsum(
        "kjrc,jcs->krs",
        tile_rows[:, :prev_cols],
        lax.all_gather(earlier, "prow", axis=1, tiled=True),
        precision=HIGHEST,
    )
    partial_value = jnp.einsum(
        "kjcq,jcs->kjqs", right_factor[:, :prev_cols], earlier, precision=HIGHEST
    )
    early_coeffs = lax.psum(partial_value, "prow")
    early_sum = early_sum + jnp.einsum(
        "kjrq,kjqs->krs", left_eff[:, :prev_cols], early_coeffs, precision=HIGHEST
    )
    pending = right_side - early_sum
    outputs = []
    for block_index in range(count_steps):
        residual_whole = lax.all_gather(pending[block_index], "prow", axis=0, tiled=True)
        solved_own = jnp.dot(inverse_rows[block_index], residual_whole, precision=HIGHEST)
        outputs.append(solved_own)
        if block_index + 1 < count_steps:
            solved_whole = lax.all_gather(solved_own, "prow", axis=0, tiled=True)
            column = prev_cols + block_index
            later = slice(block_index + 1, None)
            dense_part = jnp.einsum(
                "krc,cs->krs", tile_rows[later, column], solved_whole, precision=HIGHEST
            )
            projected = lax.psum(
                jnp.einsum(
                    "kcq,cs->kqs", right_factor[later, column], solved_own, precision=HIGHEST
                ),
                "prow",
            )
            low_part = jnp.einsum(
                "krq,kqs->krs", left_eff[later, column], projected, precision=HIGHEST
            )
            pending = pending.at[later].add(-(dense_part + low_part))
    return jnp.stack(outputs)


def halves(value, axis):
    high = value.astype(jnp.bfloat16)
    low = (value - high.astype(jnp.float32)).astype(jnp.bfloat16)
    return jnp.concatenate([high, low], axis=axis)


def dot_halves(left2, right2, dims=(((1,), (0,)), ((), ()))):
    rows = left2.shape[1 - dims[0][0][0]] // 2
    cols = right2.shape[1 - dims[0][1][0]] // 2
    out = lax.dot_general(left2, right2, dims, preferred_element_type=jnp.float32)
    return (out[:rows, :cols] + (out[:rows, cols:] + out[rows:, :cols])) + out[rows:, cols:]


def fill_ahead(out_ref, count, inv_ref, right_ref):
    nb = inv_ref.shape[1]
    share = right_ref.shape[2] // lax.axis_size("pcol")
    at = pl.multiple_of(lax.axis_index("pcol") * share, share)
    out_ref[:nb] = inv_ref[0]
    for col in range(count):
        place = nb + col * share
        out_ref[place : place + share] = right_ref[0, col, pl.ds(at, share), :]


def first_kernel(prev, ahead, known_ref, right_ref, right1_ref, inv_ref, sent_ref):
    nb, rank_pad = known_ref.shape[1], right_ref.shape[2]
    fill_ahead(sent_ref, prev + 1, inv_ref, right1_ref)
    for col in range(prev):
        known = known_ref[col]
        at = ahead + col * nb
        sent_ref[at : at + nb] = known
        at = ahead + prev * nb + col * rank_pad
        sent_ref[at : at + rank_pad] = dot_halves(halves(right_ref[0, col], 0), halves(known, 1))


def dense_kernel(rows, flags_ref, *refs):
    *dense_refs, out_ref = refs
    place = 0
    for (step, count), ref in zip(rows, dense_refs):
        for col in range(count):
            block = ref[0] if len(ref.shape) == 3 else ref[0, col] * flags_ref[step, col].astype(jnp.float32)
            out_ref[place] = block
            place += 1


def stack_kernel(*refs):
    *parts, out_ref = refs
    place = 0
    for ref in parts:
        out_ref[place : place + ref.shape[0]] = ref[...]
        place += ref.shape[0]


def masked_left(step, col, ranks_ref, flags_ref, left_ref):
    row_at = lax.broadcasted_iota(jnp.int32, left_ref.shape[2:], 0)
    flag = flags_ref[step, col].astype(jnp.float32)
    return left_ref[0, col] * jnp.where(row_at < ranks_ref[step, col], 1.0 - flag, 0.0)


OVER_ROWS = (((0,), (0,)), ((), ()))


def early_kernel(n, prev, begin, ahead, counts, *refs):
    strips, sources = refs[:n], refs[n : 2 * n]
    ranks_ref, flags_ref, left_ref, base_ref, inv_ref, right_ref, out_ref, scratch = refs[2 * n :]
    nb, rank_pad = inv_ref.shape[1], left_ref.shape[2]
    turn = lax.axis_index("pcol") ^ lax.axis_index("prow")
    total = base_ref[0]
    for col in range(prev):
        at = begin + col * nb
        for slot, ref in enumerate(sources):
            scratch[pl.ds(pl.multiple_of((turn ^ slot) * nb, nb), nb), :] = ref[at : at + nb]
        strip = jnp.concatenate([ref[col] for ref in strips], axis=1)
        total = total - dot_halves(halves(strip, 0), halves(scratch[...], 1))
    lefts, coeffs = [], []
    for col in range(prev):
        at = begin + prev * nb + col * rank_pad
        lefts.append(masked_left(0, col, ranks_ref, flags_ref, left_ref))
        coeffs.append(sum(ref[at : at + rank_pad] for ref in sources))
    left2 = halves(jnp.concatenate(lefts, axis=0), 1)
    coeff2 = halves(jnp.concatenate(coeffs, axis=0), 1)
    out_ref[ahead:] = total - dot_halves(left2, coeff2, OVER_ROWS)
    fill_ahead(out_ref, counts, inv_ref, right_ref)


def prepare_kernel(n, prev, step, first, size, known_at, last, *refs):
    dense, ahead = refs[:n], refs[n : n + 2]
    sources = refs[n + 2 : 2 * n + 2]
    solved = refs[2 * n + 2 : 2 * n + 1 + step]
    rest = refs[2 * n + 1 + step :]
    ranks_ref, flags_ref, left_ref, base_ref, out_ref, strip_ref, inv_ref, scratch, right_scr = rest
    nb = base_ref.shape[1]
    tiles, rank_pad = right_scr.shape[:2]
    share = rank_pad // n
    own_col, own_row = lax.axis_index("pcol"), lax.axis_index("prow")
    turn = own_col ^ own_row
    rows = ahead[0].shape[0] // (2 * n)

    for near in range(n):
        col_at = own_col ^ near
        for slot in range(n):
            at = ((near >> 1) * n + slot) * rows
            both = halves(ahead[near & 1][at : at + nb], 0)
            row_at = (own_row ^ slot) * nb
            lanes = pl.ds(pl.multiple_of(col_at * nb, nb), nb)
            inv_ref[pl.ds(pl.multiple_of(row_at, nb), nb), lanes] = both[:nb]
            inv_ref[pl.ds(pl.multiple_of(n * nb + row_at, nb), nb), lanes] = both[nb:]
            lanes = pl.ds(pl.multiple_of((turn ^ slot) * nb, nb), nb)
            ranks = pl.ds(pl.multiple_of(col_at * share, share), share)
            for tile in range(tiles):
                place = at + nb + tile * share
                right_scr[tile, ranks, lanes] = ahead[near & 1][place : place + share]

    def strip_of(tile):
        blocks = [ref[first + tile] for ref in dense]
        left = masked_left(step, tile, ranks_ref, flags_ref, left_ref)
        low = dot_halves(halves(left, 1), halves(right_scr[tile], 1), OVER_ROWS)
        return jnp.concatenate(blocks, axis=1) + low

    total = base_ref[0]
    for tile in range(prev):
        at = known_at + tile * nb
        for slot, ref in enumerate(sources):
            scratch[pl.ds(pl.multiple_of((turn ^ slot) * nb, nb), nb), :] = ref[at : at + nb]
        total = total - dot_halves(halves(strip_of(tile), 0), halves(scratch[...], 1))
    for index, ref in enumerate(solved):
        for d in range(n):
            rows_at = pl.ds(pl.multiple_of((own_col ^ d) * nb, nb), nb)
            scratch[d * nb : (d + 1) * nb] = ref[rows_at, :]
        total = total - dot_halves(halves(strip_of(prev + index), 0), halves(scratch[...], 1))
    out_ref[...] = total
    pair = halves(strip_of(tiles - 1), 0)
    for d in range(n):
        lanes = pl.ds(pl.multiple_of((own_col ^ d) * nb, nb), nb)
        strip_ref[0, :, lanes] = pair[:, d * nb : (d + 1) * nb]
        if last:
            strip_ref[1, :, lanes] = halves(dense[d][size - 1], 0)


def place_slots(n, at, nb, slots, scratch):
    own = lax.axis_index("prow")
    for slot, ref in enumerate(slots):
        scratch[pl.ds(pl.multiple_of((own ^ slot) * nb, nb), nb), :] = ref[at : at + nb]


def step_kernel(n, at, ahead, counts, *refs):
    inverse_ref, strip_ref, base_ref, *more, out_ref, solved_ref, scratch = refs[n:]
    nb = base_ref.shape[0]
    place_slots(n, at, nb, refs[:n], scratch)
    solved = dot_halves(inverse_ref[...], halves(scratch[...], 1))
    solved_ref[...] = solved
    out_ref[ahead:] = base_ref[...] - dot_halves(strip_ref[0], halves(solved, 1))
    if ahead:
        fill_ahead(out_ref, counts, *more)


def last_kernel(n, *refs):
    strip_ref, *solved, out_ref, scratch = refs[n:]
    nb = out_ref.shape[1]
    place_slots(n, 0, nb, refs[:n], scratch)
    own = pl.ds(pl.multiple_of(lax.axis_index("prow") * nb, nb), nb)
    for step, ref in enumerate(solved):
        out_ref[step] = ref[own, :]
    out_ref[len(solved)] = dot_halves(strip_ref[0], halves(scratch[...], 1))


def spec_of(shape, index=None):
    if index is None:
        return pl.BlockSpec(shape, lambda i: (0,) * len(shape))
    return pl.BlockSpec(shape, lambda i: index)


def square_mesh(
    n,
    right_side,
    earlier,
    inverse_diag,
    dense_tiles,
    left_factor,
    right_factor,
    tile_ranks,
    dense_flags,
):
    steps, nb, rhs = right_side.shape
    prev = earlier.shape[0]
    cols = dense_tiles.shape[1]
    rank_pad = left_factor.shape[3]
    left_t = jnp.swapaxes(left_factor, 2, 3)
    right_t = jnp.swapaxes(right_factor, 2, 3)
    params = pltpu.CompilerParams(vmem_limit_bytes=VMEM_LIMIT)
    f32 = jnp.float32

    def shift(value, axis, step):
        return lax.ppermute(value, axis, [(i, i ^ step) for i in range(n)])

    def over_rows(value):
        return [value] + [shift(value, "prow", d) for d in range(1, n)]

    def over_rows_forwarded(value):
        beside, across = shift(value, "prow", 1), shift(value, "prow", 2)
        return [value, beside, across, shift(across, "prow", 1)]

    any_spec = pl.BlockSpec(memory_space=pl.ANY)
    smem = pl.BlockSpec(memory_space=pltpu.SMEM)
    bf16 = jnp.bfloat16

    def pinned(value):
        return pltpu.with_memory_space_constraint(value, pltpu.HBM)

    def shaped(*shape, dtype=f32):
        return jax.ShapeDtypeStruct(shape, dtype)

    def call(kernel, name, shapes, args, specs, scratch=(), after=()):
        many = isinstance(shapes, list)
        out_specs = [spec_of(x.shape) for x in shapes] if many else spec_of(shapes.shape)

        def body(*refs):
            kernel(*refs[: len(args)], *refs[len(args) + len(after) :])

        return pl.pallas_call(
            body,
            grid=(1,),
            out_shape=shapes,
            in_specs=specs + [any_spec] * len(after),
            out_specs=out_specs,
            scratch_shapes=list(scratch),
            compiler_params=params,
            name=name,
        )(*args, *after)

    def blocks_of(value, step):
        return pinned(value), spec_of((1,) + value.shape[1:], (step,) + (0,) * (value.ndim - 1))

    def whole_of(value):
        return value, spec_of(value.shape)

    def run(kernel, name, shapes, pairs, scratch=(), after=()):
        args, specs = zip(*pairs)
        return call(kernel, name, shapes, list(args), list(specs), scratch, after)

    share = rank_pad // n
    ranks_flags = [(tile_ranks, smem), (dense_flags, smem)]
    source_room = pltpu.VMEM((n * nb, rhs), f32)
    aheads = [nb + (prev + step) * share for step in range(1, steps)] + [0]

    def over_cols(own):
        far = shift(own, "pcol", 2)
        return [own, shift(own, "pcol", 1), far, shift(far, "pcol", 1)]

    def shared_ahead(slots, ahead, step, after, after_far):
        head = spec_of((ahead, nb))
        shape = shaped(n * ahead, nb)
        own = run(stack_kernel, f"ahead{step}", shape, [(ref, head) for ref in slots], after=after)
        far = shift(own, "pcol", 2)
        shape = shaped(2 * n * ahead, nb)
        pairs = [whole_of(own), whole_of(far)]
        both = run(stack_kernel, f"aheads{step}", shape, pairs, after=after_far)
        return [both, shift(both, "pcol", 1)]

    sent = run(
        functools.partial(first_kernel, prev, aheads[0]),
        "first",
        shaped(aheads[0] + prev * (nb + rank_pad), rhs),
        [whole_of(pinned(earlier))]
        + [blocks_of(right_t, 0), blocks_of(right_t, 1), blocks_of(inverse_diag, 0)],
    )
    known = over_rows_forwarded(sent)
    own = run(
        functools.partial(dense_kernel, [(0, prev)]),
        "dense0",
        shaped(prev, nb, nb),
        [(dense_flags, smem), blocks_of(dense_tiles, 0)],
        after=[sent],
    )
    strips0 = over_cols(own)
    rows = [(step, prev + step) for step in range(1, steps)] + [(steps - 1, 1)]
    size = sum(count for _, count in rows)
    own = run(
        functools.partial(dense_kernel, rows),
        "dense",
        shaped(size, nb, nb),
        [(dense_flags, smem)]
        + [blocks_of(dense_tiles, step) for step in range(1, steps)]
        + [blocks_of(inverse_diag, steps - 1)],
        after=known[1:3] + strips0[1:],
    )
    dense = over_cols(own)

    pending = run(
        functools.partial(early_kernel, n, prev, aheads[0], aheads[1], prev + 2),
        "early",
        shaped(aheads[1] + nb, rhs),
        [whole_of(value) for value in strips0 + known]
        + ranks_flags
        + [blocks_of(left_t, 0), blocks_of(right_side, 0)]
        + [blocks_of(inverse_diag, 1), blocks_of(right_t, 2)],
        [source_room],
    )
    slots, solved = known, []
    for step in range(steps - 1):
        last = step + 2 == steps
        came = slots
        slots = over_rows_forwarded(pending) if aheads[step + 1] else over_rows(pending)
        later = shared_ahead(came, aheads[step], step, [pending], slots[1:3])
        tiles = prev + step + 1
        first = sum(count for row, count in rows[:-1] if row <= step)
        base, strip, inverse = run(
            functools.partial(
                prepare_kernel, n, prev, step + 1, first, size, aheads[0], last
            ),
            f"prepare{step}",
            [
                shaped(nb, rhs),
                shaped(1 + last, 2 * nb, n * nb, dtype=bf16),
                shaped(2 * n * nb, n * nb, dtype=bf16),
            ],
            [whole_of(value) for value in dense + later + known + solved]
            + ranks_flags
            + [blocks_of(left_t, step + 1), blocks_of(right_side, step + 1)],
            [source_room, pltpu.VMEM((tiles, rank_pad, n * nb), f32)],
        )
        ahead = aheads[step + 2] if step + 2 < len(aheads) else 0
        more = [blocks_of(inverse_diag, step + 2), blocks_of(right_t, step + 3)] if ahead else []
        pending, block = run(
            functools.partial(step_kernel, n, aheads[step + 1], ahead, tiles + 2),
            f"step{step}",
            [shaped(ahead + nb, rhs), shaped(n * nb, rhs)],
            [whole_of(value) for value in slots + [inverse]]
            + [(strip, spec_of((1, 2 * nb, n * nb), (0, 0, 0))), whole_of(base)]
            + more,
            [source_room],
        )
        solved.append(block)
    return run(
        functools.partial(last_kernel, n),
        "last",
        shaped(steps, nb, rhs),
        [whole_of(value) for value in over_rows(pending)]
        + [(strip, spec_of((1, 2 * nb, n * nb), (1, 0, 0)))]
        + [whole_of(value) for value in solved],
        [source_room],
    )


def solution(mesh):
    placed = (
        P("groups", "prow", "pcol"),
        P("groups", "prow", "pcol"),
        P("groups", "prow", "pcol"),
        P("groups", None, "prow", "pcol"),
        P("groups", None, "prow", None),
        P("groups", None, "prow", None),
        P("groups", None),
        P("groups", None),
    )
    n = mesh.shape["prow"]
    square = n == 4 and n == mesh.shape["pcol"]

    def local(*args):
        nb, cols = args[3].shape[2:]
        steps = args[0].shape[0]
        if square and steps == 4 and nb % 128 == 0 and cols % 128 == 0 and args[0].shape[2] % 128 == 0:
            return square_mesh(n, *args)
        return any_mesh(*args)

    return jax.shard_map(
        local, mesh=mesh, in_specs=placed, out_specs=P("groups", "prow", "pcol"), check_vma=False
    )
```

```python
import functools

import jax
import jax.numpy as jnp
from jax import lax
from jax.experimental import pallas as pl
from jax.experimental.pallas import tpu as pltpu
from jax.sharding import PartitionSpec as P

HIGHEST = lax.Precision.HIGHEST
VMEM_LIMIT = 24 * 1024 * 1024


def any_mesh(
    right_side,
    earlier,
    inverse_diag,
    dense_tiles,
    left_factor,
    right_factor,
    tile_ranks,
    dense_flags,
):
    count_steps = right_side.shape[0]
    prev_cols = earlier.shape[0]
    rank_pad = left_factor.shape[3]
    tile_flags = dense_flags.astype(jnp.float32)
    columns = lax.broadcasted_iota(jnp.int32, tile_ranks.shape + (rank_pad,), 2)
    low_mask = (columns < tile_ranks[:, :, None]).astype(jnp.float32) * (1.0 - tile_flags)[
        :, :, None
    ]
    left_eff = left_factor * low_mask[:, :, None, :]
    tile_rows = (
        lax.all_gather(dense_tiles, "pcol", axis=3, tiled=True) * tile_flags[:, :, None, None]
    )
    inverse_rows = lax.all_gather(inverse_diag, "pcol", axis=2, tiled=True)
    early_sum = jnp.einsum(
        "kjrc,jcs->krs",
        tile_rows[:, :prev_cols],
        lax.all_gather(earlier, "prow", axis=1, tiled=True),
        precision=HIGHEST,
    )
    partial_value = jnp.einsum(
        "kjcq,jcs->kjqs", right_factor[:, :prev_cols], earlier, precision=HIGHEST
    )
    early_coeffs = lax.psum(partial_value, "prow")
    early_sum = early_sum + jnp.einsum(
        "kjrq,kjqs->krs", left_eff[:, :prev_cols], early_coeffs, precision=HIGHEST
    )
    pending = right_side - early_sum
    outputs = []
    for block_index in range(count_steps):
        residual_whole = lax.all_gather(pending[block_index], "prow", axis=0, tiled=True)
        solved_own = jnp.dot(inverse_rows[block_index], residual_whole, precision=HIGHEST)
        outputs.append(solved_own)
        if block_index + 1 < count_steps:
            solved_whole = lax.all_gather(solved_own, "prow", axis=0, tiled=True)
            column = prev_cols + block_index
            later = slice(block_index + 1, None)
            dense_part = jnp.einsum(
                "krc,cs->krs", tile_rows[later, column], solved_whole, precision=HIGHEST
            )
            projected = lax.psum(
                jnp.einsum(
                    "kcq,cs->kqs", right_factor[later, column], solved_own, precision=HIGHEST
                ),
                "prow",
            )
            low_part = jnp.einsum(
                "krq,kqs->krs", left_eff[later, column], projected, precision=HIGHEST
            )
            pending = pending.at[later].add(-(dense_part + low_part))
    return jnp.stack(outputs)


def halves(value, axis):
    high = value.astype(jnp.bfloat16)
    low = (value - high.astype(jnp.float32)).astype(jnp.bfloat16)
    return jnp.concatenate([high, low], axis=axis)


def dot_halves(left2, right2, dims=(((1,), (0,)), ((), ()))):
    rows = left2.shape[1 - dims[0][0][0]] // 2
    cols = right2.shape[1 - dims[0][1][0]] // 2
    out = lax.dot_general(left2, right2, dims, preferred_element_type=jnp.float32)
    return (out[:rows, :cols] + (out[:rows, cols:] + out[rows:, :cols])) + out[rows:, cols:]


def fill_ahead(out_ref, begin, count, inv_ref, right_ref):
    nb = inv_ref.shape[1]
    share = right_ref.shape[2] // lax.axis_size("pcol")
    at = pl.multiple_of(lax.axis_index("pcol") * share, share)
    out_ref[begin : begin + nb] = inv_ref[0]
    for col in range(count):
        place = begin + nb + col * share
        out_ref[place : place + share] = right_ref[0, col, pl.ds(at, share), :]


def first_kernel(prev, room, known_ref, *refs):
    right_ref, right1_ref, right2_ref, inv_ref, inv1_ref, sent_ref = refs
    nb, rank_pad = known_ref.shape[1], right_ref.shape[2]
    sent_ref[nb:room] = jnp.zeros((room - nb, sent_ref.shape[1]), jnp.float32)
    fill_ahead(sent_ref, 0, prev + 1, inv_ref, right1_ref)
    fill_ahead(sent_ref, room, prev + 2, inv1_ref, right2_ref)
    for col in range(prev):
        known = known_ref[col]
        at = 2 * room + col * nb
        sent_ref[at : at + nb] = known
        at = 2 * room + prev * nb + col * rank_pad
        sent_ref[at : at + rank_pad] = dot_halves(halves(right_ref[0, col], 0), halves(known, 1))


def dense_kernel(rows, flags_ref, *refs):
    *dense_refs, out_ref = refs
    place = 0
    for (step, count), ref in zip(rows, dense_refs):
        for col in range(count):
            block = ref[0] if len(ref.shape) == 3 else ref[0, col] * flags_ref[step, col].astype(jnp.float32)
            out_ref[place] = block
            place += 1


def stack_kernel(*refs):
    *parts, out_ref = refs
    place = 0
    for ref in parts:
        out_ref[place : place + ref.shape[0]] = ref[...]
        place += ref.shape[0]


def masked_left(step, col, ranks_ref, flags_ref, left_ref):
    row_at = lax.broadcasted_iota(jnp.int32, left_ref.shape[2:], 0)
    flag = flags_ref[step, col].astype(jnp.float32)
    return left_ref[0, col] * jnp.where(row_at < ranks_ref[step, col], 1.0 - flag, 0.0)


OVER_ROWS = (((0,), (0,)), ((), ()))


def early_kernel(n, prev, begin, ahead, counts, *refs):
    strips, sources = refs[:n], refs[n : 2 * n]
    ranks_ref, flags_ref, left_ref, base_ref, inv_ref, right_ref, out_ref, scratch = refs[2 * n :]
    nb, rank_pad = inv_ref.shape[1], left_ref.shape[2]
    turn = lax.axis_index("pcol") ^ lax.axis_index("prow")
    total = base_ref[0]
    for col in range(prev):
        at = begin + col * nb
        for slot, ref in enumerate(sources):
            scratch[pl.ds(pl.multiple_of((turn ^ slot) * nb, nb), nb), :] = ref[at : at + nb]
        strip = jnp.concatenate([ref[col] for ref in strips], axis=1)
        total = total - dot_halves(halves(strip, 0), halves(scratch[...], 1))
    lefts, coeffs = [], []
    for col in range(prev):
        at = begin + prev * nb + col * rank_pad
        lefts.append(masked_left(0, col, ranks_ref, flags_ref, left_ref))
        coeffs.append(sum(ref[at : at + rank_pad] for ref in sources))
    left2 = halves(jnp.concatenate(lefts, axis=0), 1)
    coeff2 = halves(jnp.concatenate(coeffs, axis=0), 1)
    out_ref[ahead:] = total - dot_halves(left2, coeff2, OVER_ROWS)
    fill_ahead(out_ref, 0, counts, inv_ref, right_ref)


def prepare_kernel(n, prev, step, first, size, known_at, last, *refs):
    dense, ahead = refs[:n], refs[n : n + 2]
    sources = refs[n + 2 : 2 * n + 2]
    solved = refs[2 * n + 2 : 2 * n + 1 + step]
    rest = refs[2 * n + 1 + step :]
    ranks_ref, flags_ref, left_ref, base_ref, out_ref, strip_ref, inv_ref, scratch, right_scr = rest
    nb = base_ref.shape[1]
    tiles, rank_pad = right_scr.shape[:2]
    share = rank_pad // n
    own_col, own_row = lax.axis_index("pcol"), lax.axis_index("prow")
    turn = own_col ^ own_row
    rows = ahead[0].shape[0] // (2 * n)

    for near in range(n):
        col_at = own_col ^ near
        for slot in range(n):
            at = ((near >> 1) * n + slot) * rows
            both = halves(ahead[near & 1][at : at + nb], 0)
            row_at = (own_row ^ slot) * nb
            lanes = pl.ds(pl.multiple_of(col_at * nb, nb), nb)
            inv_ref[pl.ds(pl.multiple_of(row_at, nb), nb), lanes] = both[:nb]
            inv_ref[pl.ds(pl.multiple_of(n * nb + row_at, nb), nb), lanes] = both[nb:]
            lanes = pl.ds(pl.multiple_of((turn ^ slot) * nb, nb), nb)
            ranks = pl.ds(pl.multiple_of(col_at * share, share), share)
            for tile in range(tiles):
                place = at + nb + tile * share
                right_scr[tile, ranks, lanes] = ahead[near & 1][place : place + share]

    def strip_of(tile):
        blocks = [ref[first + tile] for ref in dense]
        left = masked_left(step, tile, ranks_ref, flags_ref, left_ref)
        low = dot_halves(halves(left, 1), halves(right_scr[tile], 1), OVER_ROWS)
        return jnp.concatenate(blocks, axis=1) + low

    total = base_ref[0]
    for tile in range(prev):
        at = known_at + tile * nb
        for slot, ref in enumerate(sources):
            scratch[pl.ds(pl.multiple_of((turn ^ slot) * nb, nb), nb), :] = ref[at : at + nb]
        total = total - dot_halves(halves(strip_of(tile), 0), halves(scratch[...], 1))
    for index, ref in enumerate(solved):
        for d in range(n):
            rows_at = pl.ds(pl.multiple_of((own_col ^ d) * nb, nb), nb)
            scratch[d * nb : (d + 1) * nb] = ref[rows_at, :]
        total = total - dot_halves(halves(strip_of(prev + index), 0), halves(scratch[...], 1))
    out_ref[...] = total
    pair = halves(strip_of(tiles - 1), 0)
    for d in range(n):
        lanes = pl.ds(pl.multiple_of((own_col ^ d) * nb, nb), nb)
        strip_ref[0, :, lanes] = pair[:, d * nb : (d + 1) * nb]
        if last:
            strip_ref[1, :, lanes] = halves(dense[d][size - 1], 0)


def place_slots(n, at, nb, slots, scratch):
    own = lax.axis_index("prow")
    for slot, ref in enumerate(slots):
        scratch[pl.ds(pl.multiple_of((own ^ slot) * nb, nb), nb), :] = ref[at : at + nb]


def step_kernel(n, at, *refs):
    inverse_ref, strip_ref, base_ref, out_ref, solved_ref, scratch = refs[n:]
    place_slots(n, at, base_ref.shape[0], refs[:n], scratch)
    solved = dot_halves(inverse_ref[...], halves(scratch[...], 1))
    solved_ref[...] = solved
    out_ref[...] = base_ref[...] - dot_halves(strip_ref[0], halves(solved, 1))


def last_kernel(n, *refs):
    strip_ref, *solved, out_ref, scratch = refs[n:]
    nb = out_ref.shape[1]
    place_slots(n, 0, nb, refs[:n], scratch)
    own = pl.ds(pl.multiple_of(lax.axis_index("prow") * nb, nb), nb)
    for step, ref in enumerate(solved):
        out_ref[step] = ref[own, :]
    out_ref[len(solved)] = dot_halves(strip_ref[0], halves(scratch[...], 1))


def spec_of(shape, index=None):
    if index is None:
        return pl.BlockSpec(shape, lambda i: (0,) * len(shape))
    return pl.BlockSpec(shape, lambda i: index)


def square_mesh(
    n,
    right_side,
    earlier,
    inverse_diag,
    dense_tiles,
    left_factor,
    right_factor,
    tile_ranks,
    dense_flags,
):
    steps, nb, rhs = right_side.shape
    prev = earlier.shape[0]
    cols = dense_tiles.shape[1]
    rank_pad = left_factor.shape[3]
    left_t = jnp.swapaxes(left_factor, 2, 3)
    right_t = jnp.swapaxes(right_factor, 2, 3)
    params = pltpu.CompilerParams(vmem_limit_bytes=VMEM_LIMIT)
    f32 = jnp.float32

    def shift(value, axis, step):
        return lax.ppermute(value, axis, [(i, i ^ step) for i in range(n)])

    def over_rows(value):
        return [value] + [shift(value, "prow", d) for d in range(1, n)]

    def over_rows_forwarded(value):
        beside, across = shift(value, "prow", 1), shift(value, "prow", 2)
        return [value, beside, across, shift(across, "prow", 1)]

    any_spec = pl.BlockSpec(memory_space=pl.ANY)
    smem = pl.BlockSpec(memory_space=pltpu.SMEM)
    bf16 = jnp.bfloat16

    def pinned(value):
        return pltpu.with_memory_space_constraint(value, pltpu.HBM)

    def shaped(*shape, dtype=f32):
        return jax.ShapeDtypeStruct(shape, dtype)

    def call(kernel, name, shapes, args, specs, scratch=(), after=()):
        many = isinstance(shapes, list)
        out_specs = [spec_of(x.shape) for x in shapes] if many else spec_of(shapes.shape)

        def body(*refs):
            kernel(*refs[: len(args)], *refs[len(args) + len(after) :])

        return pl.pallas_call(
            body,
            grid=(1,),
            out_shape=shapes,
            in_specs=specs + [any_spec] * len(after),
            out_specs=out_specs,
            scratch_shapes=list(scratch),
            compiler_params=params,
            name=name,
        )(*args, *after)

    def blocks_of(value, step):
        return pinned(value), spec_of((1,) + value.shape[1:], (step,) + (0,) * (value.ndim - 1))

    def whole_of(value):
        return value, spec_of(value.shape)

    def run(kernel, name, shapes, pairs, scratch=(), after=()):
        args, specs = zip(*pairs)
        return call(kernel, name, shapes, list(args), list(specs), scratch, after)

    share = rank_pad // n
    ranks_flags = [(tile_ranks, smem), (dense_flags, smem)]
    source_room = pltpu.VMEM((n * nb, rhs), f32)
    room1, room2 = nb + (prev + 2) * share, nb + (prev + 3) * share

    def over_cols(own):
        far = shift(own, "pcol", 2)
        return [own, shift(own, "pcol", 1), far, shift(far, "pcol", 1)]

    def ahead_far(slots, height, place, name, after):
        head = pl.BlockSpec((height, nb), lambda i: (place, 0))
        shape = shaped(n * height, nb)
        own = run(stack_kernel, name, shape, [(ref, head) for ref in slots], after=after)
        return [own, shift(own, "pcol", 2)]

    def ahead_near(halfs, name, after):
        shape = shaped(2 * halfs[0].shape[0], nb)
        both = run(stack_kernel, name, shape, [whole_of(value) for value in halfs], after=after)
        return [both, shift(both, "pcol", 1)]

    sent = run(
        functools.partial(first_kernel, prev, room1),
        "first",
        shaped(2 * room1 + prev * (nb + rank_pad), rhs),
        [whole_of(pinned(earlier))]
        + [blocks_of(right_t, step) for step in range(3)]
        + [blocks_of(inverse_diag, step) for step in range(2)],
    )
    known = over_rows_forwarded(sent)
    own = run(
        functools.partial(dense_kernel, [(0, prev)]),
        "dense0",
        shaped(prev, nb, nb),
        [(dense_flags, smem), blocks_of(dense_tiles, 0)],
        after=[sent],
    )
    strips0 = over_cols(own)
    rows = [(step, prev + step) for step in range(1, steps)] + [(steps - 1, 1)]
    size = sum(count for _, count in rows)
    own = run(
        functools.partial(dense_kernel, rows),
        "dense",
        shaped(size, nb, nb),
        [(dense_flags, smem)]
        + [blocks_of(dense_tiles, step) for step in range(1, steps)]
        + [blocks_of(inverse_diag, steps - 1)],
        after=[],
    )
    dense = over_cols(own)

    pending = run(
        functools.partial(early_kernel, n, prev, 2 * room1, room2, prev + 3),
        "early",
        shaped(room2 + nb, rhs),
        [whole_of(value) for value in strips0 + known]
        + ranks_flags
        + [blocks_of(left_t, 0), blocks_of(right_side, 0)]
        + [blocks_of(inverse_diag, 2), blocks_of(right_t, 3)],
        [source_room],
    )

    def prepare(step, later, solved):
        last = step + 1 == steps
        tiles = prev + step
        first = sum(count for row, count in rows[:-1] if row < step)
        return run(
            functools.partial(prepare_kernel, n, prev, step, first, size, 2 * room1, last),
            f"prepare{step}",
            [
                shaped(nb, rhs),
                shaped(1 + last, 2 * nb, n * nb, dtype=bf16),
                shaped(2 * n * nb, n * nb, dtype=bf16),
            ],
            [whole_of(value) for value in dense + later + known + solved]
            + ranks_flags
            + [blocks_of(left_t, step), blocks_of(right_side, step)],
            [source_room, pltpu.VMEM((tiles, rank_pad, n * nb), f32)],
        )

    def solve(step, at, slots, prepared):
        base, strip, inverse = prepared
        return run(
            functools.partial(step_kernel, n, at),
            f"step{step}",
            [shaped(nb, rhs), shaped(n * nb, rhs)],
            [whole_of(value) for value in slots + [inverse]]
            + [(strip, spec_of((1, 2 * nb, n * nb), (0, 0, 0))), whole_of(base)],
            [source_room],
        )

    slots = over_rows_forwarded(pending)
    later1 = ahead_far(known, room1, 0, "ahead1", [pending])
    later1 = ahead_near(later1, "aheads1", slots[1:3])
    later2 = ahead_far(known, room1, 1, "ahead2", slots[1:3])
    pending1, solved0 = solve(0, room2, slots, prepare(1, later1, []))

    later3 = ahead_far(slots, room2, 0, "ahead3", [pending1])
    later2 = ahead_near(later2, "aheads2", [pending1])
    slots = over_rows(pending1)
    pending2, solved1 = solve(1, 0, slots, prepare(2, later2, [solved0]))

    slots = over_rows(pending2)
    later3 = ahead_near(later3, "aheads3", [pending2])
    prepared = prepare(3, later3, [solved0, solved1])
    pending3, solved2 = solve(2, 0, slots, prepared)
    return run(
        functools.partial(last_kernel, n),
        "last",
        shaped(steps, nb, rhs),
        [whole_of(value) for value in over_rows(pending3)]
        + [(prepared[1], spec_of((1, 2 * nb, n * nb), (1, 0, 0)))]
        + [whole_of(value) for value in (solved0, solved1, solved2)],
        [source_room],
    )


def solution(mesh):
    placed = (
        P("groups", "prow", "pcol"),
        P("groups", "prow", "pcol"),
        P("groups", "prow", "pcol"),
        P("groups", None, "prow", "pcol"),
        P("groups", None, "prow", None),
        P("groups", None, "prow", None),
        P("groups", None),
        P("groups", None),
    )
    n = mesh.shape["prow"]
    square = n == 4 and n == mesh.shape["pcol"]

    def local(*args):
        nb, cols = args[3].shape[2:]
        steps = args[0].shape[0]
        if square and steps == 4 and nb % 128 == 0 and cols % 128 == 0 and args[0].shape[2] % 128 == 0:
            return square_mesh(n, *args)
        return any_mesh(*args)

    return jax.shard_map(
        local, mesh=mesh, in_specs=placed, out_specs=P("groups", "prow", "pcol"), check_vma=False
    )
```

```python
import functools

import jax
import jax.numpy as jnp
from jax import lax
from jax.experimental import pallas as pl
from jax.experimental.pallas import tpu as pltpu
from jax.sharding import PartitionSpec as P

HIGHEST = lax.Precision.HIGHEST
VMEM_LIMIT = 24 * 1024 * 1024


def any_mesh(
    right_side,
    earlier,
    inverse_diag,
    dense_tiles,
    left_factor,
    right_factor,
    tile_ranks,
    dense_flags,
):
    count_steps = right_side.shape[0]
    prev_cols = earlier.shape[0]
    rank_pad = left_factor.shape[3]
    tile_flags = dense_flags.astype(jnp.float32)
    columns = lax.broadcasted_iota(jnp.int32, tile_ranks.shape + (rank_pad,), 2)
    low_mask = (columns < tile_ranks[:, :, None]).astype(jnp.float32) * (1.0 - tile_flags)[
        :, :, None
    ]
    left_eff = left_factor * low_mask[:, :, None, :]
    tile_rows = (
        lax.all_gather(dense_tiles, "pcol", axis=3, tiled=True) * tile_flags[:, :, None, None]
    )
    inverse_rows = lax.all_gather(inverse_diag, "pcol", axis=2, tiled=True)
    early_sum = jnp.einsum(
        "kjrc,jcs->krs",
        tile_rows[:, :prev_cols],
        lax.all_gather(earlier, "prow", axis=1, tiled=True),
        precision=HIGHEST,
    )
    partial_value = jnp.einsum(
        "kjcq,jcs->kjqs", right_factor[:, :prev_cols], earlier, precision=HIGHEST
    )
    early_coeffs = lax.psum(partial_value, "prow")
    early_sum = early_sum + jnp.einsum(
        "kjrq,kjqs->krs", left_eff[:, :prev_cols], early_coeffs, precision=HIGHEST
    )
    pending = right_side - early_sum
    outputs = []
    for block_index in range(count_steps):
        residual_whole = lax.all_gather(pending[block_index], "prow", axis=0, tiled=True)
        solved_own = jnp.dot(inverse_rows[block_index], residual_whole, precision=HIGHEST)
        outputs.append(solved_own)
        if block_index + 1 < count_steps:
            solved_whole = lax.all_gather(solved_own, "prow", axis=0, tiled=True)
            column = prev_cols + block_index
            later = slice(block_index + 1, None)
            dense_part = jnp.einsum(
                "krc,cs->krs", tile_rows[later, column], solved_whole, precision=HIGHEST
            )
            projected = lax.psum(
                jnp.einsum(
                    "kcq,cs->kqs", right_factor[later, column], solved_own, precision=HIGHEST
                ),
                "prow",
            )
            low_part = jnp.einsum(
                "krq,kqs->krs", left_eff[later, column], projected, precision=HIGHEST
            )
            pending = pending.at[later].add(-(dense_part + low_part))
    return jnp.stack(outputs)


def halves(value, axis):
    high = value.astype(jnp.bfloat16)
    low = (value - high.astype(jnp.float32)).astype(jnp.bfloat16)
    return jnp.concatenate([high, low], axis=axis)


def dot_halves(left2, right2, dims=(((1,), (0,)), ((), ()))):
    rows = left2.shape[1 - dims[0][0][0]] // 2
    cols = right2.shape[1 - dims[0][1][0]] // 2
    out = lax.dot_general(left2, right2, dims, preferred_element_type=jnp.float32)
    return (out[:rows, :cols] + (out[:rows, cols:] + out[rows:, :cols])) + out[rows:, cols:]


def first_kernel(prev, *refs):
    known_ref, right_ref, inv_ref, ahead_ref, known_out = refs
    steps, nb = right_ref.shape[0], inv_ref.shape[1]
    share = right_ref.shape[2] // lax.axis_size("pcol")
    at = pl.multiple_of(lax.axis_index("pcol") * share, share)
    place = 0
    for step in range(steps):
        if step:
            ahead_ref[place : place + nb] = inv_ref[step - 1]
            place += nb
        for col in range(prev + step):
            ahead_ref[place : place + share] = right_ref[step, col, pl.ds(at, share), :]
            place += share
    known_out[...] = known_ref[...]


def dense_kernel(rows, flags_ref, *refs):
    *dense_refs, out_ref = refs
    place = 0
    for (step, count), ref in zip(rows, dense_refs):
        for col in range(count):
            block = ref[0] if len(ref.shape) == 3 else ref[0, col] * flags_ref[step, col].astype(jnp.float32)
            out_ref[place] = block
            place += 1


def stack_kernel(begin, *refs):
    *parts, out_ref = refs
    count = out_ref.shape[0] // len(parts)
    for index, ref in enumerate(parts):
        out_ref[index * count : (index + 1) * count] = ref[begin : begin + count]


def masked_left(step, col, ranks_ref, flags_ref, left_ref):
    row_at = lax.broadcasted_iota(jnp.int32, left_ref.shape[2:], 0)
    flag = flags_ref[step, col].astype(jnp.float32)
    return left_ref[0, col] * jnp.where(row_at < ranks_ref[step, col], 1.0 - flag, 0.0)


OVER_ROWS = (((0,), (0,)), ((), ()))


def prepare_kernel(n, prev, step, first, last, *refs):
    refs = list(refs)
    dense = [refs.pop(0) for _ in range(n)]
    ahead = [refs.pop(0) for _ in range(2)]
    sources = [refs.pop(0) for _ in range(n)]
    solved = [refs.pop(0) for _ in range(step - 1)]
    ranks_ref, flags_ref, left_ref, base_ref, out_ref, *outs, scratch, right_scr = refs
    strip_ref, inv_ref = outs or (None, None)
    nb = base_ref.shape[1]
    tiles, rank_pad = right_scr.shape[:2]
    share = rank_pad // n
    own_col, own_row = lax.axis_index("pcol"), lax.axis_index("prow")
    turn = own_col ^ own_row
    rows = ahead[0].shape[0] // (2 * n)
    head = nb if step else 0

    for near in range(n):
        col_at = own_col ^ near
        for slot in range(n):
            at = ((near >> 1) * n + slot) * rows
            if step:
                both = halves(ahead[near & 1][at : at + nb], 0)
                row_at = (own_row ^ slot) * nb
                lanes = pl.ds(pl.multiple_of(col_at * nb, nb), nb)
                inv_ref[pl.ds(pl.multiple_of(row_at, nb), nb), lanes] = both[:nb]
                inv_ref[pl.ds(pl.multiple_of(n * nb + row_at, nb), nb), lanes] = both[nb:]
            lanes = pl.ds(pl.multiple_of((turn ^ slot) * nb, nb), nb)
            ranks = pl.ds(pl.multiple_of(col_at * share, share), share)
            for tile in range(tiles):
                place = at + head + tile * share
                right_scr[tile, ranks, lanes] = ahead[near & 1][place : place + share]

    def strip_of(tile):
        blocks = [ref[first + tile] for ref in dense]
        left = masked_left(step, tile, ranks_ref, flags_ref, left_ref)
        low = dot_halves(halves(left, 1), halves(right_scr[tile], 1), OVER_ROWS)
        return jnp.concatenate(blocks, axis=1) + low

    total = base_ref[0]
    for tile in range(prev):
        for slot, ref in enumerate(sources):
            scratch[pl.ds(pl.multiple_of((turn ^ slot) * nb, nb), nb), :] = ref[tile]
        total = total - dot_halves(halves(strip_of(tile), 0), halves(scratch[...], 1))
    for index, ref in enumerate(solved):
        for d in range(n):
            rows_at = pl.ds(pl.multiple_of((own_col ^ d) * nb, nb), nb)
            scratch[d * nb : (d + 1) * nb] = ref[rows_at, :]
        total = total - dot_halves(halves(strip_of(prev + index), 0), halves(scratch[...], 1))
    out_ref[...] = total
    if not step:
        return
    pair = halves(strip_of(tiles - 1), 0)
    for d in range(n):
        lanes = pl.ds(pl.multiple_of((own_col ^ d) * nb, nb), nb)
        strip_ref[0, :, lanes] = pair[:, d * nb : (d + 1) * nb]
        if last:
            strip_ref[1, :, lanes] = halves(dense[d][first + tiles], 0)


def place_slots(n, nb, slots, scratch):
    own = lax.axis_index("prow")
    for slot, ref in enumerate(slots):
        scratch[pl.ds(pl.multiple_of((own ^ slot) * nb, nb), nb), :] = ref[...]


def step_kernel(n, *refs):
    inverse_ref, strip_ref, base_ref, out_ref, solved_ref, scratch = refs[n:]
    place_slots(n, base_ref.shape[0], refs[:n], scratch)
    solved = dot_halves(inverse_ref[...], halves(scratch[...], 1))
    solved_ref[...] = solved
    out_ref[...] = base_ref[...] - dot_halves(strip_ref[0], halves(solved, 1))


def last_kernel(n, *refs):
    strip_ref, *solved, out_ref, scratch = refs[n:]
    nb = out_ref.shape[1]
    place_slots(n, nb, refs[:n], scratch)
    own = pl.ds(pl.multiple_of(lax.axis_index("prow") * nb, nb), nb)
    for step, ref in enumerate(solved):
        out_ref[step] = ref[own, :]
    out_ref[len(solved)] = dot_halves(strip_ref[0], halves(scratch[...], 1))


def spec_of(shape, index=None):
    if index is None:
        return pl.BlockSpec(shape, lambda i: (0,) * len(shape))
    return pl.BlockSpec(shape, lambda i: index)


def square_mesh(
    n,
    right_side,
    earlier,
    inverse_diag,
    dense_tiles,
    left_factor,
    right_factor,
    tile_ranks,
    dense_flags,
):
    steps, nb, rhs = right_side.shape
    prev = earlier.shape[0]
    cols = dense_tiles.shape[1]
    rank_pad = left_factor.shape[3]
    left_t = jnp.swapaxes(left_factor, 2, 3)
    right_t = jnp.swapaxes(right_factor, 2, 3)
    params = pltpu.CompilerParams(vmem_limit_bytes=VMEM_LIMIT)
    f32 = jnp.float32

    def shift(value, axis, step):
        return lax.ppermute(value, axis, [(i, i ^ step) for i in range(n)])

    def over_rows(value):
        return [value] + [shift(value, "prow", d) for d in range(1, n)]

    def over_rows_forwarded(value):
        beside, across = shift(value, "prow", 1), shift(value, "prow", 2)
        return [value, beside, across, shift(across, "prow", 1)]

    any_spec = pl.BlockSpec(memory_space=pl.ANY)
    smem = pl.BlockSpec(memory_space=pltpu.SMEM)
    bf16 = jnp.bfloat16

    def pinned(value):
        return pltpu.with_memory_space_constraint(value, pltpu.HBM)

    def shaped(*shape, dtype=f32):
        return jax.ShapeDtypeStruct(shape, dtype)

    def call(kernel, name, shapes, args, specs, scratch=(), after=()):
        many = isinstance(shapes, list)
        out_specs = [spec_of(x.shape) for x in shapes] if many else spec_of(shapes.shape)

        def body(*refs):
            kernel(*refs[: len(args)], *refs[len(args) + len(after) :])

        return pl.pallas_call(
            body,
            grid=(1,),
            out_shape=shapes,
            in_specs=specs + [any_spec] * len(after),
            out_specs=out_specs,
            scratch_shapes=list(scratch),
            compiler_params=params,
            name=name,
        )(*args, *after)

    def blocks_of(value, step):
        return pinned(value), spec_of((1,) + value.shape[1:], (step,) + (0,) * (value.ndim - 1))

    def whole_of(value):
        return value, spec_of(value.shape)

    def run(kernel, name, shapes, pairs, scratch=(), after=()):
        args, specs = zip(*pairs)
        return call(kernel, name, shapes, list(args), list(specs), scratch, after)

    share = rank_pad // n
    ranks_flags = [(tile_ranks, smem), (dense_flags, smem)]
    source_room = pltpu.VMEM((n * nb, rhs), f32)
    def over_cols(own):
        far = shift(own, "pcol", 2)
        return [own, shift(own, "pcol", 1), far, shift(far, "pcol", 1)]

    heights = [(nb if step else 0) + (prev + step) * share for step in range(steps)]

    def ahead_far(step, after=()):
        own = run(
            functools.partial(stack_kernel, sum(heights[:step])),
            f"ahead{step}",
            shaped(n * heights[step], nb),
            [whole_of(value) for value in ahead],
            after=after,
        )
        return [own, shift(own, "pcol", 2)]

    def ahead_near(step, halfs, after=()):
        both = run(
            functools.partial(stack_kernel, 0),
            f"aheads{step}",
            shaped(2 * n * heights[step], nb),
            [whole_of(value) for value in halfs],
            after=after,
        )
        return [both, shift(both, "pcol", 1)]

    sent, known = run(
        functools.partial(first_kernel, prev),
        "first",
        [shaped(sum(heights), nb), shaped(*earlier.shape)],
        [whole_of(pinned(value)) for value in (earlier, right_t, inverse_diag)],
    )
    ahead = over_rows_forwarded(sent)
    known = over_rows_forwarded(known)
    own = run(
        functools.partial(dense_kernel, [(0, prev)]),
        "dense0",
        shaped(prev, nb, nb),
        [(dense_flags, smem), blocks_of(dense_tiles, 0)],
        after=[sent],
    )
    strips0 = over_cols(own)
    rows = [(step, prev + step) for step in range(1, steps)] + [(steps - 1, 1)]
    size = sum(count for _, count in rows)
    own = run(
        functools.partial(dense_kernel, rows),
        "dense",
        shaped(size, nb, nb),
        [(dense_flags, smem)]
        + [blocks_of(dense_tiles, step) for step in range(1, steps)]
        + [blocks_of(inverse_diag, steps - 1)],
        after=[sent],
    )
    dense = over_cols(own)

    def prepare(step, strips, later, solved=()):
        last = step + 1 == steps
        tiles = prev + step
        outs = [
            shaped(nb, rhs),
            shaped(1 + last, 2 * nb, n * nb, dtype=bf16),
            shaped(2 * n * nb, n * nb, dtype=bf16),
        ]
        first = sum(count for row, count in rows[:-1] if row < step)
        return run(
            functools.partial(prepare_kernel, n, prev, step, first, last),
            f"prepare{step}",
            outs if step else outs[0],
            [whole_of(value) for value in [*strips, *later, *known, *solved]]
            + ranks_flags
            + [blocks_of(left_t, step), blocks_of(right_side, step)],
            [source_room, pltpu.VMEM((tiles, rank_pad, n * nb), f32)],
        )

    def solve(step, slots, prepared):
        base, strip, inverse = prepared
        return run(
            functools.partial(step_kernel, n),
            f"step{step}",
            [shaped(nb, rhs), shaped(n * nb, rhs)],
            [whole_of(value) for value in slots + [inverse]]
            + [(strip, spec_of((1, 2 * nb, n * nb), (0, 0, 0))), whole_of(base)],
            [source_room],
        )

    pending0 = prepare(0, strips0, ahead_near(0, ahead_far(0)))
    later1 = ahead_near(1, ahead_far(1, []), [pending0])
    later2 = ahead_far(2, [pending0])
    pending1, solved0 = solve(0, over_rows(pending0), prepare(1, dense, later1))
    later2 = ahead_near(2, later2, [pending1])
    later3 = ahead_far(3, [pending1])
    pending2, solved1 = solve(1, over_rows(pending1), prepare(2, dense, later2, [solved0]))
    later3 = ahead_near(3, later3, [pending2])
    prepared = prepare(3, dense, later3, [solved0, solved1])
    pending3, solved2 = solve(2, over_rows(pending2), prepared)
    return run(
        functools.partial(last_kernel, n),
        "last",
        shaped(steps, nb, rhs),
        [whole_of(value) for value in over_rows(pending3)]
        + [(prepared[1], spec_of((1, 2 * nb, n * nb), (1, 0, 0)))]
        + [whole_of(value) for value in (solved0, solved1, solved2)],
        [source_room],
    )


def solution(mesh):
    placed = (
        P("groups", "prow", "pcol"),
        P("groups", "prow", "pcol"),
        P("groups", "prow", "pcol"),
        P("groups", None, "prow", "pcol"),
        P("groups", None, "prow", None),
        P("groups", None, "prow", None),
        P("groups", None),
        P("groups", None),
    )
    n = mesh.shape["prow"]
    square = n == 4 and n == mesh.shape["pcol"]

    def local(*args):
        nb, cols = args[3].shape[2:]
        steps = args[0].shape[0]
        if square and steps == 4 and nb % 128 == 0 and cols % 128 == 0 and args[0].shape[2] % 128 == 0:
            return square_mesh(n, *args)
        return any_mesh(*args)

    return jax.shard_map(
        local, mesh=mesh, in_specs=placed, out_specs=P("groups", "prow", "pcol"), check_vma=False
    )
```

```python
import functools

import jax
import jax.numpy as jnp
from jax import lax
from jax.experimental import pallas as pl
from jax.experimental.pallas import tpu as pltpu
from jax.sharding import PartitionSpec as P

HIGHEST = lax.Precision.HIGHEST
VMEM_LIMIT = 24 * 1024 * 1024


def any_mesh(
    right_side,
    earlier,
    inverse_diag,
    dense_tiles,
    left_factor,
    right_factor,
    tile_ranks,
    dense_flags,
):
    count_steps = right_side.shape[0]
    prev_cols = earlier.shape[0]
    rank_pad = left_factor.shape[3]
    tile_flags = dense_flags.astype(jnp.float32)
    columns = lax.broadcasted_iota(jnp.int32, tile_ranks.shape + (rank_pad,), 2)
    low_mask = (columns < tile_ranks[:, :, None]).astype(jnp.float32) * (1.0 - tile_flags)[
        :, :, None
    ]
    left_eff = left_factor * low_mask[:, :, None, :]
    tile_rows = (
        lax.all_gather(dense_tiles, "pcol", axis=3, tiled=True) * tile_flags[:, :, None, None]
    )
    inverse_rows = lax.all_gather(inverse_diag, "pcol", axis=2, tiled=True)
    early_sum = jnp.einsum(
        "kjrc,jcs->krs",
        tile_rows[:, :prev_cols],
        lax.all_gather(earlier, "prow", axis=1, tiled=True),
        precision=HIGHEST,
    )
    partial_value = jnp.einsum(
        "kjcq,jcs->kjqs", right_factor[:, :prev_cols], earlier, precision=HIGHEST
    )
    early_coeffs = lax.psum(partial_value, "prow")
    early_sum = early_sum + jnp.einsum(
        "kjrq,kjqs->krs", left_eff[:, :prev_cols], early_coeffs, precision=HIGHEST
    )
    pending = right_side - early_sum
    outputs = []
    for block_index in range(count_steps):
        residual_whole = lax.all_gather(pending[block_index], "prow", axis=0, tiled=True)
        solved_own = jnp.dot(inverse_rows[block_index], residual_whole, precision=HIGHEST)
        outputs.append(solved_own)
        if block_index + 1 < count_steps:
            solved_whole = lax.all_gather(solved_own, "prow", axis=0, tiled=True)
            column = prev_cols + block_index
            later = slice(block_index + 1, None)
            dense_part = jnp.einsum(
                "krc,cs->krs", tile_rows[later, column], solved_whole, precision=HIGHEST
            )
            projected = lax.psum(
                jnp.einsum(
                    "kcq,cs->kqs", right_factor[later, column], solved_own, precision=HIGHEST
                ),
                "prow",
            )
            low_part = jnp.einsum(
                "krq,kqs->krs", left_eff[later, column], projected, precision=HIGHEST
            )
            pending = pending.at[later].add(-(dense_part + low_part))
    return jnp.stack(outputs)


def halves(value, axis):
    high = value.astype(jnp.bfloat16)
    low = (value - high.astype(jnp.float32)).astype(jnp.bfloat16)
    return jnp.concatenate([high, low], axis=axis)


def dot_halves(left2, right2, dims=(((1,), (0,)), ((), ()))):
    rows = left2.shape[1 - dims[0][0][0]] // 2
    cols = right2.shape[1 - dims[0][1][0]] // 2
    out = lax.dot_general(left2, right2, dims, preferred_element_type=jnp.float32)
    return (out[:rows, :cols] + (out[:rows, cols:] + out[rows:, :cols])) + out[rows:, cols:]


def send_kernel(prev, rows, *refs):
    right_ref, inv_ref, out_ref = refs
    nb = inv_ref.shape[1]
    share = right_ref.shape[2] // lax.axis_size("pcol")
    at = pl.multiple_of(lax.axis_index("pcol") * share, share)
    place = 0
    for step in rows:
        if step:
            out_ref[place : place + nb] = inv_ref[step - 1]
            place += nb
        for col in range(prev + step):
            out_ref[place : place + share] = right_ref[step, col, pl.ds(at, share), :]
            place += share


def dense_kernel(rows, flags_ref, *refs):
    *dense_refs, out_ref = refs
    place = 0
    for (step, count), ref in zip(rows, dense_refs):
        for col in range(count):
            block = ref[0] if len(ref.shape) == 3 else ref[0, col] * flags_ref[step, col].astype(jnp.float32)
            out_ref[place] = block
            place += 1


def stack_kernel(begin, *refs):
    *parts, out_ref = refs
    count = out_ref.shape[0] // len(parts)
    for index, ref in enumerate(parts):
        out_ref[index * count : (index + 1) * count] = ref[begin : begin + count]


def masked_left(step, col, ranks_ref, flags_ref, left_ref):
    row_at = lax.broadcasted_iota(jnp.int32, left_ref.shape[2:], 0)
    flag = flags_ref[step, col].astype(jnp.float32)
    return left_ref[0, col] * jnp.where(row_at < ranks_ref[step, col], 1.0 - flag, 0.0)


OVER_ROWS = (((0,), (0,)), ((), ()))


def prepare_kernel(n, prev, step, first, last, *refs):
    refs = list(refs)
    dense = [refs.pop(0) for _ in range(n)]
    ahead = [refs.pop(0) for _ in range(2)]
    sources = [refs.pop(0) for _ in range(n)]
    solved = [refs.pop(0) for _ in range(step - 1)]
    ranks_ref, flags_ref, left_ref, base_ref, out_ref, *outs, scratch, right_scr = refs
    strip_ref, inv_ref = outs or (None, None)
    nb = base_ref.shape[1]
    tiles, rank_pad = right_scr.shape[:2]
    share = rank_pad // n
    own_col, own_row = lax.axis_index("pcol"), lax.axis_index("prow")
    turn = own_col ^ own_row
    rows = ahead[0].shape[0] // (2 * n)
    head = nb if step else 0

    for near in range(n):
        col_at = own_col ^ near
        for slot in range(n):
            at = ((near >> 1) * n + slot) * rows
            if step:
                both = halves(ahead[near & 1][at : at + nb], 0)
                row_at = (own_row ^ slot) * nb
                lanes = pl.ds(pl.multiple_of(col_at * nb, nb), nb)
                inv_ref[pl.ds(pl.multiple_of(row_at, nb), nb), lanes] = both[:nb]
                inv_ref[pl.ds(pl.multiple_of(n * nb + row_at, nb), nb), lanes] = both[nb:]
            lanes = pl.ds(pl.multiple_of((turn ^ slot) * nb, nb), nb)
            ranks = pl.ds(pl.multiple_of(col_at * share, share), share)
            for tile in range(tiles):
                place = at + head + tile * share
                right_scr[tile, ranks, lanes] = ahead[near & 1][place : place + share]

    def strip_of(tile):
        blocks = [ref[first + tile] for ref in dense]
        left = masked_left(step, tile, ranks_ref, flags_ref, left_ref)
        low = dot_halves(halves(left, 1), halves(right_scr[tile], 1), OVER_ROWS)
        return jnp.concatenate(blocks, axis=1) + low

    total = base_ref[0]
    for tile in range(prev):
        for slot, ref in enumerate(sources):
            scratch[pl.ds(pl.multiple_of((turn ^ slot) * nb, nb), nb), :] = ref[tile]
        total = total - dot_halves(halves(strip_of(tile), 0), halves(scratch[...], 1))
    for index, ref in enumerate(solved):
        for d in range(n):
            rows_at = pl.ds(pl.multiple_of((own_col ^ d) * nb, nb), nb)
            scratch[d * nb : (d + 1) * nb] = ref[rows_at, :]
        total = total - dot_halves(halves(strip_of(prev + index), 0), halves(scratch[...], 1))
    out_ref[...] = total
    if not step:
        return
    pair = halves(strip_of(tiles - 1), 0)
    for d in range(n):
        lanes = pl.ds(pl.multiple_of((own_col ^ d) * nb, nb), nb)
        strip_ref[0, :, lanes] = pair[:, d * nb : (d + 1) * nb]
        if last:
            strip_ref[1, :, lanes] = halves(dense[d][first + tiles], 0)


def place_slots(n, nb, slots, scratch):
    own = lax.axis_index("prow")
    for slot, ref in enumerate(slots):
        scratch[pl.ds(pl.multiple_of((own ^ slot) * nb, nb), nb), :] = ref[...]


def step_kernel(n, *refs):
    inverse_ref, strip_ref, base_ref, out_ref, solved_ref, scratch = refs[n:]
    place_slots(n, base_ref.shape[0], refs[:n], scratch)
    solved = dot_halves(inverse_ref[...], halves(scratch[...], 1))
    solved_ref[...] = solved
    out_ref[...] = base_ref[...] - dot_halves(strip_ref[0], halves(solved, 1))


def last_kernel(n, *refs):
    strip_ref, *solved, out_ref, scratch = refs[n:]
    nb = out_ref.shape[1]
    place_slots(n, nb, refs[:n], scratch)
    own = pl.ds(pl.multiple_of(lax.axis_index("prow") * nb, nb), nb)
    for step, ref in enumerate(solved):
        out_ref[step] = ref[own, :]
    out_ref[len(solved)] = dot_halves(strip_ref[0], halves(scratch[...], 1))


def spec_of(shape, index=None):
    if index is None:
        return pl.BlockSpec(shape, lambda i: (0,) * len(shape))
    return pl.BlockSpec(shape, lambda i: index)


def square_mesh(
    n,
    right_side,
    earlier,
    inverse_diag,
    dense_tiles,
    left_factor,
    right_factor,
    tile_ranks,
    dense_flags,
):
    steps, nb, rhs = right_side.shape
    prev = earlier.shape[0]
    cols = dense_tiles.shape[1]
    rank_pad = left_factor.shape[3]
    left_t = jnp.swapaxes(left_factor, 2, 3)
    right_t = jnp.swapaxes(right_factor, 2, 3)
    params = pltpu.CompilerParams(vmem_limit_bytes=VMEM_LIMIT)
    f32 = jnp.float32

    def shift(value, axis, step):
        return lax.ppermute(value, axis, [(i, i ^ step) for i in range(n)])

    def over_rows(value):
        return [value] + [shift(value, "prow", d) for d in range(1, n)]

    def over_rows_forwarded(value):
        beside, across = shift(value, "prow", 1), shift(value, "prow", 2)
        return [value, beside, across, shift(across, "prow", 1)]

    any_spec = pl.BlockSpec(memory_space=pl.ANY)
    smem = pl.BlockSpec(memory_space=pltpu.SMEM)
    bf16 = jnp.bfloat16

    def pinned(value):
        return pltpu.with_memory_space_constraint(value, pltpu.HBM)

    def shaped(*shape, dtype=f32):
        return jax.ShapeDtypeStruct(shape, dtype)

    def call(kernel, name, shapes, args, specs, scratch=(), after=()):
        many = isinstance(shapes, list)
        out_specs = [spec_of(x.shape) for x in shapes] if many else spec_of(shapes.shape)

        def body(*refs):
            kernel(*refs[: len(args)], *refs[len(args) + len(after) :])

        return pl.pallas_call(
            body,
            grid=(1,),
            out_shape=shapes,
            in_specs=specs + [any_spec] * len(after),
            out_specs=out_specs,
            scratch_shapes=list(scratch),
            compiler_params=params,
            name=name,
        )(*args, *after)

    def blocks_of(value, step):
        return pinned(value), spec_of((1,) + value.shape[1:], (step,) + (0,) * (value.ndim - 1))

    def whole_of(value):
        return value, spec_of(value.shape)

    def run(kernel, name, shapes, pairs, scratch=(), after=()):
        args, specs = zip(*pairs)
        return call(kernel, name, shapes, list(args), list(specs), scratch, after)

    share = rank_pad // n
    ranks_flags = [(tile_ranks, smem), (dense_flags, smem)]
    source_room = pltpu.VMEM((n * nb, rhs), f32)
    def over_cols(own):
        far = shift(own, "pcol", 2)
        return [own, shift(own, "pcol", 1), far, shift(far, "pcol", 1)]

    heights = [(nb if step else 0) + (prev + step) * share for step in range(steps)]

    def sent(rows, after=()):
        return run(
            functools.partial(send_kernel, prev, rows),
            f"send{rows[0]}",
            shaped(sum(heights[step] for step in rows), nb),
            [whole_of(pinned(value)) for value in (right_t, inverse_diag)],
            after=after,
        )

    def ahead_far(step, slots, begin, after=()):
        own = run(
            functools.partial(stack_kernel, begin),
            f"ahead{step}",
            shaped(n * heights[step], nb),
            [whole_of(value) for value in slots],
            after=after,
        )
        return [own, shift(own, "pcol", 2)]

    def ahead_near(step, halfs, after=()):
        both = run(
            functools.partial(stack_kernel, 0),
            f"aheads{step}",
            shaped(2 * n * heights[step], nb),
            [whole_of(value) for value in halfs],
            after=after,
        )
        return [both, shift(both, "pcol", 1)]

    first = sent((0,))
    ahead0 = over_rows(first)
    far0 = ahead_far(0, ahead0, 0)
    ahead = over_rows_forwarded(sent(tuple(range(1, steps)), ahead0[1:]))
    known = over_rows_forwarded(earlier)
    own = run(
        functools.partial(dense_kernel, [(0, prev)]),
        "dense0",
        shaped(prev, nb, nb),
        [(dense_flags, smem), blocks_of(dense_tiles, 0)],
        after=far0[1:],
    )
    strips0 = over_cols(own)
    rows = [(step, prev + step) for step in range(1, steps)] + [(steps - 1, 1)]
    size = sum(count for _, count in rows)
    own = run(
        functools.partial(dense_kernel, rows),
        "dense",
        shaped(size, nb, nb),
        [(dense_flags, smem)]
        + [blocks_of(dense_tiles, step) for step in range(1, steps)]
        + [blocks_of(inverse_diag, steps - 1)],
        after=[first],
    )
    dense = over_cols(own)

    def prepare(step, strips, later, solved=()):
        last = step + 1 == steps
        tiles = prev + step
        outs = [
            shaped(nb, rhs),
            shaped(1 + last, 2 * nb, n * nb, dtype=bf16),
            shaped(2 * n * nb, n * nb, dtype=bf16),
        ]
        begin = sum(count for row, count in rows[:-1] if row < step)
        return run(
            functools.partial(prepare_kernel, n, prev, step, begin, last),
            f"prepare{step}",
            outs if step else outs[0],
            [whole_of(value) for value in [*strips, *later, *known, *solved]]
            + ranks_flags
            + [blocks_of(left_t, step), blocks_of(right_side, step)],
            [source_room, pltpu.VMEM((tiles, rank_pad, n * nb), f32)],
        )

    def solve(step, slots, prepared):
        base, strip, inverse = prepared
        return run(
            functools.partial(step_kernel, n),
            f"step{step}",
            [shaped(nb, rhs), shaped(n * nb, rhs)],
            [whole_of(value) for value in slots + [inverse]]
            + [(strip, spec_of((1, 2 * nb, n * nb), (0, 0, 0))), whole_of(base)],
            [source_room],
        )

    pending0 = prepare(0, strips0, ahead_near(0, far0))
    later1 = ahead_near(1, ahead_far(1, ahead, 0, known[1:]), [pending0])
    later2 = ahead_far(2, ahead, heights[1], [pending0])
    pending1, solved0 = solve(0, over_rows(pending0), prepare(1, dense, later1))
    later2 = ahead_near(2, later2, [pending1])
    later3 = ahead_far(3, ahead, heights[1] + heights[2], [pending1])
    pending2, solved1 = solve(1, over_rows(pending1), prepare(2, dense, later2, [solved0]))
    later3 = ahead_near(3, later3, [pending2])
    prepared = prepare(3, dense, later3, [solved0, solved1])
    pending3, solved2 = solve(2, over_rows(pending2), prepared)
    return run(
        functools.partial(last_kernel, n),
        "last",
        shaped(steps, nb, rhs),
        [whole_of(value) for value in over_rows(pending3)]
        + [(prepared[1], spec_of((1, 2 * nb, n * nb), (1, 0, 0)))]
        + [whole_of(value) for value in (solved0, solved1, solved2)],
        [source_room],
    )


def solution(mesh):
    placed = (
        P("groups", "prow", "pcol"),
        P("groups", "prow", "pcol"),
        P("groups", "prow", "pcol"),
        P("groups", None, "prow", "pcol"),
        P("groups", None, "prow", None),
        P("groups", None, "prow", None),
        P("groups", None),
        P("groups", None),
    )
    n = mesh.shape["prow"]
    square = n == 4 and n == mesh.shape["pcol"]

    def local(*args):
        nb, cols = args[3].shape[2:]
        steps = args[0].shape[0]
        if square and steps == 4 and nb % 128 == 0 and cols % 128 == 0 and args[0].shape[2] % 128 == 0:
            return square_mesh(n, *args)
        return any_mesh(*args)

    return jax.shard_map(
        local, mesh=mesh, in_specs=placed, out_specs=P("groups", "prow", "pcol"), check_vma=False
    )
```

```python
import functools

import jax
import jax.numpy as jnp
from jax import lax
from jax.experimental import pallas as pl
from jax.experimental.pallas import tpu as pltpu
from jax.sharding import PartitionSpec as P

HIGHEST = lax.Precision.HIGHEST
VMEM_LIMIT = 24 * 1024 * 1024


def any_mesh(
    right_side,
    earlier,
    inverse_diag,
    dense_tiles,
    left_factor,
    right_factor,
    tile_ranks,
    dense_flags,
):
    count_steps = right_side.shape[0]
    prev_cols = earlier.shape[0]
    rank_pad = left_factor.shape[3]
    tile_flags = dense_flags.astype(jnp.float32)
    columns = lax.broadcasted_iota(jnp.int32, tile_ranks.shape + (rank_pad,), 2)
    low_mask = (columns < tile_ranks[:, :, None]).astype(jnp.float32) * (1.0 - tile_flags)[
        :, :, None
    ]
    left_eff = left_factor * low_mask[:, :, None, :]
    tile_rows = (
        lax.all_gather(dense_tiles, "pcol", axis=3, tiled=True) * tile_flags[:, :, None, None]
    )
    inverse_rows = lax.all_gather(inverse_diag, "pcol", axis=2, tiled=True)
    early_sum = jnp.einsum(
        "kjrc,jcs->krs",
        tile_rows[:, :prev_cols],
        lax.all_gather(earlier, "prow", axis=1, tiled=True),
        precision=HIGHEST,
    )
    partial_value = jnp.einsum(
        "kjcq,jcs->kjqs", right_factor[:, :prev_cols], earlier, precision=HIGHEST
    )
    early_coeffs = lax.psum(partial_value, "prow")
    early_sum = early_sum + jnp.einsum(
        "kjrq,kjqs->krs", left_eff[:, :prev_cols], early_coeffs, precision=HIGHEST
    )
    pending = right_side - early_sum
    outputs = []
    for block_index in range(count_steps):
        residual_whole = lax.all_gather(pending[block_index], "prow", axis=0, tiled=True)
        solved_own = jnp.dot(inverse_rows[block_index], residual_whole, precision=HIGHEST)
        outputs.append(solved_own)
        if block_index + 1 < count_steps:
            solved_whole = lax.all_gather(solved_own, "prow", axis=0, tiled=True)
            column = prev_cols + block_index
            later = slice(block_index + 1, None)
            dense_part = jnp.einsum(
                "krc,cs->krs", tile_rows[later, column], solved_whole, precision=HIGHEST
            )
            projected = lax.psum(
                jnp.einsum(
                    "kcq,cs->kqs", right_factor[later, column], solved_own, precision=HIGHEST
                ),
                "prow",
            )
            low_part = jnp.einsum(
                "krq,kqs->krs", left_eff[later, column], projected, precision=HIGHEST
            )
            pending = pending.at[later].add(-(dense_part + low_part))
    return jnp.stack(outputs)


def halves(value, axis):
    high = value.astype(jnp.bfloat16)
    low = (value - high.astype(jnp.float32)).astype(jnp.bfloat16)
    return jnp.concatenate([high, low], axis=axis)


def dot_halves(left2, right2, dims=(((1,), (0,)), ((), ()))):
    rows = left2.shape[1 - dims[0][0][0]] // 2
    cols = right2.shape[1 - dims[0][1][0]] // 2
    out = lax.dot_general(left2, right2, dims, preferred_element_type=jnp.float32)
    return (out[:rows, :cols] + (out[:rows, cols:] + out[rows:, :cols])) + out[rows:, cols:]


def first_kernel(prev, *refs):
    right_ref, inv_ref, ahead_ref = refs
    steps, nb = right_ref.shape[0], inv_ref.shape[1]
    share = right_ref.shape[2] // lax.axis_size("pcol")
    at = pl.multiple_of(lax.axis_index("pcol") * share, share)
    place = 0
    for step in range(steps):
        if step:
            ahead_ref[place : place + nb] = inv_ref[step - 1]
            place += nb
        for col in range(prev + step):
            ahead_ref[place : place + share] = right_ref[step, col, pl.ds(at, share), :]
            place += share


def dense_kernel(rows, flags_ref, *refs):
    *dense_refs, out_ref = refs
    place = 0
    for (step, count), ref in zip(rows, dense_refs):
        for col in range(count):
            block = ref[0] if len(ref.shape) == 3 else ref[0, col] * flags_ref[step, col].astype(jnp.float32)
            out_ref[place] = block
            place += 1


def stack_kernel(begin, *refs):
    *parts, out_ref = refs
    count = out_ref.shape[0] // len(parts)
    for index, ref in enumerate(parts):
        out_ref[index * count : (index + 1) * count] = ref[begin : begin + count]


def masked_left(step, col, ranks_ref, flags_ref, left_ref):
    row_at = lax.broadcasted_iota(jnp.int32, left_ref.shape[2:], 0)
    flag = flags_ref[step, col].astype(jnp.float32)
    return left_ref[0, col] * jnp.where(row_at < ranks_ref[step, col], 1.0 - flag, 0.0)


OVER_ROWS = (((0,), (0,)), ((), ()))


def prepare_kernel(n, prev, step, first, last, *refs):
    refs = list(refs)
    dense = [refs.pop(0) for _ in range(n)]
    ahead = [refs.pop(0) for _ in range(2)]
    sources = [refs.pop(0) for _ in range(n)]
    solved = [refs.pop(0) for _ in range(step - 1)]
    ranks_ref, flags_ref, left_ref, base_ref, out_ref, *outs, scratch, right_scr = refs
    strip_ref, inv_ref = outs or (None, None)
    nb = base_ref.shape[1]
    tiles, rank_pad = right_scr.shape[:2]
    share = rank_pad // n
    own_col, own_row = lax.axis_index("pcol"), lax.axis_index("prow")
    turn = own_col ^ own_row
    rows = ahead[0].shape[0] // (2 * n)
    head = nb if step else 0

    for near in range(n):
        col_at = own_col ^ near
        for slot in range(n):
            at = ((near >> 1) * n + slot) * rows
            if step:
                both = halves(ahead[near & 1][at : at + nb], 0)
                row_at = (own_row ^ slot) * nb
                lanes = pl.ds(pl.multiple_of(col_at * nb, nb), nb)
                inv_ref[pl.ds(pl.multiple_of(row_at, nb), nb), lanes] = both[:nb]
                inv_ref[pl.ds(pl.multiple_of(n * nb + row_at, nb), nb), lanes] = both[nb:]
            lanes = pl.ds(pl.multiple_of((turn ^ slot) * nb, nb), nb)
            ranks = pl.ds(pl.multiple_of(col_at * share, share), share)
            for tile in range(tiles):
                place = at + head + tile * share
                right_scr[tile, ranks, lanes] = ahead[near & 1][place : place + share]

    def strip_of(tile):
        blocks = [ref[first + tile] for ref in dense]
        left = masked_left(step, tile, ranks_ref, flags_ref, left_ref)
        low = dot_halves(halves(left, 1), halves(right_scr[tile], 1), OVER_ROWS)
        return jnp.concatenate(blocks, axis=1) + low

    total = base_ref[0]
    for tile in range(prev):
        for slot, ref in enumerate(sources):
            scratch[pl.ds(pl.multiple_of((turn ^ slot) * nb, nb), nb), :] = ref[tile]
        total = total - dot_halves(halves(strip_of(tile), 0), halves(scratch[...], 1))
    for index, ref in enumerate(solved):
        for d in range(n):
            rows_at = pl.ds(pl.multiple_of((own_col ^ d) * nb, nb), nb)
            scratch[d * nb : (d + 1) * nb] = ref[rows_at, :]
        total = total - dot_halves(halves(strip_of(prev + index), 0), halves(scratch[...], 1))
    out_ref[...] = total
    if not step:
        return
    pair = halves(strip_of(tiles - 1), 0)
    for d in range(n):
        lanes = pl.ds(pl.multiple_of((own_col ^ d) * nb, nb), nb)
        strip_ref[0, :, lanes] = pair[:, d * nb : (d + 1) * nb]
        if last:
            strip_ref[1, :, lanes] = halves(dense[d][first + tiles], 0)


def place_slots(n, nb, slots, scratch):
    own = lax.axis_index("prow")
    for slot, ref in enumerate(slots):
        scratch[pl.ds(pl.multiple_of((own ^ slot) * nb, nb), nb), :] = ref[...]


def step_kernel(n, *refs):
    inverse_ref, strip_ref, base_ref, out_ref, solved_ref, scratch = refs[n:]
    place_slots(n, base_ref.shape[0], refs[:n], scratch)
    solved = dot_halves(inverse_ref[...], halves(scratch[...], 1))
    solved_ref[...] = solved
    out_ref[...] = base_ref[...] - dot_halves(strip_ref[0], halves(solved, 1))


def last_kernel(n, *refs):
    strip_ref, *solved, out_ref, scratch = refs[n:]
    nb = out_ref.shape[1]
    place_slots(n, nb, refs[:n], scratch)
    own = pl.ds(pl.multiple_of(lax.axis_index("prow") * nb, nb), nb)
    for step, ref in enumerate(solved):
        out_ref[step] = ref[own, :]
    out_ref[len(solved)] = dot_halves(strip_ref[0], halves(scratch[...], 1))


def spec_of(shape, index=None):
    if index is None:
        return pl.BlockSpec(shape, lambda i: (0,) * len(shape))
    return pl.BlockSpec(shape, lambda i: index)


def square_mesh(
    n,
    right_side,
    earlier,
    inverse_diag,
    dense_tiles,
    left_factor,
    right_factor,
    tile_ranks,
    dense_flags,
):
    steps, nb, rhs = right_side.shape
    prev = earlier.shape[0]
    cols = dense_tiles.shape[1]
    rank_pad = left_factor.shape[3]
    left_t = jnp.swapaxes(left_factor, 2, 3)
    right_t = jnp.swapaxes(right_factor, 2, 3)
    params = pltpu.CompilerParams(vmem_limit_bytes=VMEM_LIMIT)
    f32 = jnp.float32

    def shift(value, axis, step):
        return lax.ppermute(value, axis, [(i, i ^ step) for i in range(n)])

    def over_rows(value):
        return [value] + [shift(value, "prow", d) for d in range(1, n)]

    def over_rows_forwarded(value):
        beside, across = shift(value, "prow", 1), shift(value, "prow", 2)
        return [value, beside, across, shift(across, "prow", 1)]

    any_spec = pl.BlockSpec(memory_space=pl.ANY)
    smem = pl.BlockSpec(memory_space=pltpu.SMEM)
    bf16 = jnp.bfloat16

    def pinned(value):
        return pltpu.with_memory_space_constraint(value, pltpu.HBM)

    def shaped(*shape, dtype=f32):
        return jax.ShapeDtypeStruct(shape, dtype)

    def call(kernel, name, shapes, args, specs, scratch=(), after=()):
        many = isinstance(shapes, list)
        out_specs = [spec_of(x.shape) for x in shapes] if many else spec_of(shapes.shape)

        def body(*refs):
            kernel(*refs[: len(args)], *refs[len(args) + len(after) :])

        return pl.pallas_call(
            body,
            grid=(1,),
            out_shape=shapes,
            in_specs=specs + [any_spec] * len(after),
            out_specs=out_specs,
            scratch_shapes=list(scratch),
            compiler_params=params,
            name=name,
        )(*args, *after)

    def blocks_of(value, step):
        return pinned(value), spec_of((1,) + value.shape[1:], (step,) + (0,) * (value.ndim - 1))

    def whole_of(value):
        return value, spec_of(value.shape)

    def run(kernel, name, shapes, pairs, scratch=(), after=()):
        args, specs = zip(*pairs)
        return call(kernel, name, shapes, list(args), list(specs), scratch, after)

    share = rank_pad // n
    ranks_flags = [(tile_ranks, smem), (dense_flags, smem)]
    source_room = pltpu.VMEM((n * nb, rhs), f32)
    def over_cols(own):
        far = shift(own, "pcol", 2)
        return [own, shift(own, "pcol", 1), far, shift(far, "pcol", 1)]

    heights = [(nb if step else 0) + (prev + step) * share for step in range(steps)]

    def ahead_far(step, after=()):
        own = run(
            functools.partial(stack_kernel, sum(heights[:step])),
            f"ahead{step}",
            shaped(n * heights[step], nb),
            [whole_of(value) for value in ahead],
            after=after,
        )
        return [own, shift(own, "pcol", 2)]

    def ahead_near(step, halfs, after=()):
        both = run(
            functools.partial(stack_kernel, 0),
            f"aheads{step}",
            shaped(2 * n * heights[step], nb),
            [whole_of(value) for value in halfs],
            after=after,
        )
        return [both, shift(both, "pcol", 1)]

    (sent,) = run(
        functools.partial(first_kernel, prev),
        "first",
        [shaped(sum(heights), nb)],
        [whole_of(pinned(value)) for value in (right_t, inverse_diag)],
    )
    ahead = over_rows_forwarded(sent)
    known = over_rows_forwarded(earlier)
    own = run(
        functools.partial(dense_kernel, [(0, prev)]),
        "dense0",
        shaped(prev, nb, nb),
        [(dense_flags, smem), blocks_of(dense_tiles, 0)],
        after=[sent],
    )
    strips0 = over_cols(own)
    rows = [(step, prev + step) for step in range(1, steps)] + [(steps - 1, 1)]
    size = sum(count for _, count in rows)
    own = run(
        functools.partial(dense_kernel, rows),
        "dense",
        shaped(size, nb, nb),
        [(dense_flags, smem)]
        + [blocks_of(dense_tiles, step) for step in range(1, steps)]
        + [blocks_of(inverse_diag, steps - 1)],
        after=[sent],
    )
    dense = over_cols(own)

    def prepare(step, strips, later, solved=()):
        last = step + 1 == steps
        tiles = prev + step
        outs = [
            shaped(nb, rhs),
            shaped(1 + last, 2 * nb, n * nb, dtype=bf16),
            shaped(2 * n * nb, n * nb, dtype=bf16),
        ]
        first = sum(count for row, count in rows[:-1] if row < step)
        return run(
            functools.partial(prepare_kernel, n, prev, step, first, last),
            f"prepare{step}",
            outs if step else outs[0],
            [whole_of(value) for value in [*strips, *later, *known, *solved]]
            + ranks_flags
            + [blocks_of(left_t, step), blocks_of(right_side, step)],
            [source_room, pltpu.VMEM((tiles, rank_pad, n * nb), f32)],
        )

    def solve(step, slots, prepared):
        base, strip, inverse = prepared
        return run(
            functools.partial(step_kernel, n),
            f"step{step}",
            [shaped(nb, rhs), shaped(n * nb, rhs)],
            [whole_of(value) for value in slots + [inverse]]
            + [(strip, spec_of((1, 2 * nb, n * nb), (0, 0, 0))), whole_of(base)],
            [source_room],
        )

    pending0 = prepare(0, strips0, ahead_near(0, ahead_far(0, [])))
    later1 = ahead_near(1, ahead_far(1, known[1:]), [pending0])
    later2 = ahead_far(2, [pending0])
    pending1, solved0 = solve(0, over_rows(pending0), prepare(1, dense, later1))
    later2 = ahead_near(2, later2, [pending1])
    later3 = ahead_far(3, [pending1])
    pending2, solved1 = solve(1, over_rows(pending1), prepare(2, dense, later2, [solved0]))
    later3 = ahead_near(3, later3, [pending2])
    prepared = prepare(3, dense, later3, [solved0, solved1])
    pending3, solved2 = solve(2, over_rows(pending2), prepared)
    return run(
        functools.partial(last_kernel, n),
        "last",
        shaped(steps, nb, rhs),
        [whole_of(value) for value in over_rows(pending3)]
        + [(prepared[1], spec_of((1, 2 * nb, n * nb), (1, 0, 0)))]
        + [whole_of(value) for value in (solved0, solved1, solved2)],
        [source_room],
    )


def solution(mesh):
    placed = (
        P("groups", "prow", "pcol"),
        P("groups", "prow", "pcol"),
        P("groups", "prow", "pcol"),
        P("groups", None, "prow", "pcol"),
        P("groups", None, "prow", None),
        P("groups", None, "prow", None),
        P("groups", None),
        P("groups", None),
    )
    n = mesh.shape["prow"]
    square = n == 4 and n == mesh.shape["pcol"]

    def local(*args):
        nb, cols = args[3].shape[2:]
        steps = args[0].shape[0]
        if square and steps == 4 and nb % 128 == 0 and cols % 128 == 0 and args[0].shape[2] % 128 == 0:
            return square_mesh(n, *args)
        return any_mesh(*args)

    return jax.shard_map(
        local, mesh=mesh, in_specs=placed, out_specs=P("groups", "prow", "pcol"), check_vma=False
    )
```

```python
import functools

import jax
import jax.numpy as jnp
from jax import lax
from jax.experimental import pallas as pl
from jax.experimental.pallas import tpu as pltpu
from jax.sharding import PartitionSpec as P

HIGHEST = lax.Precision.HIGHEST
VMEM_LIMIT = 24 * 1024 * 1024


def any_mesh(
    right_side,
    earlier,
    inverse_diag,
    dense_tiles,
    left_factor,
    right_factor,
    tile_ranks,
    dense_flags,
):
    count_steps = right_side.shape[0]
    prev_cols = earlier.shape[0]
    rank_pad = left_factor.shape[3]
    tile_flags = dense_flags.astype(jnp.float32)
    columns = lax.broadcasted_iota(jnp.int32, tile_ranks.shape + (rank_pad,), 2)
    low_mask = (columns < tile_ranks[:, :, None]).astype(jnp.float32) * (1.0 - tile_flags)[
        :, :, None
    ]
    left_eff = left_factor * low_mask[:, :, None, :]
    tile_rows = (
        lax.all_gather(dense_tiles, "pcol", axis=3, tiled=True) * tile_flags[:, :, None, None]
    )
    inverse_rows = lax.all_gather(inverse_diag, "pcol", axis=2, tiled=True)
    early_sum = jnp.einsum(
        "kjrc,jcs->krs",
        tile_rows[:, :prev_cols],
        lax.all_gather(earlier, "prow", axis=1, tiled=True),
        precision=HIGHEST,
    )
    partial_value = jnp.einsum(
        "kjcq,jcs->kjqs", right_factor[:, :prev_cols], earlier, precision=HIGHEST
    )
    early_coeffs = lax.psum(partial_value, "prow")
    early_sum = early_sum + jnp.einsum(
        "kjrq,kjqs->krs", left_eff[:, :prev_cols], early_coeffs, precision=HIGHEST
    )
    pending = right_side - early_sum
    outputs = []
    for block_index in range(count_steps):
        residual_whole = lax.all_gather(pending[block_index], "prow", axis=0, tiled=True)
        solved_own = jnp.dot(inverse_rows[block_index], residual_whole, precision=HIGHEST)
        outputs.append(solved_own)
        if block_index + 1 < count_steps:
            solved_whole = lax.all_gather(solved_own, "prow", axis=0, tiled=True)
            column = prev_cols + block_index
            later = slice(block_index + 1, None)
            dense_part = jnp.einsum(
                "krc,cs->krs", tile_rows[later, column], solved_whole, precision=HIGHEST
            )
            projected = lax.psum(
                jnp.einsum(
                    "kcq,cs->kqs", right_factor[later, column], solved_own, precision=HIGHEST
                ),
                "prow",
            )
            low_part = jnp.einsum(
                "krq,kqs->krs", left_eff[later, column], projected, precision=HIGHEST
            )
            pending = pending.at[later].add(-(dense_part + low_part))
    return jnp.stack(outputs)


def halves(value, axis):
    high = value.astype(jnp.bfloat16)
    low = (value - high.astype(jnp.float32)).astype(jnp.bfloat16)
    return jnp.concatenate([high, low], axis=axis)


def dot_halves(left2, right2, dims=(((1,), (0,)), ((), ()))):
    rows = left2.shape[1 - dims[0][0][0]] // 2
    cols = right2.shape[1 - dims[0][1][0]] // 2
    out = lax.dot_general(left2, right2, dims, preferred_element_type=jnp.float32)
    return (out[:rows, :cols] + (out[:rows, cols:] + out[rows:, :cols])) + out[rows:, cols:]


def first_kernel(prev, *refs):
    known_ref, right_ref, inv_ref, ahead_ref, known_out = refs
    steps, nb = right_ref.shape[0], inv_ref.shape[1]
    share = right_ref.shape[2] // lax.axis_size("pcol")
    at = pl.multiple_of(lax.axis_index("pcol") * share, share)
    place = 0
    for step in range(steps):
        if step:
            ahead_ref[place : place + nb] = inv_ref[step - 1]
            place += nb
        for col in range(prev + step):
            ahead_ref[place : place + share] = right_ref[step, col, pl.ds(at, share), :]
            place += share
    known_out[...] = known_ref[...]


def dense_kernel(rows, flags_ref, *refs):
    *dense_refs, out_ref = refs
    place = 0
    for (step, count), ref in zip(rows, dense_refs):
        for col in range(count):
            block = ref[0] if len(ref.shape) == 3 else ref[0, col] * flags_ref[step, col].astype(jnp.float32)
            out_ref[place] = block
            place += 1


def stack_kernel(begin, *refs):
    *parts, out_ref = refs
    count = out_ref.shape[0] // len(parts)
    for index, ref in enumerate(parts):
        out_ref[index * count : (index + 1) * count] = ref[begin : begin + count]


def masked_left(step, col, ranks_ref, flags_ref, left_ref):
    row_at = lax.broadcasted_iota(jnp.int32, left_ref.shape[2:], 0)
    flag = flags_ref[step, col].astype(jnp.float32)
    return left_ref[0, col] * jnp.where(row_at < ranks_ref[step, col], 1.0 - flag, 0.0)


OVER_ROWS = (((0,), (0,)), ((), ()))


def prepare_kernel(n, prev, step, first, last, *refs):
    refs = list(refs)
    dense = [refs.pop(0) for _ in range(n)]
    ahead = [refs.pop(0) for _ in range(2)]
    sources = [refs.pop(0) for _ in range(n)]
    solved = [refs.pop(0) for _ in range(step - 1)]
    ranks_ref, flags_ref, left_ref, base_ref, out_ref, *outs, scratch, right_scr = refs
    strip_ref, inv_ref = outs or (None, None)
    nb = base_ref.shape[1]
    tiles, rank_pad = right_scr.shape[:2]
    share = rank_pad // n
    own_col, own_row = lax.axis_index("pcol"), lax.axis_index("prow")
    turn = own_col ^ own_row
    rows = ahead[0].shape[0] // (2 * n)
    head = nb if step else 0

    for near in range(n):
        col_at = own_col ^ near
        for slot in range(n):
            at = ((near >> 1) * n + slot) * rows
            if step:
                both = halves(ahead[near & 1][at : at + nb], 0)
                row_at = (own_row ^ slot) * nb
                lanes = pl.ds(pl.multiple_of(col_at * nb, nb), nb)
                inv_ref[pl.ds(pl.multiple_of(row_at, nb), nb), lanes] = both[:nb]
                inv_ref[pl.ds(pl.multiple_of(n * nb + row_at, nb), nb), lanes] = both[nb:]
            lanes = pl.ds(pl.multiple_of((turn ^ slot) * nb, nb), nb)
            ranks = pl.ds(pl.multiple_of(col_at * share, share), share)
            for tile in range(tiles):
                place = at + head + tile * share
                right_scr[tile, ranks, lanes] = ahead[near & 1][place : place + share]

    def strip_of(tile):
        blocks = [ref[first + tile] for ref in dense]
        left = masked_left(step, tile, ranks_ref, flags_ref, left_ref)
        low = dot_halves(halves(left, 1), halves(right_scr[tile], 1), OVER_ROWS)
        return jnp.concatenate(blocks, axis=1) + low

    total = base_ref[0]
    for tile in range(prev):
        for slot, ref in enumerate(sources):
            scratch[pl.ds(pl.multiple_of((turn ^ slot) * nb, nb), nb), :] = ref[tile]
        total = total - dot_halves(halves(strip_of(tile), 0), halves(scratch[...], 1))
    for index, ref in enumerate(solved):
        for d in range(n):
            rows_at = pl.ds(pl.multiple_of((own_col ^ d) * nb, nb), nb)
            scratch[d * nb : (d + 1) * nb] = ref[rows_at, :]
        total = total - dot_halves(halves(strip_of(prev + index), 0), halves(scratch[...], 1))
    out_ref[...] = total
    if not step:
        return
    pair = halves(strip_of(tiles - 1), 0)
    for d in range(n):
        lanes = pl.ds(pl.multiple_of((own_col ^ d) * nb, nb), nb)
        strip_ref[0, :, lanes] = pair[:, d * nb : (d + 1) * nb]
        if last:
            strip_ref[1, :, lanes] = halves(dense[d][first + tiles], 0)


def place_slots(n, nb, slots, scratch):
    own = lax.axis_index("prow")
    for slot, ref in enumerate(slots):
        scratch[pl.ds(pl.multiple_of((own ^ slot) * nb, nb), nb), :] = ref[...]


def step_kernel(n, *refs):
    inverse_ref, strip_ref, base_ref, out_ref, solved_ref, scratch = refs[n:]
    place_slots(n, base_ref.shape[0], refs[:n], scratch)
    solved = dot_halves(inverse_ref[...], halves(scratch[...], 1))
    solved_ref[...] = solved
    out_ref[...] = base_ref[...] - dot_halves(strip_ref[0], halves(solved, 1))


def last_kernel(n, *refs):
    strip_ref, *solved, out_ref, scratch = refs[n:]
    nb = out_ref.shape[1]
    place_slots(n, nb, refs[:n], scratch)
    own = pl.ds(pl.multiple_of(lax.axis_index("prow") * nb, nb), nb)
    for step, ref in enumerate(solved):
        out_ref[step] = ref[own, :]
    out_ref[len(solved)] = dot_halves(strip_ref[0], halves(scratch[...], 1))


def spec_of(shape, index=None):
    if index is None:
        return pl.BlockSpec(shape, lambda i: (0,) * len(shape))
    return pl.BlockSpec(shape, lambda i: index)


def square_mesh(
    n,
    right_side,
    earlier,
    inverse_diag,
    dense_tiles,
    left_factor,
    right_factor,
    tile_ranks,
    dense_flags,
):
    steps, nb, rhs = right_side.shape
    prev = earlier.shape[0]
    cols = dense_tiles.shape[1]
    rank_pad = left_factor.shape[3]
    left_t = jnp.swapaxes(left_factor, 2, 3)
    right_t = jnp.swapaxes(right_factor, 2, 3)
    params = pltpu.CompilerParams(vmem_limit_bytes=VMEM_LIMIT)
    f32 = jnp.float32

    def shift(value, axis, step):
        return lax.ppermute(value, axis, [(i, i ^ step) for i in range(n)])

    def over_rows(value):
        return [value] + [shift(value, "prow", d) for d in range(1, n)]

    def over_rows_forwarded(value):
        beside, across = shift(value, "prow", 1), shift(value, "prow", 2)
        return [value, beside, across, shift(across, "prow", 1)]

    any_spec = pl.BlockSpec(memory_space=pl.ANY)
    smem = pl.BlockSpec(memory_space=pltpu.SMEM)
    bf16 = jnp.bfloat16

    def pinned(value):
        return pltpu.with_memory_space_constraint(value, pltpu.HBM)

    def shaped(*shape, dtype=f32):
        return jax.ShapeDtypeStruct(shape, dtype)

    def call(kernel, name, shapes, args, specs, scratch=(), after=()):
        many = isinstance(shapes, list)
        out_specs = [spec_of(x.shape) for x in shapes] if many else spec_of(shapes.shape)

        def body(*refs):
            kernel(*refs[: len(args)], *refs[len(args) + len(after) :])

        return pl.pallas_call(
            body,
            grid=(1,),
            out_shape=shapes,
            in_specs=specs + [any_spec] * len(after),
            out_specs=out_specs,
            scratch_shapes=list(scratch),
            compiler_params=params,
            name=name,
        )(*args, *after)

    def blocks_of(value, step):
        return pinned(value), spec_of((1,) + value.shape[1:], (step,) + (0,) * (value.ndim - 1))

    def whole_of(value):
        return value, spec_of(value.shape)

    def run(kernel, name, shapes, pairs, scratch=(), after=()):
        args, specs = zip(*pairs)
        return call(kernel, name, shapes, list(args), list(specs), scratch, after)

    share = rank_pad // n
    ranks_flags = [(tile_ranks, smem), (dense_flags, smem)]
    source_room = pltpu.VMEM((n * nb, rhs), f32)
    def over_cols(own):
        far = shift(own, "pcol", 2)
        return [own, shift(own, "pcol", 1), far, shift(far, "pcol", 1)]

    heights = [(nb if step else 0) + (prev + step) * share for step in range(steps)]

    def ahead_far(step, after=()):
        own = run(
            functools.partial(stack_kernel, sum(heights[:step])),
            f"ahead{step}",
            shaped(n * heights[step], nb),
            [whole_of(value) for value in ahead],
            after=after,
        )
        return [own, shift(own, "pcol", 2)]

    def ahead_near(step, halfs, after=()):
        both = run(
            functools.partial(stack_kernel, 0),
            f"aheads{step}",
            shaped(2 * n * heights[step], nb),
            [whole_of(value) for value in halfs],
            after=after,
        )
        return [both, shift(both, "pcol", 1)]

    sent, known = run(
        functools.partial(first_kernel, prev),
        "first",
        [shaped(sum(heights), nb), shaped(*earlier.shape)],
        [whole_of(pinned(value)) for value in (earlier, right_t, inverse_diag)],
    )
    ahead = over_rows_forwarded(sent)
    known = over_rows_forwarded(known)
    own = run(
        functools.partial(dense_kernel, [(0, prev)]),
        "dense0",
        shaped(prev, nb, nb),
        [(dense_flags, smem), blocks_of(dense_tiles, 0)],
        after=[sent],
    )
    strips0 = over_cols(own)
    rows = [(step, prev + step) for step in range(1, steps)] + [(steps - 1, 1)]
    size = sum(count for _, count in rows)
    own = run(
        functools.partial(dense_kernel, rows),
        "dense",
        shaped(size, nb, nb),
        [(dense_flags, smem)]
        + [blocks_of(dense_tiles, step) for step in range(1, steps)]
        + [blocks_of(inverse_diag, steps - 1)],
        after=[sent],
    )
    dense = over_cols(own)

    def prepare(step, strips, later, solved=()):
        last = step + 1 == steps
        tiles = prev + step
        outs = [
            shaped(nb, rhs),
            shaped(1 + last, 2 * nb, n * nb, dtype=bf16),
            shaped(2 * n * nb, n * nb, dtype=bf16),
        ]
        first = sum(count for row, count in rows[:-1] if row < step)
        return run(
            functools.partial(prepare_kernel, n, prev, step, first, last),
            f"prepare{step}",
            outs if step else outs[0],
            [whole_of(value) for value in [*strips, *later, *known, *solved]]
            + ranks_flags
            + [blocks_of(left_t, step), blocks_of(right_side, step)],
            [source_room, pltpu.VMEM((tiles, rank_pad, n * nb), f32)],
        )

    def solve(step, slots, prepared):
        base, strip, inverse = prepared
        return run(
            functools.partial(step_kernel, n),
            f"step{step}",
            [shaped(nb, rhs), shaped(n * nb, rhs)],
            [whole_of(value) for value in slots + [inverse]]
            + [(strip, spec_of((1, 2 * nb, n * nb), (0, 0, 0))), whole_of(base)],
            [source_room],
        )

    pending0 = prepare(0, strips0, ahead_near(0, ahead_far(0, [])))
    later1 = ahead_near(1, ahead_far(1, known[1:2]), [pending0])
    later2 = ahead_far(2, [pending0])
    pending1, solved0 = solve(0, over_rows(pending0), prepare(1, dense, later1))
    later2 = ahead_near(2, later2, [pending1])
    later3 = ahead_far(3, [pending1])
    pending2, solved1 = solve(1, over_rows(pending1), prepare(2, dense, later2, [solved0]))
    later3 = ahead_near(3, later3, [pending2])
    prepared = prepare(3, dense, later3, [solved0, solved1])
    pending3, solved2 = solve(2, over_rows(pending2), prepared)
    return run(
        functools.partial(last_kernel, n),
        "last",
        shaped(steps, nb, rhs),
        [whole_of(value) for value in over_rows(pending3)]
        + [(prepared[1], spec_of((1, 2 * nb, n * nb), (1, 0, 0)))]
        + [whole_of(value) for value in (solved0, solved1, solved2)],
        [source_room],
    )


def solution(mesh):
    placed = (
        P("groups", "prow", "pcol"),
        P("groups", "prow", "pcol"),
        P("groups", "prow", "pcol"),
        P("groups", None, "prow", "pcol"),
        P("groups", None, "prow", None),
        P("groups", None, "prow", None),
        P("groups", None),
        P("groups", None),
    )
    n = mesh.shape["prow"]
    square = n == 4 and n == mesh.shape["pcol"]

    def local(*args):
        nb, cols = args[3].shape[2:]
        steps = args[0].shape[0]
        if square and steps == 4 and nb % 128 == 0 and cols % 128 == 0 and args[0].shape[2] % 128 == 0:
            return square_mesh(n, *args)
        return any_mesh(*args)

    return jax.shard_map(
        local, mesh=mesh, in_specs=placed, out_specs=P("groups", "prow", "pcol"), check_vma=False
    )
```

```python
import functools

import jax
import jax.numpy as jnp
from jax import lax
from jax.experimental import pallas as pl
from jax.experimental.pallas import tpu as pltpu
from jax.sharding import PartitionSpec as P

HIGHEST = lax.Precision.HIGHEST
VMEM_LIMIT = 24 * 1024 * 1024


def any_mesh(
    right_side,
    earlier,
    inverse_diag,
    dense_tiles,
    left_factor,
    right_factor,
    tile_ranks,
    dense_flags,
):
    count_steps = right_side.shape[0]
    prev_cols = earlier.shape[0]
    rank_pad = left_factor.shape[3]
    tile_flags = dense_flags.astype(jnp.float32)
    columns = lax.broadcasted_iota(jnp.int32, tile_ranks.shape + (rank_pad,), 2)
    low_mask = (columns < tile_ranks[:, :, None]).astype(jnp.float32) * (1.0 - tile_flags)[
        :, :, None
    ]
    left_eff = left_factor * low_mask[:, :, None, :]
    tile_rows = (
        lax.all_gather(dense_tiles, "pcol", axis=3, tiled=True) * tile_flags[:, :, None, None]
    )
    inverse_rows = lax.all_gather(inverse_diag, "pcol", axis=2, tiled=True)
    early_sum = jnp.einsum(
        "kjrc,jcs->krs",
        tile_rows[:, :prev_cols],
        lax.all_gather(earlier, "prow", axis=1, tiled=True),
        precision=HIGHEST,
    )
    partial_value = jnp.einsum(
        "kjcq,jcs->kjqs", right_factor[:, :prev_cols], earlier, precision=HIGHEST
    )
    early_coeffs = lax.psum(partial_value, "prow")
    early_sum = early_sum + jnp.einsum(
        "kjrq,kjqs->krs", left_eff[:, :prev_cols], early_coeffs, precision=HIGHEST
    )
    pending = right_side - early_sum
    outputs = []
    for block_index in range(count_steps):
        residual_whole = lax.all_gather(pending[block_index], "prow", axis=0, tiled=True)
        solved_own = jnp.dot(inverse_rows[block_index], residual_whole, precision=HIGHEST)
        outputs.append(solved_own)
        if block_index + 1 < count_steps:
            solved_whole = lax.all_gather(solved_own, "prow", axis=0, tiled=True)
            column = prev_cols + block_index
            later = slice(block_index + 1, None)
            dense_part = jnp.einsum(
                "krc,cs->krs", tile_rows[later, column], solved_whole, precision=HIGHEST
            )
            projected = lax.psum(
                jnp.einsum(
                    "kcq,cs->kqs", right_factor[later, column], solved_own, precision=HIGHEST
                ),
                "prow",
            )
            low_part = jnp.einsum(
                "krq,kqs->krs", left_eff[later, column], projected, precision=HIGHEST
            )
            pending = pending.at[later].add(-(dense_part + low_part))
    return jnp.stack(outputs)


def halves(value, axis):
    high = value.astype(jnp.bfloat16)
    low = (value - high.astype(jnp.float32)).astype(jnp.bfloat16)
    return jnp.concatenate([high, low], axis=axis)


def dot_halves(left2, right2, dims=(((1,), (0,)), ((), ()))):
    rows = left2.shape[1 - dims[0][0][0]] // 2
    cols = right2.shape[1 - dims[0][1][0]] // 2
    out = lax.dot_general(left2, right2, dims, preferred_element_type=jnp.float32)
    return (out[:rows, :cols] + (out[:rows, cols:] + out[rows:, :cols])) + out[rows:, cols:]


def first_kernel(prev, *refs):
    known_ref, right_ref, inv_ref, ahead_ref, known_out = refs
    steps, nb = right_ref.shape[0], inv_ref.shape[1]
    share = right_ref.shape[2] // lax.axis_size("pcol")
    at = pl.multiple_of(lax.axis_index("pcol") * share, share)
    place = 0
    for step in range(steps):
        if step:
            ahead_ref[place : place + nb] = inv_ref[step - 1]
            place += nb
        for col in range(prev + step):
            ahead_ref[place : place + share] = right_ref[step, col, pl.ds(at, share), :]
            place += share
    known_out[...] = known_ref[...]


def dense_kernel(rows, flags_ref, *refs):
    *dense_refs, out_ref = refs
    place = 0
    for (step, count), ref in zip(rows, dense_refs):
        for col in range(count):
            block = ref[0] if len(ref.shape) == 3 else ref[0, col] * flags_ref[step, col].astype(jnp.float32)
            out_ref[place] = block
            place += 1


def stack_kernel(begin, *refs):
    *parts, out_ref = refs
    count = out_ref.shape[0] // len(parts)
    for index, ref in enumerate(parts):
        out_ref[index * count : (index + 1) * count] = ref[begin : begin + count]


def masked_left(step, col, ranks_ref, flags_ref, left_ref):
    row_at = lax.broadcasted_iota(jnp.int32, left_ref.shape[2:], 0)
    flag = flags_ref[step, col].astype(jnp.float32)
    return left_ref[0, col] * jnp.where(row_at < ranks_ref[step, col], 1.0 - flag, 0.0)


OVER_ROWS = (((0,), (0,)), ((), ()))


def prepare_kernel(n, prev, step, first, last, *refs):
    refs = list(refs)
    dense = [refs.pop(0) for _ in range(n)]
    ahead = [refs.pop(0) for _ in range(2)]
    sources = [refs.pop(0) for _ in range(n)]
    solved = [refs.pop(0) for _ in range(step - 1)]
    ranks_ref, flags_ref, left_ref, base_ref, out_ref, *outs, scratch, right_scr = refs
    strip_ref, inv_ref = outs or (None, None)
    nb = base_ref.shape[1]
    tiles, rank_pad = right_scr.shape[:2]
    share = rank_pad // n
    own_col, own_row = lax.axis_index("pcol"), lax.axis_index("prow")
    turn = own_col ^ own_row
    rows = ahead[0].shape[0] // (2 * n)
    head = nb if step else 0

    for near in range(n):
        col_at = own_col ^ near
        for slot in range(n):
            at = ((near >> 1) * n + slot) * rows
            if step:
                both = halves(ahead[near & 1][at : at + nb], 0)
                row_at = (own_row ^ slot) * nb
                lanes = pl.ds(pl.multiple_of(col_at * nb, nb), nb)
                inv_ref[pl.ds(pl.multiple_of(row_at, nb), nb), lanes] = both[:nb]
                inv_ref[pl.ds(pl.multiple_of(n * nb + row_at, nb), nb), lanes] = both[nb:]
            lanes = pl.ds(pl.multiple_of((turn ^ slot) * nb, nb), nb)
            ranks = pl.ds(pl.multiple_of(col_at * share, share), share)
            for tile in range(tiles):
                place = at + head + tile * share
                right_scr[tile, ranks, lanes] = ahead[near & 1][place : place + share]

    def strip_of(tile):
        blocks = [ref[first + tile] for ref in dense]
        left = masked_left(step, tile, ranks_ref, flags_ref, left_ref)
        low = dot_halves(halves(left, 1), halves(right_scr[tile], 1), OVER_ROWS)
        return jnp.concatenate(blocks, axis=1) + low

    total = base_ref[0]
    for tile in range(prev):
        for slot, ref in enumerate(sources):
            scratch[pl.ds(pl.multiple_of((turn ^ slot) * nb, nb), nb), :] = ref[tile]
        total = total - dot_halves(halves(strip_of(tile), 0), halves(scratch[...], 1))
    for index, ref in enumerate(solved):
        for d in range(n):
            rows_at = pl.ds(pl.multiple_of((own_col ^ d) * nb, nb), nb)
            scratch[d * nb : (d + 1) * nb] = ref[rows_at, :]
        total = total - dot_halves(halves(strip_of(prev + index), 0), halves(scratch[...], 1))
    out_ref[...] = total
    if not step:
        return
    pair = halves(strip_of(tiles - 1), 0)
    for d in range(n):
        lanes = pl.ds(pl.multiple_of((own_col ^ d) * nb, nb), nb)
        strip_ref[0, :, lanes] = pair[:, d * nb : (d + 1) * nb]
        if last:
            strip_ref[1, :, lanes] = halves(dense[d][first + tiles], 0)


def place_slots(n, nb, slots, scratch):
    own = lax.axis_index("prow")
    for slot, ref in enumerate(slots):
        scratch[pl.ds(pl.multiple_of((own ^ slot) * nb, nb), nb), :] = ref[...]


def step_kernel(n, *refs):
    inverse_ref, strip_ref, base_ref, out_ref, solved_ref, scratch = refs[n:]
    place_slots(n, base_ref.shape[0], refs[:n], scratch)
    solved = dot_halves(inverse_ref[...], halves(scratch[...], 1))
    solved_ref[...] = solved
    out_ref[...] = base_ref[...] - dot_halves(strip_ref[0], halves(solved, 1))


def last_kernel(n, *refs):
    strip_ref, *solved, out_ref, scratch = refs[n:]
    nb = out_ref.shape[1]
    place_slots(n, nb, refs[:n], scratch)
    own = pl.ds(pl.multiple_of(lax.axis_index("prow") * nb, nb), nb)
    for step, ref in enumerate(solved):
        out_ref[step] = ref[own, :]
    out_ref[len(solved)] = dot_halves(strip_ref[0], halves(scratch[...], 1))


def spec_of(shape, index=None):
    if index is None:
        return pl.BlockSpec(shape, lambda i: (0,) * len(shape))
    return pl.BlockSpec(shape, lambda i: index)


def square_mesh(
    n,
    right_side,
    earlier,
    inverse_diag,
    dense_tiles,
    left_factor,
    right_factor,
    tile_ranks,
    dense_flags,
):
    steps, nb, rhs = right_side.shape
    prev = earlier.shape[0]
    cols = dense_tiles.shape[1]
    rank_pad = left_factor.shape[3]
    left_t = jnp.swapaxes(left_factor, 2, 3)
    right_t = jnp.swapaxes(right_factor, 2, 3)
    params = pltpu.CompilerParams(vmem_limit_bytes=VMEM_LIMIT)
    f32 = jnp.float32

    def shift(value, axis, step):
        return lax.ppermute(value, axis, [(i, i ^ step) for i in range(n)])

    def over_rows(value):
        return [value] + [shift(value, "prow", d) for d in range(1, n)]

    def over_rows_forwarded(value):
        beside, across = shift(value, "prow", 1), shift(value, "prow", 2)
        return [value, beside, across, shift(across, "prow", 1)]

    any_spec = pl.BlockSpec(memory_space=pl.ANY)
    smem = pl.BlockSpec(memory_space=pltpu.SMEM)
    bf16 = jnp.bfloat16

    def pinned(value):
        return pltpu.with_memory_space_constraint(value, pltpu.HBM)

    def shaped(*shape, dtype=f32):
        return jax.ShapeDtypeStruct(shape, dtype)

    def call(kernel, name, shapes, args, specs, scratch=(), after=()):
        many = isinstance(shapes, list)
        out_specs = [spec_of(x.shape) for x in shapes] if many else spec_of(shapes.shape)

        def body(*refs):
            kernel(*refs[: len(args)], *refs[len(args) + len(after) :])

        return pl.pallas_call(
            body,
            grid=(1,),
            out_shape=shapes,
            in_specs=specs + [any_spec] * len(after),
            out_specs=out_specs,
            scratch_shapes=list(scratch),
            compiler_params=params,
            name=name,
        )(*args, *after)

    def blocks_of(value, step):
        return pinned(value), spec_of((1,) + value.shape[1:], (step,) + (0,) * (value.ndim - 1))

    def whole_of(value):
        return value, spec_of(value.shape)

    def run(kernel, name, shapes, pairs, scratch=(), after=()):
        args, specs = zip(*pairs)
        return call(kernel, name, shapes, list(args), list(specs), scratch, after)

    share = rank_pad // n
    ranks_flags = [(tile_ranks, smem), (dense_flags, smem)]
    source_room = pltpu.VMEM((n * nb, rhs), f32)
    def over_cols(own):
        far = shift(own, "pcol", 2)
        return [own, shift(own, "pcol", 1), far, shift(far, "pcol", 1)]

    heights = [(nb if step else 0) + (prev + step) * share for step in range(steps)]

    def ahead_far(step, after=()):
        own = run(
            functools.partial(stack_kernel, sum(heights[:step])),
            f"ahead{step}",
            shaped(n * heights[step], nb),
            [whole_of(value) for value in ahead],
            after=after,
        )
        return [own, shift(own, "pcol", 2)]

    def ahead_near(step, halfs, after=()):
        both = run(
            functools.partial(stack_kernel, 0),
            f"aheads{step}",
            shaped(2 * n * heights[step], nb),
            [whole_of(value) for value in halfs],
            after=after,
        )
        return [both, shift(both, "pcol", 1)]

    sent, known = run(
        functools.partial(first_kernel, prev),
        "first",
        [shaped(sum(heights), nb), shaped(*earlier.shape)],
        [whole_of(pinned(value)) for value in (earlier, right_t, inverse_diag)],
    )
    ahead = over_rows_forwarded(sent)
    known = over_rows_forwarded(known)
    own = run(
        functools.partial(dense_kernel, [(0, prev)]),
        "dense0",
        shaped(prev, nb, nb),
        [(dense_flags, smem), blocks_of(dense_tiles, 0)],
        after=[sent],
    )
    strips0 = over_cols(own)
    rows = [(step, prev + step) for step in range(1, steps)] + [(steps - 1, 1)]
    size = sum(count for _, count in rows)
    own = run(
        functools.partial(dense_kernel, rows),
        "dense",
        shaped(size, nb, nb),
        [(dense_flags, smem)]
        + [blocks_of(dense_tiles, step) for step in range(1, steps)]
        + [blocks_of(inverse_diag, steps - 1)],
        after=[sent],
    )
    dense = over_cols(own)

    def prepare(step, strips, later, solved=()):
        last = step + 1 == steps
        tiles = prev + step
        outs = [
            shaped(nb, rhs),
            shaped(1 + last, 2 * nb, n * nb, dtype=bf16),
            shaped(2 * n * nb, n * nb, dtype=bf16),
        ]
        first = sum(count for row, count in rows[:-1] if row < step)
        return run(
            functools.partial(prepare_kernel, n, prev, step, first, last),
            f"prepare{step}",
            outs if step else outs[0],
            [whole_of(value) for value in [*strips, *later, *known, *solved]]
            + ranks_flags
            + [blocks_of(left_t, step), blocks_of(right_side, step)],
            [source_room, pltpu.VMEM((tiles, rank_pad, n * nb), f32)],
        )

    def solve(step, slots, prepared):
        base, strip, inverse = prepared
        return run(
            functools.partial(step_kernel, n),
            f"step{step}",
            [shaped(nb, rhs), shaped(n * nb, rhs)],
            [whole_of(value) for value in slots + [inverse]]
            + [(strip, spec_of((1, 2 * nb, n * nb), (0, 0, 0))), whole_of(base)],
            [source_room],
        )

    pending0 = prepare(0, strips0, ahead_near(0, ahead_far(0, known[1:3])))
    later1 = ahead_near(1, ahead_far(1, known[1:3]), [pending0])
    later2 = ahead_far(2, [pending0])
    pending1, solved0 = solve(0, over_rows(pending0), prepare(1, dense, later1))
    later2 = ahead_near(2, later2, [pending1])
    later3 = ahead_far(3, [pending1])
    pending2, solved1 = solve(1, over_rows(pending1), prepare(2, dense, later2, [solved0]))
    later3 = ahead_near(3, later3, [pending2])
    prepared = prepare(3, dense, later3, [solved0, solved1])
    pending3, solved2 = solve(2, over_rows(pending2), prepared)
    return run(
        functools.partial(last_kernel, n),
        "last",
        shaped(steps, nb, rhs),
        [whole_of(value) for value in over_rows(pending3)]
        + [(prepared[1], spec_of((1, 2 * nb, n * nb), (1, 0, 0)))]
        + [whole_of(value) for value in (solved0, solved1, solved2)],
        [source_room],
    )


def solution(mesh):
    placed = (
        P("groups", "prow", "pcol"),
        P("groups", "prow", "pcol"),
        P("groups", "prow", "pcol"),
        P("groups", None, "prow", "pcol"),
        P("groups", None, "prow", None),
        P("groups", None, "prow", None),
        P("groups", None),
        P("groups", None),
    )
    n = mesh.shape["prow"]
    square = n == 4 and n == mesh.shape["pcol"]

    def local(*args):
        nb, cols = args[3].shape[2:]
        steps = args[0].shape[0]
        if square and steps == 4 and nb % 128 == 0 and cols % 128 == 0 and args[0].shape[2] % 128 == 0:
            return square_mesh(n, *args)
        return any_mesh(*args)

    return jax.shard_map(
        local, mesh=mesh, in_specs=placed, out_specs=P("groups", "prow", "pcol"), check_vma=False
    )
```

```python
import functools

import jax
import jax.numpy as jnp
from jax import lax
from jax.experimental import pallas as pl
from jax.experimental.pallas import tpu as pltpu
from jax.sharding import PartitionSpec as P

HIGHEST = lax.Precision.HIGHEST
VMEM_LIMIT = 24 * 1024 * 1024


def any_mesh(
    right_side,
    earlier,
    inverse_diag,
    dense_tiles,
    left_factor,
    right_factor,
    tile_ranks,
    dense_flags,
):
    count_steps = right_side.shape[0]
    prev_cols = earlier.shape[0]
    rank_pad = left_factor.shape[3]
    tile_flags = dense_flags.astype(jnp.float32)
    columns = lax.broadcasted_iota(jnp.int32, tile_ranks.shape + (rank_pad,), 2)
    low_mask = (columns < tile_ranks[:, :, None]).astype(jnp.float32) * (1.0 - tile_flags)[
        :, :, None
    ]
    left_eff = left_factor * low_mask[:, :, None, :]
    tile_rows = (
        lax.all_gather(dense_tiles, "pcol", axis=3, tiled=True) * tile_flags[:, :, None, None]
    )
    inverse_rows = lax.all_gather(inverse_diag, "pcol", axis=2, tiled=True)
    early_sum = jnp.einsum(
        "kjrc,jcs->krs",
        tile_rows[:, :prev_cols],
        lax.all_gather(earlier, "prow", axis=1, tiled=True),
        precision=HIGHEST,
    )
    partial_value = jnp.einsum(
        "kjcq,jcs->kjqs", right_factor[:, :prev_cols], earlier, precision=HIGHEST
    )
    early_coeffs = lax.psum(partial_value, "prow")
    early_sum = early_sum + jnp.einsum(
        "kjrq,kjqs->krs", left_eff[:, :prev_cols], early_coeffs, precision=HIGHEST
    )
    pending = right_side - early_sum
    outputs = []
    for block_index in range(count_steps):
        residual_whole = lax.all_gather(pending[block_index], "prow", axis=0, tiled=True)
        solved_own = jnp.dot(inverse_rows[block_index], residual_whole, precision=HIGHEST)
        outputs.append(solved_own)
        if block_index + 1 < count_steps:
            solved_whole = lax.all_gather(solved_own, "prow", axis=0, tiled=True)
            column = prev_cols + block_index
            later = slice(block_index + 1, None)
            dense_part = jnp.einsum(
                "krc,cs->krs", tile_rows[later, column], solved_whole, precision=HIGHEST
            )
            projected = lax.psum(
                jnp.einsum(
                    "kcq,cs->kqs", right_factor[later, column], solved_own, precision=HIGHEST
                ),
                "prow",
            )
            low_part = jnp.einsum(
                "krq,kqs->krs", left_eff[later, column], projected, precision=HIGHEST
            )
            pending = pending.at[later].add(-(dense_part + low_part))
    return jnp.stack(outputs)


def halves(value, axis):
    high = value.astype(jnp.bfloat16)
    low = (value - high.astype(jnp.float32)).astype(jnp.bfloat16)
    return jnp.concatenate([high, low], axis=axis)


def dot_halves(left2, right2, dims=(((1,), (0,)), ((), ()))):
    axis_left, axis_right = 1 - dims[0][0][0], 1 - dims[0][1][0]
    rows, cols = left2.shape[axis_left] // 2, right2.shape[axis_right] // 2
    high_left = left2[:rows] if axis_left == 0 else left2[:, :rows]
    high_right, low_right = right2[:, :cols], right2[:, cols:]
    out = lax.dot_general(left2, high_right, dims, preferred_element_type=jnp.float32)
    rest = lax.dot_general(high_left, low_right, dims, preferred_element_type=jnp.float32)
    return out[:rows] + (out[rows:] + rest)


def first_kernel(prev, *refs):
    known_ref, right_ref, inv_ref, ahead_ref, known_out = refs
    steps, nb = right_ref.shape[0], inv_ref.shape[1]
    share = right_ref.shape[2] // lax.axis_size("pcol")
    at = pl.multiple_of(lax.axis_index("pcol") * share, share)
    place = 0
    for step in range(steps):
        if step:
            ahead_ref[place : place + nb] = inv_ref[step - 1]
            place += nb
        for col in range(prev + step):
            ahead_ref[place : place + share] = right_ref[step, col, pl.ds(at, share), :]
            place += share
    known_out[...] = known_ref[...]


def dense_kernel(rows, flags_ref, *refs):
    *dense_refs, out_ref = refs
    place = 0
    for (step, count), ref in zip(rows, dense_refs):
        for col in range(count):
            block = ref[0] if len(ref.shape) == 3 else ref[0, col] * flags_ref[step, col].astype(jnp.float32)
            out_ref[place] = block
            place += 1


def stack_kernel(begin, *refs):
    *parts, out_ref = refs
    count = out_ref.shape[0] // len(parts)
    for index, ref in enumerate(parts):
        out_ref[index * count : (index + 1) * count] = ref[begin : begin + count]


def masked_left(step, col, ranks_ref, flags_ref, left_ref):
    row_at = lax.broadcasted_iota(jnp.int32, left_ref.shape[2:], 0)
    flag = flags_ref[step, col].astype(jnp.float32)
    return left_ref[0, col] * jnp.where(row_at < ranks_ref[step, col], 1.0 - flag, 0.0)


OVER_ROWS = (((0,), (0,)), ((), ()))


def prepare_kernel(n, prev, step, first, last, *refs):
    refs = list(refs)
    dense = [refs.pop(0) for _ in range(n)]
    ahead = [refs.pop(0) for _ in range(2)]
    sources = [refs.pop(0) for _ in range(n)]
    solved = [refs.pop(0) for _ in range(step - 1)]
    ranks_ref, flags_ref, left_ref, base_ref, out_ref, *outs, scratch, right_scr = refs
    strip_ref, inv_ref = outs or (None, None)
    nb = base_ref.shape[1]
    tiles, rank_pad = right_scr.shape[:2]
    share = rank_pad // n
    own_col, own_row = lax.axis_index("pcol"), lax.axis_index("prow")
    turn = own_col ^ own_row
    rows = ahead[0].shape[0] // (2 * n)
    head = nb if step else 0

    for near in range(n):
        col_at = own_col ^ near
        for slot in range(n):
            at = ((near >> 1) * n + slot) * rows
            if step:
                both = halves(ahead[near & 1][at : at + nb], 0)
                row_at = (own_row ^ slot) * nb
                lanes = pl.ds(pl.multiple_of(col_at * nb, nb), nb)
                inv_ref[pl.ds(pl.multiple_of(row_at, nb), nb), lanes] = both[:nb]
                inv_ref[pl.ds(pl.multiple_of(n * nb + row_at, nb), nb), lanes] = both[nb:]
            lanes = pl.ds(pl.multiple_of((turn ^ slot) * nb, nb), nb)
            ranks = pl.ds(pl.multiple_of(col_at * share, share), share)
            for tile in range(tiles):
                place = at + head + tile * share
                right_scr[tile, ranks, lanes] = ahead[near & 1][place : place + share]

    def strip_of(tile):
        blocks = [ref[first + tile] for ref in dense]
        left = masked_left(step, tile, ranks_ref, flags_ref, left_ref)
        low = dot_halves(halves(left, 1), halves(right_scr[tile], 1), OVER_ROWS)
        return jnp.concatenate(blocks, axis=1) + low

    total = base_ref[0]
    for tile in range(prev):
        for slot, ref in enumerate(sources):
            scratch[pl.ds(pl.multiple_of((turn ^ slot) * nb, nb), nb), :] = ref[tile]
        total = total - dot_halves(halves(strip_of(tile), 0), halves(scratch[...], 1))
    for index, ref in enumerate(solved):
        for d in range(n):
            rows_at = pl.ds(pl.multiple_of((own_col ^ d) * nb, nb), nb)
            scratch[d * nb : (d + 1) * nb] = ref[rows_at, :]
        total = total - dot_halves(halves(strip_of(prev + index), 0), halves(scratch[...], 1))
    out_ref[...] = total
    if not step:
        return
    pair = halves(strip_of(tiles - 1), 0)
    for d in range(n):
        lanes = pl.ds(pl.multiple_of((own_col ^ d) * nb, nb), nb)
        strip_ref[0, :, lanes] = pair[:, d * nb : (d + 1) * nb]
        if last:
            strip_ref[1, :, lanes] = halves(dense[d][first + tiles], 0)


def place_slots(n, nb, slots, scratch):
    own = lax.axis_index("prow")
    for slot, ref in enumerate(slots):
        scratch[pl.ds(pl.multiple_of((own ^ slot) * nb, nb), nb), :] = ref[...]


def step_kernel(n, *refs):
    inverse_ref, strip_ref, base_ref, out_ref, solved_ref, scratch = refs[n:]
    place_slots(n, base_ref.shape[0], refs[:n], scratch)
    solved = dot_halves(inverse_ref[...], halves(scratch[...], 1))
    solved_ref[...] = solved
    out_ref[...] = base_ref[...] - dot_halves(strip_ref[0], halves(solved, 1))


def last_kernel(n, *refs):
    strip_ref, *solved, out_ref, scratch = refs[n:]
    nb = out_ref.shape[1]
    place_slots(n, nb, refs[:n], scratch)
    own = pl.ds(pl.multiple_of(lax.axis_index("prow") * nb, nb), nb)
    for step, ref in enumerate(solved):
        out_ref[step] = ref[own, :]
    out_ref[len(solved)] = dot_halves(strip_ref[0], halves(scratch[...], 1))


def spec_of(shape, index=None):
    if index is None:
        return pl.BlockSpec(shape, lambda i: (0,) * len(shape))
    return pl.BlockSpec(shape, lambda i: index)


def square_mesh(
    n,
    right_side,
    earlier,
    inverse_diag,
    dense_tiles,
    left_factor,
    right_factor,
    tile_ranks,
    dense_flags,
):
    steps, nb, rhs = right_side.shape
    prev = earlier.shape[0]
    cols = dense_tiles.shape[1]
    rank_pad = left_factor.shape[3]
    left_t = jnp.swapaxes(left_factor, 2, 3)
    right_t = jnp.swapaxes(right_factor, 2, 3)
    params = pltpu.CompilerParams(vmem_limit_bytes=VMEM_LIMIT)
    f32 = jnp.float32

    def shift(value, axis, step):
        return lax.ppermute(value, axis, [(i, i ^ step) for i in range(n)])

    def over_rows(value):
        return [value] + [shift(value, "prow", d) for d in range(1, n)]

    def over_rows_forwarded(value):
        beside, across = shift(value, "prow", 1), shift(value, "prow", 2)
        return [value, beside, across, shift(across, "prow", 1)]

    any_spec = pl.BlockSpec(memory_space=pl.ANY)
    smem = pl.BlockSpec(memory_space=pltpu.SMEM)
    bf16 = jnp.bfloat16

    def pinned(value):
        return pltpu.with_memory_space_constraint(value, pltpu.HBM)

    def shaped(*shape, dtype=f32):
        return jax.ShapeDtypeStruct(shape, dtype)

    def call(kernel, name, shapes, args, specs, scratch=(), after=()):
        many = isinstance(shapes, list)
        out_specs = [spec_of(x.shape) for x in shapes] if many else spec_of(shapes.shape)

        def body(*refs):
            kernel(*refs[: len(args)], *refs[len(args) + len(after) :])

        return pl.pallas_call(
            body,
            grid=(1,),
            out_shape=shapes,
            in_specs=specs + [any_spec] * len(after),
            out_specs=out_specs,
            scratch_shapes=list(scratch),
            compiler_params=params,
            name=name,
        )(*args, *after)

    def blocks_of(value, step):
        return pinned(value), spec_of((1,) + value.shape[1:], (step,) + (0,) * (value.ndim - 1))

    def whole_of(value):
        return value, spec_of(value.shape)

    def run(kernel, name, shapes, pairs, scratch=(), after=()):
        args, specs = zip(*pairs)
        return call(kernel, name, shapes, list(args), list(specs), scratch, after)

    share = rank_pad // n
    ranks_flags = [(tile_ranks, smem), (dense_flags, smem)]
    source_room = pltpu.VMEM((n * nb, rhs), f32)
    def over_cols(own):
        far = shift(own, "pcol", 2)
        return [own, shift(own, "pcol", 1), far, shift(far, "pcol", 1)]

    heights = [(nb if step else 0) + (prev + step) * share for step in range(steps)]

    def ahead_far(step, after=()):
        own = run(
            functools.partial(stack_kernel, sum(heights[:step])),
            f"ahead{step}",
            shaped(n * heights[step], nb),
            [whole_of(value) for value in ahead],
            after=after,
        )
        return [own, shift(own, "pcol", 2)]

    def ahead_near(step, halfs, after=()):
        both = run(
            functools.partial(stack_kernel, 0),
            f"aheads{step}",
            shaped(2 * n * heights[step], nb),
            [whole_of(value) for value in halfs],
            after=after,
        )
        return [both, shift(both, "pcol", 1)]

    sent, known = run(
        functools.partial(first_kernel, prev),
        "first",
        [shaped(sum(heights), nb), shaped(*earlier.shape)],
        [whole_of(pinned(value)) for value in (earlier, right_t, inverse_diag)],
    )
    ahead = over_rows_forwarded(sent)
    known = over_rows_forwarded(known)
    own = run(
        functools.partial(dense_kernel, [(0, prev)]),
        "dense0",
        shaped(prev, nb, nb),
        [(dense_flags, smem), blocks_of(dense_tiles, 0)],
        after=[sent],
    )
    strips0 = over_cols(own)
    rows = [(step, prev + step) for step in range(1, steps)] + [(steps - 1, 1)]
    size = sum(count for _, count in rows)
    own = run(
        functools.partial(dense_kernel, rows),
        "dense",
        shaped(size, nb, nb),
        [(dense_flags, smem)]
        + [blocks_of(dense_tiles, step) for step in range(1, steps)]
        + [blocks_of(inverse_diag, steps - 1)],
        after=[sent],
    )
    dense = over_cols(own)

    def prepare(step, strips, later, solved=()):
        last = step + 1 == steps
        tiles = prev + step
        outs = [
            shaped(nb, rhs),
            shaped(1 + last, 2 * nb, n * nb, dtype=bf16),
            shaped(2 * n * nb, n * nb, dtype=bf16),
        ]
        first = sum(count for row, count in rows[:-1] if row < step)
        return run(
            functools.partial(prepare_kernel, n, prev, step, first, last),
            f"prepare{step}",
            outs if step else outs[0],
            [whole_of(value) for value in [*strips, *later, *known, *solved]]
            + ranks_flags
            + [blocks_of(left_t, step), blocks_of(right_side, step)],
            [source_room, pltpu.VMEM((tiles, rank_pad, n * nb), f32)],
        )

    def solve(step, slots, prepared):
        base, strip, inverse = prepared
        return run(
            functools.partial(step_kernel, n),
            f"step{step}",
            [shaped(nb, rhs), shaped(n * nb, rhs)],
            [whole_of(value) for value in slots + [inverse]]
            + [(strip, spec_of((1, 2 * nb, n * nb), (0, 0, 0))), whole_of(base)],
            [source_room],
        )

    pending0 = prepare(0, strips0, ahead_near(0, ahead_far(0)))
    later1 = ahead_near(1, ahead_far(1, []), [pending0])
    later2 = ahead_far(2, [pending0])
    pending1, solved0 = solve(0, over_rows(pending0), prepare(1, dense, later1))
    later2 = ahead_near(2, later2, [pending1])
    later3 = ahead_far(3, [pending1])
    pending2, solved1 = solve(1, over_rows(pending1), prepare(2, dense, later2, [solved0]))
    later3 = ahead_near(3, later3, [pending2])
    prepared = prepare(3, dense, later3, [solved0, solved1])
    pending3, solved2 = solve(2, over_rows(pending2), prepared)
    return run(
        functools.partial(last_kernel, n),
        "last",
        shaped(steps, nb, rhs),
        [whole_of(value) for value in over_rows(pending3)]
        + [(prepared[1], spec_of((1, 2 * nb, n * nb), (1, 0, 0)))]
        + [whole_of(value) for value in (solved0, solved1, solved2)],
        [source_room],
    )


def solution(mesh):
    placed = (
        P("groups", "prow", "pcol"),
        P("groups", "prow", "pcol"),
        P("groups", "prow", "pcol"),
        P("groups", None, "prow", "pcol"),
        P("groups", None, "prow", None),
        P("groups", None, "prow", None),
        P("groups", None),
        P("groups", None),
    )
    n = mesh.shape["prow"]
    square = n == 4 and n == mesh.shape["pcol"]

    def local(*args):
        nb, cols = args[3].shape[2:]
        steps = args[0].shape[0]
        if square and steps == 4 and nb % 128 == 0 and cols % 128 == 0 and args[0].shape[2] % 128 == 0:
            return square_mesh(n, *args)
        return any_mesh(*args)

    return jax.shard_map(
        local, mesh=mesh, in_specs=placed, out_specs=P("groups", "prow", "pcol"), check_vma=False
    )
```
